256 devices in a mesh: seq: 64 (over z, y, core), head: 4 (over x).
Axes of the slice: x: 4, y: 4, z: 8, core: 2. Of those that a mesh axis runs over, the one named last changes fastest.
Arguments:
- query_rows: bfloat16 [65536, 3072], P('seq', 'head'), may hold values from -6 to 6
- key_rows: bfloat16 [65536, 3072], P('seq', 'head'), may hold values from -6 to 6
- value_rows: bfloat16 [65536, 3072], P('seq', 'head'), may hold values from -6 to 6
- query_gain: float32 [128], replicated, may hold values from 1 to 2.5
- key_gain: float32 [128], replicated, may hold values from 1 to 2.5
- head_class: int32 [24], P('head'), may hold values from 0 to 1, as said below
- out_weight: bfloat16 [3072, 3072], P('head'), may hold values from -0.109375 to 0.109375
Outputs:
- attn_out: bfloat16 [65536, 3072], P('seq', 'head')
The draws below stay inside these ranges and needn't reach their ends.
Inputs may be any that keep to these rules, and one draw needn't show every extreme that they name: `head_class`: in every group of 6 consecutive heads, 1 to 4 heads are temporal, and some group has exactly 4.
All inputs are finite; a program needn't handle non-finite values.
Results may differ from the reference program's by a relative error of at most 0.013.
Values may be sent and summed in bfloat16 or wider, within the bound.
No kernel may reach another device: no remote copies, remote signals or barrier semaphores. Data moves between devices by JAX's collectives and lax.ppermute only.
A program may use at most 128 MiB of HBM per device.

```python
import math
import jax
import jax.numpy as jnp
from jax import lax

D = 3072
H = 24
HD = 128
FRAMES = 32
TMAX = 4
HG = 6
TOKENS = 65536
PF = 2048
N_HEAD = 4


def draw_head_class(key, part):
    key = jax.random.fold_in(key, 3)
    group_count = H // HG
    counts = jax.random.randint(jax.random.fold_in(key, 1), (group_count,), 1, TMAX + 1)
    busiest = jax.random.randint(jax.random.fold_in(key, 2), (), 0, group_count)
    counts = jnp.where(jnp.arange(group_count) == busiest, TMAX, counts)
    group_keys = jax.random.split(jax.random.fold_in(key, 4), group_count)

    def shuffled(group_key):
        return jax.random.permutation(group_key, HG)
    orders = jax.vmap(shuffled)(group_keys)
    return (orders < counts[:, None]).astype(jnp.int32).reshape(H)


def levels(stream_key, dims, shards, smallest, high):
    def one(axis_at, blocks):
        heights = jax.random.uniform(jax.random.fold_in(jax.random.fold_in(stream_key, 6), axis_at), (blocks,), jnp.float32, smallest / len(shards), high / len(shards))
        return jnp.repeat(jnp.exp(heights), dims[axis_at] // blocks).reshape((-1,) + (1,) * (len(dims) - axis_at - 1))

    gain = one(*shards[0])
    for cut in shards[1:]:
        gain = gain * one(*cut)
    return gain


def bell_draw(own_key, shape, deviation, limit, pieces=(), held_as=jnp.bfloat16):
    array = deviation * jax.random.normal(own_key, shape, jnp.float32)
    if pieces:
        array = array * levels(own_key, shape, pieces, -0.22, 0.18)
    return jnp.clip(array, -limit, limit).astype(held_as)


def setup_inputs(seed: int = 0) -> dict:
    streams_of = jax.random.split(jax.random.key(seed), 8)
    return {
        "query_rows": bell_draw(streams_of[0], (TOKENS, H * HD), 1.0, 6.0, ((0, 64), (1, 4))),
        "key_rows": bell_draw(streams_of[1], (TOKENS, H * HD), 1.0, 6.0, ((0, 64), (1, 4))),
        "value_rows": bell_draw(streams_of[2], (TOKENS, H * HD), 1.0, 6.0, ((0, 64), (1, 4))),
        "query_gain": jnp.clip(jnp.exp(jax.random.uniform(streams_of[3], (HD,), jnp.float32, math.log(1.0), math.log(2.5))), 1.0, 2.5),
        "key_gain": jnp.clip(jnp.exp(jax.random.uniform(streams_of[4], (HD,), jnp.float32, math.log(1.0), math.log(2.5))), 1.0, 2.5),
        "head_class": draw_head_class(jax.random.fold_in(streams_of[7], 71), 0),
        "out_weight": bell_draw(streams_of[6], (H * HD, D), (H * HD) ** -0.5, 0.109375, ((0, 4),)),
    }


epsilon = 1e-06

def normed(row_block, gain_row):
    widened = row_block.astype(jnp.float32).reshape(row_block.shape[0], H, HD)
    scaled = widened * lax.rsqrt(lax.optimization_barrier(jnp.mean(widened * widened, axis=-1, keepdims=True)) + epsilon) * gain_row
    return scaled.astype(jnp.bfloat16)

def softmax_weights(scores):
    exponent = jnp.exp(scores)
    return (exponent / lax.optimization_barrier(jnp.sum(exponent, axis=-1, keepdims=True))).astype(jnp.bfloat16)

def one_frame(inputs):
    frame_q, frame_k, frame_v = inputs
    spatial_scores = jnp.dot(frame_q, frame_k.T, precision=lax.Precision.HIGHEST) * (1.0 / math.sqrt(HD))
    spatial_weights = softmax_weights(spatial_scores)
    spatial_out = jnp.dot(spatial_weights.astype(jnp.float32), frame_v, precision=lax.Precision.HIGHEST)
    return spatial_out.astype(jnp.bfloat16)

def one_head(inputs):
    queries, keys_in, values_in, head_kind = inputs
    score_scale = 1.0 / math.sqrt(HD)
    frame_q = queries.astype(jnp.float32).reshape(FRAMES, PF, HD)
    frame_k = keys_in.astype(jnp.float32).reshape(FRAMES, PF, HD)
    frame_v = values_in.astype(jnp.float32).reshape(FRAMES, PF, HD)
    spatial_out = lax.map(one_frame, (frame_q, frame_k, frame_v)).reshape(TOKENS, HD)
    temporal_scores = jnp.einsum('fpd,gpd->pfg', frame_q, frame_k, precision=lax.Precision.HIGHEST) * score_scale
    temporal_weights = softmax_weights(temporal_scores)
    temporal_out = jnp.einsum('pfg,gpd->fpd', temporal_weights.astype(jnp.float32), frame_v, precision=lax.Precision.HIGHEST)
    temporal_out = temporal_out.astype(jnp.bfloat16).reshape(TOKENS, HD)
    return jnp.where(head_kind == 1, temporal_out, spatial_out)

def reference(query_rows, key_rows, value_rows, query_gain, key_gain, head_class, out_weight):
    query_normed = normed(query_rows, query_gain)
    key_normed = normed(key_rows, key_gain)
    value_heads = value_rows.reshape(TOKENS, H, HD)
    stacked = (jnp.transpose(query_normed, (1, 0, 2)), jnp.transpose(key_normed, (1, 0, 2)), jnp.transpose(value_heads, (1, 0, 2)), head_class)
    head_out = lax.map(one_head, stacked)
    flattened = jnp.transpose(head_out, (1, 0, 2)).reshape(TOKENS, H * HD)
    group_width = HG * HD
    summed = jnp.zeros((TOKENS, D), jnp.float32)
    for group_index in range(N_HEAD):
        first = group_index * group_width
        partial_value = jnp.dot(flattened[:, first:first + group_width], out_weight[first:first + group_width, :], preferred_element_type=jnp.float32)
        rounded = lax.optimization_barrier(partial_value.astype(jnp.bfloat16))
        summed = summed + rounded.astype(jnp.float32)
    return summed.astype(jnp.bfloat16)
```

```python
import functools
import math

import jax
import jax.numpy as jnp
from jax import lax
from jax.experimental import pallas as pl
from jax.experimental.pallas import tpu as pltpu
from jax.sharding import PartitionSpec as P

FRAMES = 32
TMAX = 4
CORES = 2
HD = 128
EPSILON = 1e-06
LOG2_SCALE = math.log2(math.e) / math.sqrt(HD)
VMEM_LIMIT = 40 * 1024 * 1024


def temporal_count(classes, head_count):
    total = classes[0]
    for head in range(1, head_count):
        total = total + classes[head]
    return total


def head_of(classes, slot, head_count):
    temporal_seen = jnp.int32(0)
    spatial_seen = temporal_count(classes, head_count)
    found = jnp.int32(0)
    for head in range(head_count):
        kind = classes[head]
        rank = jnp.where(kind == 1, temporal_seen, spatial_seen)
        found = jnp.where(rank == slot, jnp.int32(head), found)
        temporal_seen = temporal_seen + kind
        spatial_seen = spatial_seen + 1 - kind
    return found


def normed(rows, gain):
    widened = rows.astype(jnp.float32)
    mean = jnp.mean(widened * widened, axis=-1, keepdims=True)
    return (widened * lax.rsqrt(mean + EPSILON) * gain).astype(jnp.bfloat16)


def scores_of(queries, keys):
    return lax.dot_general(queries, keys, (((1,), (1,)), ((), ())), preferred_element_type=jnp.float32)


def pack_kernel(classes, query, key, value, query_gain, key_gain, out):
    out[:, :HD] = normed(query[...], query_gain[...])
    out[:, HD : 2 * HD] = normed(key[...], key_gain[...])
    out[:, 2 * HD :] = value[...]


def pack(head_class, query_rows, key_rows, value_rows, query_gain, key_gain):
    tokens, width = query_rows.shape
    head_count = width // HD
    block = tokens // 2

    def rows(slot, row, classes):
        return row, head_of(classes, slot, head_count)

    row_spec = pl.BlockSpec((block, HD), rows)
    gain_spec = pl.BlockSpec((1, HD), lambda slot, row, classes: (0, 0))
    return pl.pallas_call(
        pack_kernel,
        grid_spec=pltpu.PrefetchScalarGridSpec(
            num_scalar_prefetch=1,
            grid=(TMAX, tokens // block),
            in_specs=[row_spec, row_spec, row_spec, gain_spec, gain_spec],
            out_specs=pl.BlockSpec((block, 3 * HD), lambda slot, row, classes: (row, slot)),
        ),
        out_shape=jax.ShapeDtypeStruct((tokens, TMAX * 3 * HD), jnp.bfloat16),
        cost_estimate=pl.CostEstimate(flops=8 * tokens * TMAX * HD, bytes_accessed=12 * tokens * TMAX * HD, transcendentals=0),
        name="pack",
    )(head_class, query_rows, key_rows, value_rows, query_gain, key_gain)


def spatial_kernel(head_count, classes, query, key, other_key, value, other_value, query_gain, key_gain, front, back, keys, values):
    slot = pl.program_id(0)
    tokens = query.shape[0]
    chunk = tokens // 4
    is_front = slot < TMAX

    @pl.when(slot >= temporal_count(classes, head_count))
    def _():
        keys[:tokens] = normed(key[...], key_gain[...])
        keys[tokens:] = normed(other_key[...], key_gain[...])
        values[:tokens, :HD] = value[...]
        values[tokens:, :HD] = other_value[...]
        values[:, HD:] = jnp.ones((2 * tokens, HD), jnp.bfloat16)

        def step(index, carry):
            rows = pl.ds(pl.multiple_of(index * chunk, chunk), chunk)
            queries = normed(query[rows, :], query_gain[...])
            weights = jnp.exp2(scores_of(queries, keys[...]) * LOG2_SCALE).astype(jnp.bfloat16)
            summed = jnp.dot(weights, values[...], preferred_element_type=jnp.float32)
            result = (summed[:, :HD] / summed[:, HD:]).astype(jnp.bfloat16)

            @pl.when(is_front)
            def _():
                front[rows, :] = result

            @pl.when(jnp.logical_not(is_front))
            def _():
                back[rows, :] = result

            return carry

        lax.fori_loop(0, tokens // chunk, step, 0)

    @pl.when(slot < temporal_count(classes, head_count))
    def _():
        front[...] = jnp.zeros_like(front)


def spatial(head_class, query_rows, key_rows, other_keys, value_rows, other_values, query_gain, key_gain):
    tokens, width = query_rows.shape
    head_count = width // HD

    def rows(slot, classes):
        return 0, head_of(classes, slot, head_count)

    row_spec = pl.BlockSpec((tokens, HD), rows)
    gain_spec = pl.BlockSpec((1, HD), lambda slot, classes: (0, 0))
    return pl.pallas_call(
        functools.partial(spatial_kernel, head_count),
        grid_spec=pltpu.PrefetchScalarGridSpec(
            num_scalar_prefetch=1,
            grid=(head_count,),
            in_specs=[row_spec] * 5 + [gain_spec] * 2,
            out_specs=[
                pl.BlockSpec((tokens, HD), lambda slot, classes: (0, jnp.minimum(slot, TMAX - 1))),
                pl.BlockSpec((tokens, HD), lambda slot, classes: (0, jnp.maximum(slot - TMAX, 0))),
            ],
            scratch_shapes=[
                pltpu.VMEM((2 * tokens, HD), jnp.bfloat16),
                pltpu.VMEM((2 * tokens, 2 * HD), jnp.bfloat16),
            ],
        ),
        out_shape=[
            jax.ShapeDtypeStruct((tokens, TMAX * HD), jnp.bfloat16),
            jax.ShapeDtypeStruct((tokens, width - TMAX * HD), jnp.bfloat16),
        ],
        compiler_params=pltpu.CompilerParams(vmem_limit_bytes=VMEM_LIMIT),
        cost_estimate=pl.CostEstimate(
            flops=16 * tokens * tokens * width, bytes_accessed=12 * tokens * width, transcendentals=2 * tokens * tokens * head_count
        ),
        name="spatial",
    )(head_class, query_rows, key_rows, other_keys, value_rows, other_values, query_gain, key_gain)


def temporal_kernel(head_count, first, classes, packed, out):
    slot = first + pl.program_id(0)
    frames, places = packed.shape[0], packed.shape[1]
    count = frames * places

    @pl.when(slot < temporal_count(classes, head_count))
    def _():
        block = packed[...]
        queries = block[:, :, :HD].reshape(count, HD)
        keys = block[:, :, HD : 2 * HD].reshape(count, HD)
        values = block[:, :, 2 * HD :].reshape(count, HD)
        row = lax.broadcasted_iota(jnp.int32, (count, count), 0)
        column = lax.broadcasted_iota(jnp.int32, (count, count), 1)
        same = (row & (places - 1)) == (column & (places - 1))
        scaled = jnp.where(same, scores_of(queries, keys) * LOG2_SCALE, -1e30)
        weights = jnp.exp2(scaled).astype(jnp.bfloat16)
        both = jnp.concatenate([values, jnp.ones_like(values)], axis=1)
        summed = jnp.dot(weights, both, preferred_element_type=jnp.float32)
        out[...] = (summed[:, :HD] / summed[:, HD:]).astype(jnp.bfloat16).reshape(out.shape)

    @pl.when(slot >= temporal_count(classes, head_count))
    def _():
        out[...] = jnp.zeros_like(out)


def temporal(head_class, packed, first, slots):
    frames, positions, _ = packed.shape
    places = 16
    return pl.pallas_call(
        functools.partial(temporal_kernel, head_class.shape[0], first),
        grid_spec=pltpu.PrefetchScalarGridSpec(
            num_scalar_prefetch=1,
            grid=(slots, positions // places),
            in_specs=[pl.BlockSpec((frames, places, 3 * HD), lambda slot, part, classes: (0, part, slot + first))],
            out_specs=pl.BlockSpec((frames, places, HD), lambda slot, part, classes: (0, part, slot)),
        ),
        out_shape=jax.ShapeDtypeStruct((frames, positions, slots * HD), jnp.bfloat16),
        compiler_params=pltpu.CompilerParams(vmem_limit_bytes=VMEM_LIMIT),
        cost_estimate=pl.CostEstimate(
            flops=6 * frames * frames * places * positions * slots * HD,
            bytes_accessed=8 * frames * positions * slots * HD,
            transcendentals=frames * frames * places * positions * slots,
        ),
        name="temporal",
    )(head_class, packed)


def weight_kernel(classes, place, weight, out):
    out[...] = weight[...][None]


def weight_blocks(head_class, place, weight, group_count):
    rows, columns = weight.shape
    head_count = rows // HD
    width = columns // group_count
    return pl.pallas_call(
        weight_kernel,
        grid_spec=pltpu.PrefetchScalarGridSpec(
            num_scalar_prefetch=2,
            grid=(group_count, head_count),
            in_specs=[
                pl.BlockSpec(
                    (HD, width),
                    lambda shift, slot, classes, place: (head_of(classes, slot, head_count), lax.rem(place[0] + shift, group_count)),
                )
            ],
            out_specs=pl.BlockSpec((1, HD, width), lambda shift, slot, classes, place: (shift, slot, 0)),
        ),
        out_shape=jax.ShapeDtypeStruct((group_count, rows, width), jnp.bfloat16),
        cost_estimate=pl.CostEstimate(flops=0, bytes_accessed=4 * rows * columns, transcendentals=0),
        name="weight_blocks",
    )(head_class, place, weight)


def project_kernel(with_sum, own, right, left, far_top, far_bottom, w_own, w_right, w_far, w_left, *rest):
    out = rest[-1]
    top = pl.program_id(0) < pl.num_programs(0) // 2
    far = jnp.where(top, far_top[...], far_bottom[...])
    total = jnp.dot(own[...], w_own[...], preferred_element_type=jnp.float32)
    total += jnp.dot(right[...], w_right[...], preferred_element_type=jnp.float32)
    total += jnp.dot(left[...], w_left[...], preferred_element_type=jnp.float32)
    total += jnp.dot(far, w_far[...], preferred_element_type=jnp.float32)
    if with_sum:
        total += rest[0][...]
    out[...] = total.astype(out.dtype)


def project(pieces, weights, row_block, total, out_dtype):
    own = pieces[0]
    tokens, depth = own.shape
    width = weights[0].shape[1]
    steps = 4
    block = tokens // steps
    row_spec = pl.BlockSpec((block, depth), lambda step: (step, 0))
    top_spec = pl.BlockSpec((block, depth), lambda step: (jnp.minimum(step, steps // 2 - 1), 0))
    bottom_spec = pl.BlockSpec((block, depth), lambda step: (jnp.maximum(step - steps // 2, 0), 0))
    weight_spec = pl.BlockSpec((depth, width), lambda step: (row_block, 0))
    sum_spec = pl.BlockSpec((block, width), lambda step: (step, 0))
    sums = [] if total is None else [total]
    return pl.pallas_call(
        functools.partial(project_kernel, total is not None),
        grid=(steps,),
        in_specs=[row_spec] * 3 + [top_spec, bottom_spec] + [weight_spec] * 4 + [sum_spec] * len(sums),
        out_specs=sum_spec,
        out_shape=jax.ShapeDtypeStruct((tokens, width), out_dtype),
        compiler_params=pltpu.CompilerParams(vmem_limit_bytes=VMEM_LIMIT),
        cost_estimate=pl.CostEstimate(
            flops=8 * tokens * depth * width, bytes_accessed=8 * tokens * depth + 8 * depth * width + 8 * tokens * width, transcendentals=0
        ),
        name="project",
    )(*pieces, *weights, *sums)


def shifted(block, by):
    count = lax.axis_size("head")
    return lax.ppermute(block, "head", [(at, (at + by) % count) for at in range(count)])


def ring(block):
    half = block.shape[0] // 2
    right, left = shifted(block, 1), shifted(block, -1)
    return block, right, left, shifted(right[:half], 1), shifted(left[half:], -1)


def other_core(block):
    count = lax.axis_size("seq")
    return lax.ppermute(block, "seq", [(at, at ^ 1) for at in range(count)])


def over_frames(blocks):
    count = lax.axis_size("seq")
    groups = [list(range(core, count, CORES)) for core in range(CORES)]
    return lax.all_to_all(blocks, "seq", 0, 0, axis_index_groups=groups)


def body(query_rows, key_rows, value_rows, query_gain, key_gain, head_class, out_weight):
    tokens = query_rows.shape[0]
    group_count = lax.axis_size("head")
    query_gain = query_gain.reshape(1, HD)
    key_gain = key_gain.reshape(1, HD)
    packed = pack(head_class, query_rows, key_rows, value_rows, query_gain, key_gain)
    arrived = over_frames(packed.reshape(FRAMES, tokens // FRAMES, TMAX * 3 * HD))

    other_keys, other_values = other_core(key_rows), other_core(value_rows)
    front, back = spatial(head_class, query_rows, key_rows, other_keys, value_rows, other_values, query_gain, key_gain)
    place = lax.axis_index("head").reshape(1).astype(jnp.int32)
    blocks = weight_blocks(head_class, place, out_weight, group_count)
    weights = [blocks[0]] + [shifted(blocks[by], by) for by in range(1, group_count)]
    total = project(ring(back), weights, TMAX // 2, None, jnp.float32)

    half = TMAX // 2
    temporal_slots = jnp.sum(head_class)
    for part in range(2):
        first = part * half
        returned = over_frames(temporal(head_class, arrived, first, half)).reshape(tokens, half * HD)
        slots = first + lax.broadcasted_iota(jnp.int32, (1, half * HD), 1) // HD
        chosen = jnp.where(slots < temporal_slots, returned, front[:, first * HD : (first + half) * HD])
        total = project(ring(chosen), weights, part, total, jnp.bfloat16 if part else jnp.float32)
    return total


def solution(mesh):
    return jax.shard_map(
        body,
        mesh=mesh,
        in_specs=(
            P("seq", "head"),
            P("seq", "head"),
            P("seq", "head"),
            P(),
            P(),
            P("head"),
            P("head", None),
        ),
        out_specs=P("seq", "head"),
        check_vma=False,
    )
```

```python
import functools
import math

import jax
import jax.numpy as jnp
from jax import lax
from jax.experimental import pallas as pl
from jax.experimental.pallas import tpu as pltpu
from jax.sharding import PartitionSpec as P

FRAMES = 32
TMAX = 4
SMALL_VMEM = 16 * 1024 * 1024
CORES = 2
HD = 128
EPSILON = 1e-06
LOG2_SCALE = math.log2(math.e) / math.sqrt(HD)


def in_hbm(shape, dtype):
    return pltpu.HBM(shape, dtype)


def from_hbm(array):
    return pltpu.with_memory_space_constraint(array, pltpu.HBM)


def from_vmem(array):
    return pltpu.with_memory_space_constraint(array, pltpu.VMEM)


def temporal_count(classes, head_count):
    total = classes[0]
    for head in range(1, head_count):
        total = total + classes[head]
    return total


def head_of(classes, slot, head_count):
    temporal_seen = jnp.int32(0)
    spatial_seen = temporal_count(classes, head_count)
    found = jnp.int32(0)
    for head in range(head_count):
        kind = classes[head]
        rank = jnp.where(kind == 1, temporal_seen, spatial_seen)
        found = jnp.where(rank == slot, jnp.int32(head), found)
        temporal_seen = temporal_seen + kind
        spatial_seen = spatial_seen + 1 - kind
    return found


def normed(rows, gain):
    widened = rows.astype(jnp.float32)
    mean = jnp.mean(widened * widened, axis=-1, keepdims=True)
    return (widened * lax.rsqrt(mean + EPSILON) * gain).astype(jnp.bfloat16)


def scores_of(queries, keys):
    return lax.dot_general(queries, keys, (((1,), (1,)), ((), ())), preferred_element_type=jnp.float32)


def pack_kernel(head_count, classes, query, key, value, query_gain, key_gain, out, raw, ready, in_sems, out_sems):
    tokens = query.shape[0]
    heads = [head_of(classes, slot, head_count) for slot in range(TMAX)]

    def columns(slot):
        return pl.ds(pl.multiple_of(heads[slot] * HD, HD), HD)

    loads, moves = [], []
    for slot in range(TMAX):
        for which, source in enumerate((query, key)):
            at = 2 * slot + which
            loads.append(pltpu.make_async_copy(source.at[:, columns(slot)], raw.at[at], in_sems.at[at]))
            loads[-1].start()
    for slot in range(TMAX):
        target = out.at[:, pl.ds((3 * slot + 2) * HD, HD)]
        moves.append(pltpu.make_async_copy(value.at[:, columns(slot)], target, out_sems.at[2 * TMAX + slot]))
        moves[-1].start()
    for slot in range(TMAX):
        for which, gain in enumerate((query_gain, key_gain)):
            at = 2 * slot + which
            loads[at].wait()
            ready[at] = normed(raw[at], gain[...])
            target = out.at[:, pl.ds((3 * slot + which) * HD, HD)]
            moves.append(pltpu.make_async_copy(ready.at[at], target, out_sems.at[at]))
            moves[-1].start()
    for move in moves:
        move.wait()


def pack(head_class, query_rows, key_rows, value_rows, query_gain, key_gain):
    tokens, width = query_rows.shape
    anywhere = pl.BlockSpec(memory_space=pl.ANY)
    gain_spec = pl.BlockSpec((1, HD), lambda step, classes: (0, 0))
    return pl.pallas_call(
        functools.partial(pack_kernel, width // HD),
        grid_spec=pltpu.PrefetchScalarGridSpec(
            num_scalar_prefetch=1,
            grid=(1,),
            in_specs=[anywhere] * 3 + [gain_spec] * 2,
            out_specs=anywhere,
            scratch_shapes=[
                pltpu.VMEM((2 * TMAX, tokens, HD), jnp.bfloat16),
                pltpu.VMEM((2 * TMAX, tokens, HD), jnp.bfloat16),
                pltpu.SemaphoreType.DMA((2 * TMAX,)),
                pltpu.SemaphoreType.DMA((3 * TMAX,)),
            ],
        ),
        out_shape=in_hbm((tokens, TMAX * 3 * HD), jnp.bfloat16),
        cost_estimate=pl.CostEstimate(flops=8 * tokens * TMAX * HD, bytes_accessed=12 * tokens * TMAX * HD, transcendentals=0),
        name="pack",
    )(head_class, from_hbm(query_rows), from_hbm(key_rows), from_hbm(value_rows), query_gain, key_gain)


def spatial_kernel(head_count, classes, query, key, other_key, value, other_value, query_gain, key_gain, front, back, keys, values):
    slot = pl.program_id(0)
    tokens = query.shape[0]
    chunk = tokens // 4
    is_front = slot < TMAX

    @pl.when(slot >= temporal_count(classes, head_count))
    def _():
        keys[:tokens] = normed(key[...], key_gain[...])
        keys[tokens:] = normed(other_key[...], key_gain[...])
        values[:tokens, :HD] = value[...]
        values[tokens:, :HD] = other_value[...]
        values[:, HD:] = jnp.ones((2 * tokens, HD), jnp.bfloat16)

        def step(index, carry):
            rows = pl.ds(pl.multiple_of(index * chunk, chunk), chunk)
            queries = normed(query[rows, :], query_gain[...])
            weights = jnp.exp2(scores_of(queries, keys[...]) * LOG2_SCALE).astype(jnp.bfloat16)
            summed = jnp.dot(weights, values[...], preferred_element_type=jnp.float32)
            result = (summed[:, :HD] / summed[:, HD:]).astype(jnp.bfloat16)

            @pl.when(is_front)
            def _():
                front[rows, :] = result

            @pl.when(jnp.logical_not(is_front))
            def _():
                back[rows, :] = result

            return carry

        lax.fori_loop(0, tokens // chunk, step, 0)

    @pl.when(slot < temporal_count(classes, head_count))
    def _():
        front[...] = jnp.zeros_like(front)


def spatial(head_class, query_rows, key_rows, other_keys, value_rows, other_values, query_gain, key_gain):
    tokens, width = query_rows.shape
    head_count = width // HD

    def rows(slot, classes):
        return 0, head_of(classes, slot, head_count)

    row_spec = pl.BlockSpec((tokens, HD), rows)
    gain_spec = pl.BlockSpec((1, HD), lambda slot, classes: (0, 0))
    return pl.pallas_call(
        functools.partial(spatial_kernel, head_count),
        grid_spec=pltpu.PrefetchScalarGridSpec(
            num_scalar_prefetch=1,
            grid=(head_count,),
            in_specs=[row_spec] * 5 + [gain_spec] * 2,
            out_specs=[
                pl.BlockSpec((tokens, HD), lambda slot, classes: (0, jnp.minimum(slot, TMAX - 1))),
                pl.BlockSpec((tokens, HD), lambda slot, classes: (0, jnp.maximum(slot - TMAX, 0))),
            ],
            scratch_shapes=[
                pltpu.VMEM((2 * tokens, HD), jnp.bfloat16),
                pltpu.VMEM((2 * tokens, 2 * HD), jnp.bfloat16),
            ],
        ),
        out_shape=[
            in_hbm((tokens, TMAX * HD), jnp.bfloat16),
            in_hbm((tokens, width - TMAX * HD), jnp.bfloat16),
        ],
        cost_estimate=pl.CostEstimate(
            flops=16 * tokens * tokens * width, bytes_accessed=12 * tokens * width, transcendentals=2 * tokens * tokens * head_count
        ),
        name="spatial",
    )(head_class, query_rows, key_rows, from_hbm(other_keys), value_rows, from_hbm(other_values), query_gain, key_gain)


def temporal_kernel(head_count, first, classes, packed, after, out):
    slot = first + pl.program_id(0)
    frames, places = packed.shape[0], packed.shape[1]
    count = frames * places

    @pl.when(slot < temporal_count(classes, head_count))
    def _():
        block = packed[...]
        queries = block[:, :, :HD].reshape(count, HD)
        keys = block[:, :, HD : 2 * HD].reshape(count, HD)
        values = block[:, :, 2 * HD :].reshape(count, HD)
        row = lax.broadcasted_iota(jnp.int32, (count, count), 0)
        column = lax.broadcasted_iota(jnp.int32, (count, count), 1)
        same = (row & (places - 1)) == (column & (places - 1))
        scaled = jnp.where(same, scores_of(queries, keys) * LOG2_SCALE, -1e30)
        weights = jnp.exp2(scaled).astype(jnp.bfloat16)
        both = jnp.concatenate([values, jnp.ones_like(values)], axis=1)
        summed = jnp.dot(weights, both, preferred_element_type=jnp.float32)
        out[...] = (summed[:, :HD] / summed[:, HD:]).astype(jnp.bfloat16).reshape(out.shape)

    @pl.when(slot >= temporal_count(classes, head_count))
    def _():
        out[...] = jnp.zeros_like(out)


def temporal(head_class, packed, first, slots, after):
    frames, positions, _ = packed.shape
    places = 16
    return pl.pallas_call(
        functools.partial(temporal_kernel, head_class.shape[0], first),
        grid_spec=pltpu.PrefetchScalarGridSpec(
            num_scalar_prefetch=1,
            grid=(slots, positions // places),
            in_specs=[
                pl.BlockSpec((frames, places, 3 * HD), lambda slot, part, classes: (0, part, slot + first)),
                pl.BlockSpec(memory_space=pl.ANY),
            ],
            out_specs=pl.BlockSpec((frames, places, HD), lambda slot, part, classes: (0, part, slot)),
        ),
        out_shape=in_hbm((frames, positions, slots * HD), jnp.bfloat16),
        cost_estimate=pl.CostEstimate(
            flops=6 * frames * frames * places * positions * slots * HD,
            bytes_accessed=8 * frames * positions * slots * HD,
            transcendentals=frames * frames * places * positions * slots,
        ),
        compiler_params=pltpu.CompilerParams(vmem_limit_bytes=SMALL_VMEM),
        name="temporal",
    )(head_class, from_vmem(packed), from_hbm(after))


def weight_kernel(classes, place, weight, out):
    group_count, _, width = out.shape
    for shift in range(group_count):
        block = lax.rem(place[0] + shift, group_count)
        out[shift] = weight[:, pl.ds(pl.multiple_of(block * width, width), width)]


def weight_blocks(head_class, place, weight, group_count):
    rows, columns = weight.shape
    head_count = rows // HD
    width = columns // group_count
    return pl.pallas_call(
        weight_kernel,
        grid_spec=pltpu.PrefetchScalarGridSpec(
            num_scalar_prefetch=2,
            grid=(head_count,),
            in_specs=[pl.BlockSpec((HD, columns), lambda slot, classes, place: (head_of(classes, slot, head_count), 0))],
            out_specs=pl.BlockSpec((group_count, HD, width), lambda slot, classes, place: (0, slot, 0)),
        ),
        out_shape=in_hbm((group_count, rows, width), jnp.bfloat16),
        cost_estimate=pl.CostEstimate(flops=0, bytes_accessed=4 * rows * columns, transcendentals=0),
        name="weight_blocks",
    )(head_class, place, weight)


def choose_kernel(head_count, first, classes, returned, front, later, out, later_out):
    count = temporal_count(classes, head_count)
    for slot in range(out.shape[1] // HD):
        columns = slice(slot * HD, (slot + 1) * HD)

        @pl.when(first + slot < count)
        def _(columns=columns):
            out[:, columns] = returned[:, columns]

        @pl.when(first + slot >= count)
        def _(columns=columns):
            out[:, columns] = front[:, columns]


def choose(head_class, returned, front, first, later):
    tokens, width = returned.shape
    steps = 2
    spec = pl.BlockSpec((tokens // steps, width), lambda step, classes: (step, 0))
    front_spec = pl.BlockSpec((tokens // steps, width), lambda step, classes: (step, first * HD // width))
    anywhere = pl.BlockSpec(memory_space=pl.ANY)
    return pl.pallas_call(
        functools.partial(choose_kernel, head_class.shape[0], first),
        grid_spec=pltpu.PrefetchScalarGridSpec(
            num_scalar_prefetch=1,
            grid=(steps,),
            in_specs=[spec, front_spec, anywhere],
            out_specs=[spec, anywhere],
        ),
        out_shape=[in_hbm(returned.shape, returned.dtype), in_hbm(later.shape, later.dtype)],
        input_output_aliases={3: 1},
        cost_estimate=pl.CostEstimate(flops=0, bytes_accessed=6 * tokens * width, transcendentals=0),
        compiler_params=pltpu.CompilerParams(vmem_limit_bytes=SMALL_VMEM),
        name="choose",
    )(head_class, from_vmem(returned), from_hbm(front), from_hbm(later))


def near_kernel(with_sum, own, right, left, w_own, w_right, w_left, *rest):
    out = rest[-1]
    total = jnp.dot(own[...], w_own[...], preferred_element_type=jnp.float32)
    total += jnp.dot(right[...], w_right[...], preferred_element_type=jnp.float32)
    total += jnp.dot(left[...], w_left[...], preferred_element_type=jnp.float32)
    if with_sum:
        total += rest[0][...]
    out[...] = total.astype(out.dtype)


def far_kernel(far_top, far_bottom, w_far, total, out):
    top = pl.program_id(0) < pl.num_programs(0) // 2
    far = jnp.where(top, far_top[...], far_bottom[...])
    out[...] = (jnp.dot(far, w_far[...], preferred_element_type=jnp.float32) + total[...]).astype(out.dtype)


def project_ring(pieces, weights, row_block, total, out_dtype):
    own, right, left, far_top, far_bottom = pieces
    w_own, w_right, w_far, w_left = weights
    tokens, depth = own.shape
    width = w_own.shape[1]
    steps = 4
    block = tokens // steps
    row_spec = pl.BlockSpec((block, depth), lambda step: (step, 0))
    top_spec = pl.BlockSpec((block, depth), lambda step: (jnp.minimum(step, steps // 2 - 1), 0))
    bottom_spec = pl.BlockSpec((block, depth), lambda step: (jnp.maximum(step - steps // 2, 0), 0))
    weight_spec = pl.BlockSpec((depth, width), lambda step: (row_block, 0))
    sum_spec = pl.BlockSpec((block, width), lambda step: (step, 0))
    sums = [] if total is None else [total]
    near = pl.pallas_call(
        functools.partial(near_kernel, total is not None),
        grid=(steps,),
        in_specs=[row_spec] * 3 + [weight_spec] * 3 + [sum_spec] * len(sums),
        out_specs=sum_spec,
        out_shape=in_hbm((tokens, width), jnp.float32),
        cost_estimate=pl.CostEstimate(
            flops=6 * tokens * depth * width, bytes_accessed=6 * tokens * depth + 6 * depth * width + 8 * tokens * width, transcendentals=0
        ),
        compiler_params=pltpu.CompilerParams(vmem_limit_bytes=SMALL_VMEM),
        name="near",
    )(from_hbm(own), from_vmem(right), from_vmem(left), *[from_hbm(array) for array in (w_own, w_right, w_left, *sums)])
    return pl.pallas_call(
        far_kernel,
        grid=(steps,),
        in_specs=[top_spec, bottom_spec, weight_spec, sum_spec],
        out_specs=sum_spec,
        out_shape=in_hbm((tokens, width), out_dtype),
        cost_estimate=pl.CostEstimate(
            flops=2 * tokens * depth * width, bytes_accessed=2 * tokens * depth + 2 * depth * width + 8 * tokens * width, transcendentals=0
        ),
        compiler_params=pltpu.CompilerParams(vmem_limit_bytes=SMALL_VMEM),
        name="far",
    )(from_vmem(far_top), from_vmem(far_bottom), from_hbm(w_far), from_hbm(near))


def gathered_kernel(with_sum, place, *refs):
    out = refs[-1]
    group_count = (len(refs) - 1 - with_sum) // 2
    total = refs[2 * group_count][...] if with_sum else jnp.zeros(out.shape, jnp.float32)
    for by in range(group_count):
        total += jnp.dot(refs[by][0], refs[group_count + by][...], preferred_element_type=jnp.float32)
    out[...] = total


def project_gathered(place, gathered, weights, row_block, total):
    group_count, tokens, depth = gathered.shape
    width = weights[0].shape[1]
    steps = 4
    block = tokens // steps

    def rows(by):
        return pl.BlockSpec((1, block, depth), lambda step, place: (lax.rem(place[0] + group_count - by, group_count), step, 0))

    weight_spec = pl.BlockSpec((depth, width), lambda step, place: (row_block, 0))
    sum_spec = pl.BlockSpec((block, width), lambda step, place: (step, 0))
    sums = [] if total is None else [total]
    return pl.pallas_call(
        functools.partial(gathered_kernel, len(sums)),
        grid_spec=pltpu.PrefetchScalarGridSpec(
            num_scalar_prefetch=1,
            grid=(steps,),
            in_specs=[rows(by) for by in range(group_count)] + [weight_spec] * group_count + [sum_spec] * len(sums),
            out_specs=sum_spec,
        ),
        out_shape=in_hbm((tokens, width), jnp.float32),
        cost_estimate=pl.CostEstimate(
            flops=8 * tokens * depth * width, bytes_accessed=8 * tokens * depth + 8 * depth * width + 8 * tokens * width, transcendentals=0
        ),
        name="project",
    )(place, *[from_hbm(gathered)] * group_count, *[from_hbm(array) for array in (*weights, *sums)])


def shifted(block, by):
    count = lax.axis_size("head")
    return lax.ppermute(block, "head", [(at, (at + by) % count) for at in range(count)])


def ring(block):
    half = block.shape[0] // 2
    right, left = shifted(block, 1), shifted(block, -1)
    return block, right, left, shifted(right[:half], 1), shifted(left[half:], -1)


def other_core(block):
    count = lax.axis_size("seq")
    return lax.ppermute(block, "seq", [(at, at ^ 1) for at in range(count)])


def over_frames(blocks):
    count = lax.axis_size("seq")
    groups = [list(range(core, count, CORES)) for core in range(CORES)]
    return lax.all_to_all(blocks, "seq", 0, 0, axis_index_groups=groups)


def body(query_rows, key_rows, value_rows, query_gain, key_gain, head_class, out_weight):
    tokens = query_rows.shape[0]
    group_count = lax.axis_size("head")
    query_gain = query_gain.reshape(1, HD)
    key_gain = key_gain.reshape(1, HD)
    packed = pack(head_class, query_rows, key_rows, value_rows, query_gain, key_gain)
    arrived = over_frames(packed.reshape(FRAMES, tokens // FRAMES, TMAX * 3 * HD))

    other_keys, other_values = other_core(key_rows), other_core(value_rows)
    front, back = spatial(head_class, query_rows, key_rows, other_keys, value_rows, other_values, query_gain, key_gain)
    place = lax.axis_index("head").reshape(1).astype(jnp.int32)
    blocks = weight_blocks(head_class, place, out_weight, group_count)
    weights = [blocks[0]] + [shifted(blocks[by], by) for by in range(1, group_count)]
    early = project_gathered(place, lax.all_gather(back, "head"), weights, TMAX // 2, None)

    half = TMAX // 2
    sent = [temporal(head_class, arrived, part * half, half, early) for part in range(2)]
    returned = over_frames(sent[0]).reshape(tokens, half * HD)
    chosen, later = choose(head_class, returned, front, 0, sent[1])
    total = project_gathered(place, lax.all_gather(chosen, "head"), weights, 0, early)
    returned = over_frames(later).reshape(tokens, half * HD)
    chosen, _ = choose(head_class, returned, front, half, jnp.zeros((8, HD), jnp.float32))
    return project_ring(ring(chosen), weights, 1, total, jnp.bfloat16)


def solution(mesh):
    return jax.shard_map(
        body,
        mesh=mesh,
        in_specs=(
            P("seq", "head"),
            P("seq", "head"),
            P("seq", "head"),
            P(),
            P(),
            P("head"),
            P("head", None),
        ),
        out_specs=P("seq", "head"),
        check_vma=False,
    )
```

```python
import functools
import math

import jax
import jax.numpy as jnp
from jax import lax
from jax.experimental import pallas as pl
from jax.experimental.pallas import tpu as pltpu
from jax.sharding import PartitionSpec as P

FRAMES = 32
TMAX = 4
SMALL_VMEM = 16 * 1024 * 1024
CORES = 2
HD = 128
EPSILON = 1e-06
LOG2_SCALE = math.log2(math.e) / math.sqrt(HD)


def in_hbm(shape, dtype):
    return pltpu.HBM(shape, dtype)


def from_hbm(array):
    return pltpu.with_memory_space_constraint(array, pltpu.HBM)


def from_vmem(array):
    return pltpu.with_memory_space_constraint(array, pltpu.VMEM)


def temporal_count(classes, head_count):
    total = classes[0]
    for head in range(1, head_count):
        total = total + classes[head]
    return total


def head_of(classes, slot, head_count):
    temporal_seen = jnp.int32(0)
    spatial_seen = temporal_count(classes, head_count)
    found = jnp.int32(0)
    for head in range(head_count):
        kind = classes[head]
        rank = jnp.where(kind == 1, temporal_seen, spatial_seen)
        found = jnp.where(rank == slot, jnp.int32(head), found)
        temporal_seen = temporal_seen + kind
        spatial_seen = spatial_seen + 1 - kind
    return found


def normed(rows, gain):
    widened = rows.astype(jnp.float32)
    mean = jnp.mean(widened * widened, axis=-1, keepdims=True)
    return (widened * lax.rsqrt(mean + EPSILON) * gain).astype(jnp.bfloat16)


def scores_of(queries, keys):
    return lax.dot_general(queries, keys, (((1,), (1,)), ((), ())), preferred_element_type=jnp.float32)


def pack_kernel(head_count, classes, query, key, value, query_gain, key_gain, out, raw, ready, in_sems, out_sems):
    heads = [head_of(classes, slot, head_count) for slot in range(TMAX)]
    gains = (query_gain, key_gain, None)
    loads, stores = [], []
    for at in range(3 * TMAX):
        slot, which = divmod(at, 3)
        source = (query, key, value)[which].at[:, pl.ds(pl.multiple_of(heads[slot] * HD, HD), HD)]
        landing = raw if gains[which] is not None else ready
        loads.append(pltpu.make_async_copy(source, landing.at[at], in_sems.at[at]))
        loads[-1].start()
    for at in range(3 * TMAX):
        gain = gains[at % 3]
        loads[at].wait()
        if gain is not None:
            ready[at] = normed(raw[at], gain[...])
        stores.append(pltpu.make_async_copy(ready.at[at], out.at[:, pl.ds(at * HD, HD)], out_sems.at[at]))
        stores[-1].start()
    for store in stores:
        store.wait()


def pack(head_class, query_rows, key_rows, value_rows, query_gain, key_gain):
    tokens, width = query_rows.shape
    anywhere = pl.BlockSpec(memory_space=pl.ANY)
    gain_spec = pl.BlockSpec((1, HD), lambda step, classes: (0, 0))
    return pl.pallas_call(
        functools.partial(pack_kernel, width // HD),
        grid_spec=pltpu.PrefetchScalarGridSpec(
            num_scalar_prefetch=1,
            grid=(1,),
            in_specs=[anywhere] * 3 + [gain_spec] * 2,
            out_specs=anywhere,
            scratch_shapes=[
                pltpu.VMEM((3 * TMAX, tokens, HD), jnp.bfloat16),
                pltpu.VMEM((3 * TMAX, tokens, HD), jnp.bfloat16),
                pltpu.SemaphoreType.DMA((3 * TMAX,)),
                pltpu.SemaphoreType.DMA((3 * TMAX,)),
            ],
        ),
        out_shape=in_hbm((tokens, TMAX * 3 * HD), jnp.bfloat16),
        cost_estimate=pl.CostEstimate(flops=8 * tokens * TMAX * HD, bytes_accessed=12 * tokens * TMAX * HD, transcendentals=0),
        name="pack",
    )(head_class, from_hbm(query_rows), from_hbm(key_rows), from_hbm(value_rows), query_gain, key_gain)


def spatial_kernel(head_count, classes, query, key, other_key, value, other_value, query_gain, key_gain, out, keys, values):
    slot = pl.program_id(0)
    tokens = query.shape[0]
    chunk = tokens // 4

    @pl.when(slot >= temporal_count(classes, head_count))
    def _():
        keys[:tokens] = normed(key[...], key_gain[...])
        keys[tokens:] = normed(other_key[...], key_gain[...])
        values[:tokens, :HD] = value[...]
        values[tokens:, :HD] = other_value[...]
        values[:, HD:] = jnp.ones((2 * tokens, HD), jnp.bfloat16)

        def step(index, carry):
            rows = pl.ds(pl.multiple_of(index * chunk, chunk), chunk)
            queries = normed(query[rows, :], query_gain[...])
            weights = jnp.exp2(scores_of(queries, keys[...]) * LOG2_SCALE).astype(jnp.bfloat16)
            summed = jnp.dot(weights, values[...], preferred_element_type=jnp.float32)
            out[rows, :] = (summed[:, :HD] / summed[:, HD:]).astype(jnp.bfloat16)
            return carry

        lax.fori_loop(0, tokens // chunk, step, 0)

    @pl.when(slot < temporal_count(classes, head_count))
    def _():
        out[...] = jnp.zeros_like(out)


def spatial(head_class, query_rows, key_rows, other_keys, value_rows, other_values, query_gain, key_gain):
    tokens, width = query_rows.shape
    head_count = width // HD

    def rows(slot, classes):
        return 0, head_of(classes, slot, head_count)

    row_spec = pl.BlockSpec((tokens, HD), rows)
    gain_spec = pl.BlockSpec((1, HD), lambda slot, classes: (0, 0))
    return pl.pallas_call(
        functools.partial(spatial_kernel, head_count),
        grid_spec=pltpu.PrefetchScalarGridSpec(
            num_scalar_prefetch=1,
            grid=(head_count,),
            in_specs=[row_spec] * 5 + [gain_spec] * 2,
            out_specs=pl.BlockSpec((tokens, HD), lambda slot, classes: (0, slot)),
            scratch_shapes=[
                pltpu.VMEM((2 * tokens, HD), jnp.bfloat16),
                pltpu.VMEM((2 * tokens, 2 * HD), jnp.bfloat16),
            ],
        ),
        out_shape=in_hbm((tokens, width), jnp.bfloat16),
        cost_estimate=pl.CostEstimate(
            flops=16 * tokens * tokens * width, bytes_accessed=12 * tokens * width, transcendentals=2 * tokens * tokens * head_count
        ),
        name="spatial",
    )(head_class, query_rows, key_rows, from_hbm(other_keys), value_rows, from_hbm(other_values), query_gain, key_gain)


def temporal_kernel(head_count, classes, packed, *rest):
    out = rest[-1]
    slot = pl.program_id(0)
    frames, positions, _ = packed.shape
    places = 16
    count = frames * places

    @pl.when(slot < temporal_count(classes, head_count))
    def _():
        row = lax.broadcasted_iota(jnp.int32, (count, count), 0)
        column = lax.broadcasted_iota(jnp.int32, (count, count), 1)
        same = (row & (places - 1)) == (column & (places - 1))
        base = pl.multiple_of(slot * 3 * HD, HD)
        for part in range(positions // places):
            at = slice(part * places, (part + 1) * places)
            queries, keys, values = (packed[:, at, pl.ds(base + which * HD, HD)].reshape(count, HD) for which in range(3))
            scaled = jnp.where(same, scores_of(queries, keys) * LOG2_SCALE, -1e30)
            weights = jnp.exp2(scaled).astype(jnp.bfloat16)
            both = jnp.concatenate([values, jnp.ones_like(values)], axis=1)
            summed = jnp.dot(weights, both, preferred_element_type=jnp.float32)
            out[:, at, :] = (summed[:, :HD] / summed[:, HD:]).astype(jnp.bfloat16).reshape(frames, places, HD)

    @pl.when(slot >= temporal_count(classes, head_count))
    def _():
        out[...] = jnp.zeros_like(out)


def temporal(head_class, packed, after):
    frames, positions, _ = packed.shape
    return pl.pallas_call(
        functools.partial(temporal_kernel, head_class.shape[0]),
        grid_spec=pltpu.PrefetchScalarGridSpec(
            num_scalar_prefetch=1,
            grid=(TMAX,),
            in_specs=[pl.BlockSpec(memory_space=pltpu.VMEM)] + [pl.BlockSpec(memory_space=pl.ANY)] * len(after),
            out_specs=pl.BlockSpec((frames, positions, HD), lambda slot, classes: (0, 0, slot)),
        ),
        out_shape=in_hbm((frames, positions, TMAX * HD), jnp.bfloat16),
        compiler_params=pltpu.CompilerParams(vmem_limit_bytes=SMALL_VMEM),
        cost_estimate=pl.CostEstimate(
            flops=64 * frames * frames * positions * TMAX * HD,
            bytes_accessed=8 * frames * positions * TMAX * HD,
            transcendentals=16 * frames * frames * positions * TMAX,
        ),
        name="temporal",
    )(head_class, from_vmem(packed), *[from_hbm(array) for array in after])


def weight_kernel(classes, place, weight, out):
    group_count, _, width = out.shape
    for shift in range(group_count):
        block = lax.rem(place[0] + shift, group_count)
        out[shift] = weight[:, pl.ds(pl.multiple_of(block * width, width), width)]


def weight_blocks(head_class, place, weight, group_count):
    rows, columns = weight.shape
    head_count = rows // HD
    width = columns // group_count
    return pl.pallas_call(
        weight_kernel,
        grid_spec=pltpu.PrefetchScalarGridSpec(
            num_scalar_prefetch=2,
            grid=(head_count,),
            in_specs=[pl.BlockSpec((HD, columns), lambda slot, classes, place: (head_of(classes, slot, head_count), 0))],
            out_specs=pl.BlockSpec((group_count, HD, width), lambda slot, classes, place: (0, slot, 0)),
        ),
        out_shape=in_hbm((group_count, rows, width), jnp.bfloat16),
        cost_estimate=pl.CostEstimate(flops=0, bytes_accessed=4 * rows * columns, transcendentals=0),
        name="weight_blocks",
    )(head_class, place, weight)


def early_kernel(own, right_top, right_bottom, left_top, left_bottom, far_top, far_bottom, w_own, w_right, w_far, w_left, out):
    top = pl.program_id(0) < pl.num_programs(0) // 2
    total = jnp.dot(own[...], w_own[...], preferred_element_type=jnp.float32)
    for upper, lower, weight in ((right_top, right_bottom, w_right), (left_top, left_bottom, w_left), (far_top, far_bottom, w_far)):
        rows = jnp.where(top, upper[...], lower[...])
        total += jnp.dot(rows, weight[...], preferred_element_type=jnp.float32)
    out[...] = total


def project_early(pieces, weights):
    tokens, depth = pieces[0].shape
    width = weights[0].shape[1]
    steps = 4
    block = tokens // steps
    row_spec = pl.BlockSpec((block, depth), lambda step: (step, 0))
    top_spec = pl.BlockSpec((block, depth), lambda step: (jnp.minimum(step, steps // 2 - 1), 0))
    bottom_spec = pl.BlockSpec((block, depth), lambda step: (jnp.maximum(step - steps // 2, 0), 0))
    weight_spec = pl.BlockSpec((depth, width), lambda step: (0, 0))
    return pl.pallas_call(
        early_kernel,
        grid=(steps,),
        in_specs=[row_spec] + [top_spec, bottom_spec] * 3 + [weight_spec] * 4,
        out_specs=pl.BlockSpec((block, width), lambda step: (step, 0)),
        out_shape=in_hbm((tokens, width), jnp.float32),
        compiler_params=pltpu.CompilerParams(vmem_limit_bytes=2 * SMALL_VMEM),
        cost_estimate=pl.CostEstimate(
            flops=8 * tokens * depth * width, bytes_accessed=8 * tokens * depth + 8 * depth * width + 4 * tokens * width, transcendentals=0
        ),
        name="project_early",
    )(*[from_hbm(array) for array in (*pieces, *weights)])


def near_kernel(own, right_top, right_bottom, left_top, left_bottom, w_own, w_right, w_left, total, out):
    depth = own.shape[1]
    half = own.shape[0] // 2
    for part, right, left in ((0, right_top, left_top), (1, right_bottom, left_bottom)):
        rows = slice(part * half, (part + 1) * half)
        summed = total[rows] + jnp.dot(own[rows], w_own[:depth], preferred_element_type=jnp.float32)
        summed += jnp.dot(right[...], w_right[:depth], preferred_element_type=jnp.float32)
        summed += jnp.dot(left[...], w_left[:depth], preferred_element_type=jnp.float32)
        out[rows] = summed


def far_kernel(far_top, far_bottom, w_far, total, out):
    depth = far_top.shape[1]

    @pl.when(pl.program_id(0) == 0)
    def _():
        out[...] = (jnp.dot(far_top[...], w_far[:depth], preferred_element_type=jnp.float32) + total[...]).astype(out.dtype)

    @pl.when(pl.program_id(0) == 1)
    def _():
        out[...] = (jnp.dot(far_bottom[...], w_far[:depth], preferred_element_type=jnp.float32) + total[...]).astype(out.dtype)


def project_late(pieces, weights, total):
    tokens, depth = pieces[0].shape
    rows, width = weights[0].shape
    half = tokens // 2
    whole = pl.BlockSpec(memory_space=pltpu.VMEM)
    w_own, w_right, w_far, w_left = weights
    near = pl.pallas_call(
        near_kernel,
        in_specs=[whole] * 9,
        out_specs=whole,
        out_shape=pltpu.VMEM((tokens, width), jnp.float32),
        compiler_params=pltpu.CompilerParams(vmem_limit_bytes=SMALL_VMEM),
        cost_estimate=pl.CostEstimate(
            flops=6 * tokens * depth * width, bytes_accessed=6 * tokens * depth + 6 * depth * width + 8 * tokens * width, transcendentals=0
        ),
        name="near",
    )(*[from_vmem(array) for array in (*pieces[:5], w_own, w_right, w_left, total)])
    sum_spec = pl.BlockSpec((half, width), lambda step: (step, 0))
    return pl.pallas_call(
        far_kernel,
        grid=(2,),
        in_specs=[whole] * 3 + [sum_spec],
        out_specs=sum_spec,
        out_shape=in_hbm((tokens, width), jnp.bfloat16),
        compiler_params=pltpu.CompilerParams(vmem_limit_bytes=SMALL_VMEM),
        cost_estimate=pl.CostEstimate(
            flops=2 * tokens * depth * width, bytes_accessed=2 * tokens * depth + 2 * depth * width + 8 * tokens * width, transcendentals=0
        ),
        name="far",
    )(*[from_vmem(array) for array in (*pieces[5:], w_far, near)])


def shifted(block, by):
    count = lax.axis_size("head")
    return lax.ppermute(block, "head", [(at, (at + by) % count) for at in range(count)])


def ring(block):
    half = block.shape[0] // 2
    top, bottom = block[:half], block[half:]
    right_top, left_bottom = shifted(top, 1), shifted(bottom, -1)
    right_bottom, left_top = shifted(bottom, 1), shifted(top, -1)
    far_top, far_bottom = shifted(right_top, 1), shifted(left_bottom, -1)
    return block, right_top, right_bottom, left_top, left_bottom, far_top, far_bottom


def other_core(block):
    count = lax.axis_size("seq")
    return lax.ppermute(block, "seq", [(at, at ^ 1) for at in range(count)])


def over_frames(blocks):
    count = lax.axis_size("seq")
    groups = [list(range(core, count, CORES)) for core in range(CORES)]
    return lax.all_to_all(blocks, "seq", 0, 0, axis_index_groups=groups)


def body(query_rows, key_rows, value_rows, query_gain, key_gain, head_class, out_weight):
    tokens = query_rows.shape[0]
    group_count = lax.axis_size("head")
    query_gain = query_gain.reshape(1, HD)
    key_gain = key_gain.reshape(1, HD)
    packed = pack(head_class, query_rows, key_rows, value_rows, query_gain, key_gain)
    arrived = over_frames(packed.reshape(FRAMES, tokens // FRAMES, TMAX * 3 * HD))

    other_keys, other_values = other_core(key_rows), other_core(value_rows)
    near_out = spatial(head_class, query_rows, key_rows, other_keys, value_rows, other_values, query_gain, key_gain)
    place = lax.axis_index("head").reshape(1).astype(jnp.int32)
    blocks = weight_blocks(head_class, place, out_weight, group_count)

    core = lax.rem(lax.axis_index("seq"), CORES)
    half = blocks.shape[1] // CORES
    mine = lax.dynamic_slice_in_dim(blocks, core * half, half, axis=1)
    fetched = jnp.stack([shifted(mine[by], by) for by in range(1, group_count)])
    rest = other_core(fetched)
    others = jnp.where(core == 0, jnp.concatenate([fetched, rest], axis=1), jnp.concatenate([rest, fetched], axis=1))
    weights = [blocks[0]] + [others[by] for by in range(group_count - 1)]

    pieces = ring(near_out)
    returned = over_frames(temporal(head_class, arrived, (*pieces[1:5], others))).reshape(tokens, TMAX * HD)
    early = project_early(pieces, weights)
    return project_late(ring(returned), weights, early)


def solution(mesh):
    return jax.shard_map(
        body,
        mesh=mesh,
        in_specs=(
            P("seq", "head"),
            P("seq", "head"),
            P("seq", "head"),
            P(),
            P(),
            P("head"),
            P("head", None),
        ),
        out_specs=P("seq", "head"),
        check_vma=False,
    )
```

```python
import functools
import math

import jax
import jax.numpy as jnp
from jax import lax
from jax.experimental import pallas as pl
from jax.experimental.pallas import tpu as pltpu
from jax.sharding import PartitionSpec as P

FRAMES = 32
TMAX = 4
SMALL_VMEM = 16 * 1024 * 1024
CORES = 2
HD = 128
EPSILON = 1e-06
LOG2_SCALE = math.log2(math.e) / math.sqrt(HD)


def in_hbm(shape, dtype):
    return pltpu.HBM(shape, dtype)


def from_hbm(array):
    return pltpu.with_memory_space_constraint(array, pltpu.HBM)


def from_vmem(array):
    return pltpu.with_memory_space_constraint(array, pltpu.VMEM)


def temporal_count(classes, head_count):
    total = classes[0]
    for head in range(1, head_count):
        total = total + classes[head]
    return total


def head_of(classes, slot, head_count):
    temporal_seen = jnp.int32(0)
    spatial_seen = temporal_count(classes, head_count)
    found = jnp.int32(0)
    for head in range(head_count):
        kind = classes[head]
        rank = jnp.where(kind == 1, temporal_seen, spatial_seen)
        found = jnp.where(rank == slot, jnp.int32(head), found)
        temporal_seen = temporal_seen + kind
        spatial_seen = spatial_seen + 1 - kind
    return found


def normed(rows, gain):
    widened = rows.astype(jnp.float32)
    mean = jnp.mean(widened * widened, axis=-1, keepdims=True)
    return (widened * lax.rsqrt(mean + EPSILON) * gain).astype(jnp.bfloat16)


def scores_of(queries, keys):
    return lax.dot_general(queries, keys, (((1,), (1,)), ((), ())), preferred_element_type=jnp.float32)


def hold_kernel(*refs):
    pass


def hold(arrays, after):
    anywhere = pl.BlockSpec(memory_space=pl.ANY)
    return pl.pallas_call(
        hold_kernel,
        in_specs=[anywhere] * (len(arrays) + len(after)),
        out_specs=[anywhere] * len(arrays),
        out_shape=[in_hbm(array.shape, array.dtype) for array in arrays],
        input_output_aliases={at: at for at in range(len(arrays))},
        cost_estimate=pl.CostEstimate(flops=0, bytes_accessed=0, transcendentals=0),
        name="hold",
    )(*[from_hbm(array) for array in (*arrays, *after)])


def pack_kernel(head_count, classes, query, key, value, query_gain, key_gain, out, raw, ready, in_sems, out_sems):
    heads = [head_of(classes, slot, head_count) for slot in range(TMAX)]
    gains = (query_gain, key_gain, None)
    loads, stores = [], []
    for at in range(3 * TMAX):
        slot, which = divmod(at, 3)
        source = (query, key, value)[which].at[:, pl.ds(pl.multiple_of(heads[slot] * HD, HD), HD)]
        landing = raw if gains[which] is not None else ready
        loads.append(pltpu.make_async_copy(source, landing.at[at], in_sems.at[at]))
        loads[-1].start()
    for at in range(3 * TMAX):
        gain = gains[at % 3]
        loads[at].wait()
        if gain is not None:
            ready[at] = normed(raw[at], gain[...])
        stores.append(pltpu.make_async_copy(ready.at[at], out.at[:, pl.ds(at * HD, HD)], out_sems.at[at]))
        stores[-1].start()
    for store in stores:
        store.wait()


def pack(head_class, query_rows, key_rows, value_rows, query_gain, key_gain):
    tokens, width = query_rows.shape
    anywhere = pl.BlockSpec(memory_space=pl.ANY)
    gain_spec = pl.BlockSpec((1, HD), lambda step, classes: (0, 0))
    return pl.pallas_call(
        functools.partial(pack_kernel, width // HD),
        grid_spec=pltpu.PrefetchScalarGridSpec(
            num_scalar_prefetch=1,
            grid=(1,),
            in_specs=[anywhere] * 3 + [gain_spec] * 2,
            out_specs=anywhere,
            scratch_shapes=[
                pltpu.VMEM((3 * TMAX, tokens, HD), jnp.bfloat16),
                pltpu.VMEM((3 * TMAX, tokens, HD), jnp.bfloat16),
                pltpu.SemaphoreType.DMA((3 * TMAX,)),
                pltpu.SemaphoreType.DMA((3 * TMAX,)),
            ],
        ),
        out_shape=in_hbm((tokens, TMAX * 3 * HD), jnp.bfloat16),
        cost_estimate=pl.CostEstimate(flops=8 * tokens * TMAX * HD, bytes_accessed=12 * tokens * TMAX * HD, transcendentals=0),
        name="pack",
    )(head_class, from_hbm(query_rows), from_hbm(key_rows), from_hbm(value_rows), query_gain, key_gain)


def spatial_kernel(head_count, classes, query, key, other_key, value, other_value, query_gain, key_gain, front, back, keys, values):
    slot = pl.program_id(0)
    tokens = query.shape[0]
    chunk = tokens // 4
    is_front = slot < TMAX

    @pl.when(slot >= temporal_count(classes, head_count))
    def _():
        keys[:tokens] = normed(key[...], key_gain[...])
        keys[tokens:] = normed(other_key[...], key_gain[...])
        values[:tokens, :HD] = value[...]
        values[tokens:, :HD] = other_value[...]
        values[:, HD:] = jnp.ones((2 * tokens, HD), jnp.bfloat16)

        def step(index, carry):
            rows = pl.ds(pl.multiple_of(index * chunk, chunk), chunk)
            queries = normed(query[rows, :], query_gain[...])
            weights = jnp.exp2(scores_of(queries, keys[...]) * LOG2_SCALE).astype(jnp.bfloat16)
            summed = jnp.dot(weights, values[...], preferred_element_type=jnp.float32)
            result = (summed[:, :HD] / summed[:, HD:]).astype(jnp.bfloat16)

            @pl.when(is_front)
            def _():
                front[rows, :] = result

            @pl.when(jnp.logical_not(is_front))
            def _():
                back[rows, :] = result

            return carry

        lax.fori_loop(0, tokens // chunk, step, 0)

    @pl.when(slot < temporal_count(classes, head_count))
    def _():
        front[...] = jnp.zeros_like(front)


def spatial(head_class, query_rows, key_rows, other_keys, value_rows, other_values, query_gain, key_gain):
    tokens, width = query_rows.shape
    head_count = width // HD

    def rows(slot, classes):
        return 0, head_of(classes, slot, head_count)

    row_spec = pl.BlockSpec((tokens, HD), rows)
    gain_spec = pl.BlockSpec((1, HD), lambda slot, classes: (0, 0))
    return pl.pallas_call(
        functools.partial(spatial_kernel, head_count),
        grid_spec=pltpu.PrefetchScalarGridSpec(
            num_scalar_prefetch=1,
            grid=(head_count,),
            in_specs=[row_spec] * 5 + [gain_spec] * 2,
            out_specs=[
                pl.BlockSpec((tokens, HD), lambda slot, classes: (0, jnp.minimum(slot, TMAX - 1))),
                pl.BlockSpec((tokens, HD), lambda slot, classes: (0, jnp.maximum(slot - TMAX, 0))),
            ],
            scratch_shapes=[
                pltpu.VMEM((2 * tokens, HD), jnp.bfloat16),
                pltpu.VMEM((2 * tokens, 2 * HD), jnp.bfloat16),
            ],
        ),
        out_shape=[
            in_hbm((tokens, TMAX * HD), jnp.bfloat16),
            in_hbm((tokens, width - TMAX * HD), jnp.bfloat16),
        ],
        cost_estimate=pl.CostEstimate(
            flops=16 * tokens * tokens * width, bytes_accessed=12 * tokens * width, transcendentals=2 * tokens * tokens * head_count
        ),
        name="spatial",
    )(head_class, query_rows, key_rows, from_hbm(other_keys), value_rows, from_hbm(other_values), query_gain, key_gain)


def temporal_kernel(head_count, classes, packed, *rest):
    out = rest[-1]
    slot = pl.program_id(0)
    frames, positions, _ = packed.shape
    places = 16
    count = frames * places

    @pl.when(slot < temporal_count(classes, head_count))
    def _():
        row = lax.broadcasted_iota(jnp.int32, (count, count), 0)
        column = lax.broadcasted_iota(jnp.int32, (count, count), 1)
        same = (row & (places - 1)) == (column & (places - 1))
        base = pl.multiple_of(slot * 3 * HD, HD)
        for part in range(positions // places):
            at = slice(part * places, (part + 1) * places)
            queries, keys, values = (packed[:, at, pl.ds(base + which * HD, HD)].reshape(count, HD) for which in range(3))
            scaled = jnp.where(same, scores_of(queries, keys) * LOG2_SCALE, -1e30)
            weights = jnp.exp2(scaled).astype(jnp.bfloat16)
            both = jnp.concatenate([values, jnp.ones_like(values)], axis=1)
            summed = jnp.dot(weights, both, preferred_element_type=jnp.float32)
            out[:, at, :] = (summed[:, :HD] / summed[:, HD:]).astype(jnp.bfloat16).reshape(frames, places, HD)

    @pl.when(slot >= temporal_count(classes, head_count))
    def _():
        out[...] = jnp.zeros_like(out)


def temporal(head_class, packed, after):
    frames, positions, _ = packed.shape
    return pl.pallas_call(
        functools.partial(temporal_kernel, head_class.shape[0]),
        grid_spec=pltpu.PrefetchScalarGridSpec(
            num_scalar_prefetch=1,
            grid=(TMAX,),
            in_specs=[pl.BlockSpec(memory_space=pltpu.VMEM)] + [pl.BlockSpec(memory_space=pl.ANY)] * len(after),
            out_specs=pl.BlockSpec((frames, positions, HD), lambda slot, classes: (0, 0, slot)),
        ),
        out_shape=in_hbm((frames, positions, TMAX * HD), jnp.bfloat16),
        compiler_params=pltpu.CompilerParams(vmem_limit_bytes=SMALL_VMEM),
        cost_estimate=pl.CostEstimate(
            flops=64 * frames * frames * positions * TMAX * HD,
            bytes_accessed=8 * frames * positions * TMAX * HD,
            transcendentals=16 * frames * frames * positions * TMAX,
        ),
        name="temporal",
    )(head_class, from_vmem(packed), *[from_hbm(array) for array in after])


def weight_kernel(classes, place, weight, own, *others):
    width = own.shape[1]
    group_count = len(others) + 1

    def columns(shift):
        block = lax.rem(place[0] + shift, group_count)
        return weight[:, pl.ds(pl.multiple_of(block * width, width), width)]

    own[...] = columns(0)

    @pl.when(pl.program_id(0) // (pl.num_programs(0) // CORES) == place[1])
    def _():
        for shift, other in enumerate(others):
            other[...] = columns(shift + 1)


def weight_blocks(head_class, place, weight, group_count):
    rows, columns = weight.shape
    head_count = rows // HD
    share = head_count // CORES
    width = columns // group_count

    def half_rows(slot, classes, place):
        return jnp.clip(slot - place[1] * share, 0, share - 1), 0

    return pl.pallas_call(
        weight_kernel,
        grid_spec=pltpu.PrefetchScalarGridSpec(
            num_scalar_prefetch=2,
            grid=(head_count,),
            in_specs=[pl.BlockSpec((HD, columns), lambda slot, classes, place: (head_of(classes, slot, head_count), 0))],
            out_specs=[pl.BlockSpec((HD, width), lambda slot, classes, place: (slot, 0))]
            + [pl.BlockSpec((HD, width), half_rows)] * (group_count - 1),
        ),
        out_shape=[in_hbm((rows, width), jnp.bfloat16)] + [in_hbm((rows // CORES, width), jnp.bfloat16)] * (group_count - 1),
        cost_estimate=pl.CostEstimate(flops=0, bytes_accessed=4 * rows * columns, transcendentals=0),
        name="weight_blocks",
    )(head_class, place, weight)


def product(rows, weight, first):
    return jnp.dot(rows, weight[first : first + rows.shape[1]], preferred_element_type=jnp.float32)


def near_sum(own, right, left, w_own, w_others, first):
    return product(own[...], w_own, first) + product(right[...], w_others.at[0], first) + product(left[...], w_others.at[2], first)


def early_kernel(first, own_top, own_bottom, right_top, right_bottom, left_top, left_bottom, far_top, far_bottom, w_own, w_others, out):
    half = own_top.shape[0]
    parts = ((own_top, right_top, left_top, far_top), (own_bottom, right_bottom, left_bottom, far_bottom))
    for part, (own, right, left, far) in enumerate(parts):
        total = near_sum(own, right, left, w_own, w_others, first) + product(far[...], w_others.at[1], first)
        out[part * half : (part + 1) * half] = total


def near_kernel(own_top, own_bottom, right_top, right_bottom, left_top, left_bottom, w_own, w_others, total, out):
    half = own_top.shape[0]
    for part, (own, right, left) in enumerate(((own_top, right_top, left_top), (own_bottom, right_bottom, left_bottom))):
        rows = slice(part * half, (part + 1) * half)
        out[rows] = total[rows] + near_sum(own, right, left, w_own, w_others, 0)


def far_kernel(far_top, far_bottom, w_others, total, out):
    for part, far in enumerate((far_top, far_bottom)):

        @pl.when(pl.program_id(0) == part)
        def _(far=far):
            out[...] = (product(far[...], w_others.at[1], 0) + total[...]).astype(out.dtype)


def summing(kernel, name, operands, depth_terms):
    tokens, width = 2 * operands[0].shape[0], operands[-1].shape[-1]
    depth = operands[0].shape[1]
    whole = pl.BlockSpec(memory_space=pltpu.VMEM)
    return pl.pallas_call(
        kernel,
        in_specs=[whole] * len(operands),
        out_specs=whole,
        out_shape=pltpu.VMEM((tokens, width), jnp.float32),
        compiler_params=pltpu.CompilerParams(vmem_limit_bytes=SMALL_VMEM),
        cost_estimate=pl.CostEstimate(
            flops=2 * depth_terms * tokens * depth * width, bytes_accessed=8 * tokens * width, transcendentals=0
        ),
        name=name,
    )(*[from_vmem(array) for array in operands])


def project_early(pieces, w_own, w_others):
    first = TMAX * HD
    return summing(functools.partial(early_kernel, first), "project_early", (*pieces, w_own, w_others), 4)


def project_late(pieces, w_own, w_others, total):
    near = summing(near_kernel, "near", (*pieces[:6], w_own, w_others, total), 3)
    tokens, width = near.shape
    half, depth = pieces[0].shape
    whole = pl.BlockSpec(memory_space=pltpu.VMEM)
    sum_spec = pl.BlockSpec((half, width), lambda step: (step, 0))
    return pl.pallas_call(
        far_kernel,
        grid=(2,),
        in_specs=[whole] * 3 + [sum_spec],
        out_specs=sum_spec,
        out_shape=in_hbm((tokens, width), jnp.bfloat16),
        compiler_params=pltpu.CompilerParams(vmem_limit_bytes=SMALL_VMEM),
        cost_estimate=pl.CostEstimate(flops=2 * tokens * depth * width, bytes_accessed=8 * tokens * width, transcendentals=0),
        name="far",
    )(*[from_vmem(array) for array in (*pieces[6:], w_others, near)])


def shifted(block, by):
    count = lax.axis_size("head")
    return lax.ppermute(block, "head", [(at, (at + by) % count) for at in range(count)])


def ring(top, bottom):
    right_top, left_bottom = shifted(top, 1), shifted(bottom, -1)
    right_bottom, left_top = shifted(bottom, 1), shifted(top, -1)
    far_top, far_bottom = shifted(right_top, 1), shifted(left_bottom, -1)
    return top, bottom, right_top, right_bottom, left_top, left_bottom, far_top, far_bottom


def other_core(block):
    count = lax.axis_size("seq")
    return lax.ppermute(block, "seq", [(at, at ^ 1) for at in range(count)])


def over_frames(blocks):
    count = lax.axis_size("seq")
    groups = [list(range(core, count, CORES)) for core in range(CORES)]
    return lax.all_to_all(blocks, "seq", 0, 0, axis_index_groups=groups)


def body(query_rows, key_rows, value_rows, query_gain, key_gain, head_class, out_weight):
    tokens = query_rows.shape[0]
    group_count = lax.axis_size("head")
    query_gain = query_gain.reshape(1, HD)
    key_gain = key_gain.reshape(1, HD)
    packed = pack(head_class, query_rows, key_rows, value_rows, query_gain, key_gain)
    arrived = over_frames(packed.reshape(FRAMES, tokens // FRAMES, TMAX * 3 * HD))

    other_keys, other_values = other_core(key_rows), other_core(value_rows)
    front, back = spatial(head_class, query_rows, key_rows, other_keys, value_rows, other_values, query_gain, key_gain)
    core = lax.rem(lax.axis_index("seq"), CORES)
    place = jnp.stack([lax.axis_index("head"), core]).astype(jnp.int32)
    w_own, *halves = weight_blocks(head_class, place, out_weight, group_count)

    fetched = [shifted(half, by + 1) for by, half in enumerate(halves)]
    fetched = jnp.stack(hold(fetched, (back,)))
    rest = other_core(fetched)
    w_others = jnp.where(core == 0, jnp.concatenate([fetched, rest], axis=1), jnp.concatenate([rest, fetched], axis=1))

    middle = tokens // 2
    pieces = ring(back[:middle], back[middle:])
    returned = over_frames(temporal(head_class, arrived, (*pieces[2:], w_others))).reshape(tokens, TMAX * HD)
    early = project_early(pieces, w_own, w_others)
    pieces = ring(returned[:middle] + front[:middle], returned[middle:] + front[middle:])
    return project_late(pieces, w_own, w_others, early)


def solution(mesh):
    return jax.shard_map(
        body,
        mesh=mesh,
        in_specs=(
            P("seq", "head"),
            P("seq", "head"),
            P("seq", "head"),
            P(),
            P(),
            P("head"),
            P("head", None),
        ),
        out_specs=P("seq", "head"),
        check_vma=False,
    )
```

```python
import functools
import math

import jax
import jax.numpy as jnp
from jax import lax
from jax.experimental import pallas as pl
from jax.experimental.pallas import tpu as pltpu
from jax.sharding import Mesh
from jax.sharding import PartitionSpec as P

TMAX = 4
SMALL_VMEM = 16 * 1024 * 1024
CORES = 2
ROWS = 8
HD = 128
EPSILON = 1e-06
LOG2_SCALE = math.log2(math.e) / math.sqrt(HD)


def in_hbm(shape, dtype):
    return pltpu.HBM(shape, dtype)


def from_hbm(array):
    return pltpu.with_memory_space_constraint(array, pltpu.HBM)


def from_vmem(array):
    return pltpu.with_memory_space_constraint(array, pltpu.VMEM)


def temporal_count(classes, head_count):
    total = classes[0]
    for head in range(1, head_count):
        total = total + classes[head]
    return total


def head_of(classes, slot, head_count):
    temporal_seen = jnp.int32(0)
    spatial_seen = temporal_count(classes, head_count)
    found = jnp.int32(0)
    for head in range(head_count):
        kind = classes[head]
        rank = jnp.where(kind == 1, temporal_seen, spatial_seen)
        found = jnp.where(rank == slot, jnp.int32(head), found)
        temporal_seen = temporal_seen + kind
        spatial_seen = spatial_seen + 1 - kind
    return found


def scaled(widened, gain):
    mean = jnp.mean(widened * widened, axis=-1, keepdims=True)
    return widened * lax.rsqrt(mean + EPSILON) * gain


def normed(rows, gain):
    return scaled(rows.astype(jnp.float32), gain).astype(jnp.bfloat16)


def scores_of(queries, keys):
    return lax.dot_general(queries, keys, (((1,), (1,)), ((), ())), preferred_element_type=jnp.float32)


def hold_kernel(*refs):
    pass


def hold(arrays, after):
    anywhere = pl.BlockSpec(memory_space=pl.ANY)
    return pl.pallas_call(
        hold_kernel,
        in_specs=[anywhere] * (len(arrays) + len(after)),
        out_specs=[anywhere] * len(arrays),
        out_shape=[in_hbm(array.shape, array.dtype) for array in arrays],
        input_output_aliases={at: at for at in range(len(arrays))},
        cost_estimate=pl.CostEstimate(flops=0, bytes_accessed=0, transcendentals=0),
        name="hold",
    )(*[from_hbm(array) for array in (*arrays, *after)])


def pack_kernel(head_count, classes, query, key, value, query_gain, key_gain, out, raw, ready, in_sems, out_sems):
    heads = [head_of(classes, slot, head_count) for slot in range(TMAX)]
    gains = (query_gain, key_gain, None)
    frames, positions, _ = out.shape
    quarters = positions // ROWS
    tokens = frames * positions
    chunk = 8
    loads, stores = [], []
    for at in range(3 * TMAX):
        slot, which = divmod(at, 3)
        source = (query, key, value)[which].at[:, pl.ds(pl.multiple_of(heads[slot] * HD, HD), HD)]
        loads.append(pltpu.make_async_copy(source, raw.at[at], in_sems.at[at]))
        loads[-1].start()
    for at in range(3 * TMAX):
        gain = gains[at % 3]
        loads[at].wait()
        for first in range(0, frames, chunk):
            blocks = []
            for quarter in range(quarters):
                begin = quarter * (tokens // quarters) + first * ROWS
                rows = raw[at, begin : begin + chunk * ROWS].astype(jnp.float32)
                if gain is not None:
                    rows = scaled(rows, gain[...])
                blocks.append(rows.reshape(chunk, ROWS, HD))
            ready[at, first : first + chunk] = jnp.concatenate(blocks, axis=1).astype(jnp.bfloat16)
        stores.append(pltpu.make_async_copy(ready.at[at], out.at[:, :, pl.ds(at * HD, HD)], out_sems.at[at]))
        stores[-1].start()
    for store in stores:
        store.wait()


def pack(head_class, query_rows, key_rows, value_rows, query_gain, key_gain, frames):
    tokens, width = query_rows.shape
    positions = tokens // frames
    anywhere = pl.BlockSpec(memory_space=pl.ANY)
    gain_spec = pl.BlockSpec((1, HD), lambda step, classes: (0, 0))
    return pl.pallas_call(
        functools.partial(pack_kernel, width // HD),
        grid_spec=pltpu.PrefetchScalarGridSpec(
            num_scalar_prefetch=1,
            grid=(1,),
            in_specs=[anywhere] * 3 + [gain_spec] * 2,
            out_specs=anywhere,
            scratch_shapes=[
                pltpu.VMEM((3 * TMAX, tokens, HD), jnp.bfloat16),
                pltpu.VMEM((3 * TMAX, frames, positions, HD), jnp.bfloat16),
                pltpu.SemaphoreType.DMA((3 * TMAX,)),
                pltpu.SemaphoreType.DMA((3 * TMAX,)),
            ],
        ),
        out_shape=in_hbm((frames, positions, TMAX * 3 * HD), jnp.bfloat16),
        cost_estimate=pl.CostEstimate(flops=8 * tokens * TMAX * HD, bytes_accessed=12 * tokens * TMAX * HD, transcendentals=0),
        name="pack",
    )(head_class, from_hbm(query_rows), from_hbm(key_rows), from_hbm(value_rows), query_gain, key_gain)


def spatial_kernel(head_count, classes, query, key, other_key, value, other_value, query_gain, key_gain, out, keys, values):
    slot = pl.program_id(0)
    tokens = query.shape[0]
    chunk = tokens // 4

    @pl.when(slot >= temporal_count(classes, head_count))
    def _():
        keys[:tokens] = normed(key[...], key_gain[...])
        keys[tokens:] = normed(other_key[...], key_gain[...])
        values[:tokens, :HD] = value[...]
        values[tokens:, :HD] = other_value[...]
        values[:, HD:] = jnp.ones((2 * tokens, HD), jnp.bfloat16)

        def step(index, carry):
            rows = pl.ds(pl.multiple_of(index * chunk, chunk), chunk)
            queries = normed(query[rows, :], query_gain[...])
            weights = jnp.exp2(scores_of(queries, keys[...]) * LOG2_SCALE).astype(jnp.bfloat16)
            summed = jnp.dot(weights, values[...], preferred_element_type=jnp.float32)
            out[rows, :] = (summed[:, :HD] / summed[:, HD:]).astype(jnp.bfloat16)
            return carry

        lax.fori_loop(0, tokens // chunk, step, 0)

    @pl.when(slot < temporal_count(classes, head_count))
    def _():
        out[...] = jnp.zeros_like(out)


def spatial(head_class, query_rows, key_rows, other_keys, value_rows, other_values, query_gain, key_gain):
    tokens, width = query_rows.shape
    head_count = width // HD

    def rows(slot, classes):
        return 0, head_of(classes, slot, head_count)

    row_spec = pl.BlockSpec((tokens, HD), rows)
    gain_spec = pl.BlockSpec((1, HD), lambda slot, classes: (0, 0))
    return pl.pallas_call(
        functools.partial(spatial_kernel, head_count),
        grid_spec=pltpu.PrefetchScalarGridSpec(
            num_scalar_prefetch=1,
            grid=(head_count,),
            in_specs=[row_spec] * 5 + [gain_spec] * 2,
            out_specs=pl.BlockSpec((tokens, HD), lambda slot, classes: (0, slot)),
            scratch_shapes=[
                pltpu.VMEM((2 * tokens, HD), jnp.bfloat16),
                pltpu.VMEM((2 * tokens, 2 * HD), jnp.bfloat16),
            ],
        ),
        out_shape=in_hbm((tokens, width), jnp.bfloat16),
        cost_estimate=pl.CostEstimate(
            flops=16 * tokens * tokens * width, bytes_accessed=12 * tokens * width, transcendentals=2 * tokens * tokens * head_count
        ),
        name="spatial",
    )(head_class, query_rows, key_rows, from_hbm(other_keys), value_rows, from_hbm(other_values), query_gain, key_gain)


def temporal_kernel(head_count, classes, packed, *rest):
    out = rest[-1]
    slot = pl.program_id(0)
    frames, positions, _ = packed.shape
    places = 2 * ROWS
    count = frames * places

    @pl.when(slot < temporal_count(classes, head_count))
    def _():
        row = lax.broadcasted_iota(jnp.int32, (count, count), 0)
        column = lax.broadcasted_iota(jnp.int32, (count, count), 1)
        same = (row & (places - 1)) == (column & (places - 1))
        base = pl.multiple_of(slot * 3 * HD, HD)
        for part in range(positions // places):
            at = slice(part * places, (part + 1) * places)
            queries, keys, values = (packed[:, at, pl.ds(base + which * HD, HD)].reshape(count, HD) for which in range(3))
            exponents = jnp.where(same, scores_of(queries, keys) * LOG2_SCALE, -1e30)
            weights = jnp.exp2(exponents).astype(jnp.bfloat16)
            both = jnp.concatenate([values, jnp.ones_like(values)], axis=1)
            summed = jnp.dot(weights, both, preferred_element_type=jnp.float32)
            result = (summed[:, :HD] / summed[:, HD:]).reshape(frames, 2, ROWS, HD)
            out[:, 2 * part : 2 * part + 2] = result.astype(jnp.bfloat16)

    @pl.when(slot >= temporal_count(classes, head_count))
    def _():
        out[...] = jnp.zeros_like(out)


def temporal(head_class, packed, after):
    frames, positions, _ = packed.shape
    quarters = positions // ROWS
    return pl.pallas_call(
        functools.partial(temporal_kernel, head_class.shape[0]),
        grid_spec=pltpu.PrefetchScalarGridSpec(
            num_scalar_prefetch=1,
            grid=(TMAX,),
            in_specs=[pl.BlockSpec(memory_space=pltpu.VMEM)] + [pl.BlockSpec(memory_space=pl.ANY)] * len(after),
            out_specs=pl.BlockSpec((frames, quarters, ROWS, HD), lambda slot, classes: (0, 0, 0, slot)),
        ),
        out_shape=in_hbm((frames, quarters, ROWS, TMAX * HD), jnp.bfloat16),
        compiler_params=pltpu.CompilerParams(vmem_limit_bytes=SMALL_VMEM),
        cost_estimate=pl.CostEstimate(
            flops=64 * frames * frames * positions * TMAX * HD,
            bytes_accessed=8 * frames * positions * TMAX * HD,
            transcendentals=16 * frames * frames * positions * TMAX,
        ),
        name="temporal",
    )(head_class, from_vmem(packed), *[from_hbm(array) for array in after])


def weight_kernel(classes, place, weight, left, right):
    width = left.shape[1]
    left[...] = weight[:, :width]
    right[...] = weight[:, width:]


def weight_half(head_class, place, weight):
    rows, columns = weight.shape
    head_count = rows // HD
    share = head_count // CORES
    spec = pl.BlockSpec((HD, columns // 2), lambda step, classes, place: (step, 0))

    def source(step, classes, place):
        return head_of(classes, place[1] * share + step, head_count), 0

    return pl.pallas_call(
        weight_kernel,
        grid_spec=pltpu.PrefetchScalarGridSpec(
            num_scalar_prefetch=2,
            grid=(share,),
            in_specs=[pl.BlockSpec((HD, columns), source)],
            out_specs=[spec, spec],
        ),
        out_shape=[in_hbm((rows // CORES, columns // 2), jnp.bfloat16)] * 2,
        cost_estimate=pl.CostEstimate(flops=0, bytes_accessed=2 * rows * columns, transcendentals=0),
        name="weight_half",
    )(head_class, place, weight)


def combine_kernel(place, returned, *refs):
    out = refs[-1]
    group_count = out.shape[0]
    width = returned.shape[-1]
    rows = out.shape[1]
    for by in range(group_count):
        group = lax.rem(place[0] + group_count - by, group_count)
        temporal_rows = returned[:, pl.ds(group, 1)].astype(jnp.float32).reshape(rows, width)
        out[by, :, :width] = (temporal_rows + refs[by][:, :width].astype(jnp.float32)).astype(jnp.bfloat16)
        out[by, :, width:] = refs[by][:, width:]


def combine(place, returned, pieces):
    rows, width = pieces[0].shape
    whole = pl.BlockSpec(memory_space=pltpu.VMEM)
    return pl.pallas_call(
        combine_kernel,
        grid_spec=pltpu.PrefetchScalarGridSpec(
            num_scalar_prefetch=1, grid=(1,), in_specs=[whole] * (1 + len(pieces)), out_specs=whole
        ),
        out_shape=pltpu.VMEM((len(pieces), rows, width), jnp.bfloat16),
        compiler_params=pltpu.CompilerParams(vmem_limit_bytes=SMALL_VMEM),
        cost_estimate=pl.CostEstimate(flops=0, bytes_accessed=8 * len(pieces) * rows * width, transcendentals=0),
        name="combine",
    )(place, from_vmem(returned), *[from_vmem(piece) for piece in pieces])


def project_kernel(by, place, heads, *refs):
    out = refs[-1]
    group_count = heads.shape[0]
    block = lax.rem(place[0] + by, group_count)
    width = out.shape[1]
    share = refs[0].shape[0]
    columns = pl.ds(pl.multiple_of(lax.rem(block, 2) * width, HD), width)
    for side in range(2):

        @pl.when(block // 2 == side)
        def _(side=side):
            total = jnp.zeros(out.shape, jnp.float32)
            for group in range(group_count):
                for core in range(CORES):
                    weight = refs[(core * group_count + group) * 2 + side]
                    first = (place[1] if core == 0 else 1 - place[1]) * share
                    rows = heads[group, :, pl.ds(pl.multiple_of(first, HD), share)]
                    total += jnp.dot(rows, weight[:, columns], preferred_element_type=jnp.float32)
            out[...] = total.astype(out.dtype)


def project(place, heads, weights, by):
    group_count, rows, depth = heads.shape
    width = weights[0].shape[1] * 2 // group_count
    whole = pl.BlockSpec(memory_space=pltpu.VMEM)
    return pl.pallas_call(
        functools.partial(project_kernel, by),
        grid_spec=pltpu.PrefetchScalarGridSpec(
            num_scalar_prefetch=1, grid=(1,), in_specs=[whole] * (1 + len(weights)), out_specs=whole
        ),
        out_shape=jax.ShapeDtypeStruct((rows, width), jnp.bfloat16),
        compiler_params=pltpu.CompilerParams(vmem_limit_bytes=SMALL_VMEM),
        cost_estimate=pl.CostEstimate(flops=2 * group_count * rows * depth * width, bytes_accessed=2 * rows * width, transcendentals=0),
        name="project",
    )(place, heads, *[from_vmem(weight) for weight in weights])


def join_kernel(place, *refs):
    *pieces, out, sems = refs
    rows = pieces[0].shape[0]
    group_count = len(pieces)
    copies = []
    for by, piece in enumerate(pieces):
        quarter = lax.rem(place[0] + group_count - by, group_count)
        target = out.at[pl.ds(pl.multiple_of(quarter * rows, rows), rows), :]
        copies.append(pltpu.make_async_copy(piece, target, sems.at[by]))
        copies[-1].start()
    for copy in copies:
        copy.wait()


def join(place, pieces):
    rows, width = pieces[0].shape
    return pl.pallas_call(
        join_kernel,
        grid_spec=pltpu.PrefetchScalarGridSpec(
            num_scalar_prefetch=1,
            grid=(1,),
            in_specs=[pl.BlockSpec(memory_space=pltpu.VMEM)] * len(pieces),
            out_specs=pl.BlockSpec(memory_space=pl.ANY),
            scratch_shapes=[pltpu.SemaphoreType.DMA((len(pieces),))],
        ),
        out_shape=in_hbm((len(pieces) * rows, width), jnp.bfloat16),
        compiler_params=pltpu.CompilerParams(vmem_limit_bytes=SMALL_VMEM),
        cost_estimate=pl.CostEstimate(flops=0, bytes_accessed=4 * len(pieces) * rows * width, transcendentals=0),
        name="join",
    )(place, *[from_vmem(piece) for piece in pieces])


def shifted(block, by):
    count = lax.axis_size("head")
    if by == 0:
        return block
    return lax.ppermute(block, "head", [(at, (at + by) % count) for at in range(count)])


def other_core(block):
    return lax.ppermute(block, "core", [(0, 1), (1, 0)])


def body(query_rows, key_rows, value_rows, query_gain, key_gain, head_class, out_weight):
    tokens = query_rows.shape[0]
    frames = lax.axis_size("frame")
    group_count = lax.axis_size("head")
    group = lax.axis_index("head")
    place = jnp.stack([group, lax.axis_index("core")]).astype(jnp.int32)
    query_gain = query_gain.reshape(1, HD)
    key_gain = key_gain.reshape(1, HD)
    packed = pack(head_class, query_rows, key_rows, value_rows, query_gain, key_gain, frames)
    arrived = lax.all_to_all(packed, "frame", 0, 0)

    w_left, w_right = weight_half(head_class, place, out_weight)
    right_of_left, left_of_right = shifted(w_left, 1), shifted(w_right, -1)
    right_of_right, left_of_left = shifted(w_right, 1), shifted(w_left, -1)

    other_keys, other_values = other_core(key_rows), other_core(value_rows)
    near_out = spatial(head_class, query_rows, key_rows, other_keys, value_rows, other_values, query_gain, key_gain)
    right_of_left, left_of_right = hold((right_of_left, left_of_right), (near_out,))
    far_of_left, far_of_right = shifted(right_of_left, 1), shifted(left_of_right, -1)
    mine = (w_left, w_right, right_of_left, right_of_right, far_of_left, far_of_right, left_of_left, left_of_right)
    weights = (*mine, *[other_core(array) for array in mine])

    quarter = tokens // group_count
    pieces = []
    for by in range(group_count):
        first = lax.rem(group + by, group_count) * quarter
        pieces.append(shifted(lax.dynamic_slice_in_dim(near_out, first, quarter), by))

    sent = temporal(head_class, arrived, (*pieces[1:], right_of_right, left_of_left))
    sent = sent.reshape(frames * group_count, ROWS, TMAX * HD)
    returned = lax.all_to_all(sent, ("frame", "head"), 0, 0).reshape(frames, group_count, ROWS, TMAX * HD)
    heads = combine(place, returned, pieces)
    results = {by: shifted(project(place, heads, weights, by), by) for by in (2, 1, 3, 0)}
    return join(place, [results[by] for by in range(group_count)])


def solution(mesh):
    seq, head = mesh.devices.shape
    split = Mesh(mesh.devices.reshape(seq // CORES, CORES, head), ("frame", "core", "head"))
    rows = P(("frame", "core"), "head")
    return jax.shard_map(
        body,
        mesh=split,
        in_specs=(rows, rows, rows, P(), P(), P("head"), P("head", None)),
        out_specs=rows,
        check_vma=False,
    )
```

```python
import functools
import math

import jax
import jax.numpy as jnp
from jax import lax
from jax.experimental import pallas as pl
from jax.experimental.pallas import tpu as pltpu
from jax.sharding import Mesh
from jax.sharding import PartitionSpec as P

TMAX = 4
SMALL_VMEM = 16 * 1024 * 1024
CORES = 2
ROWS = 8
HD = 128
EPSILON = 1e-06
LOG2_SCALE = math.log2(math.e) / math.sqrt(HD)


def in_hbm(shape, dtype):
    return pltpu.HBM(shape, dtype)


def from_hbm(array):
    return pltpu.with_memory_space_constraint(array, pltpu.HBM)


def from_vmem(array):
    return pltpu.with_memory_space_constraint(array, pltpu.VMEM)


def temporal_count(classes, head_count):
    total = classes[0]
    for head in range(1, head_count):
        total = total + classes[head]
    return total


def head_of(classes, slot, head_count):
    temporal_seen = jnp.int32(0)
    spatial_seen = temporal_count(classes, head_count)
    found = jnp.int32(0)
    for head in range(head_count):
        kind = classes[head]
        rank = jnp.where(kind == 1, temporal_seen, spatial_seen)
        found = jnp.where(rank == slot, jnp.int32(head), found)
        temporal_seen = temporal_seen + kind
        spatial_seen = spatial_seen + 1 - kind
    return found


def scaled(widened, gain):
    mean = jnp.mean(widened * widened, axis=-1, keepdims=True)
    return widened * lax.rsqrt(mean + EPSILON) * gain


def normed(rows, gain):
    return scaled(rows.astype(jnp.float32), gain).astype(jnp.bfloat16)


def scores_of(queries, keys):
    return lax.dot_general(queries, keys, (((1,), (1,)), ((), ())), preferred_element_type=jnp.float32)


def hold_kernel(*refs):
    pass


def hold(arrays, after):
    anywhere = pl.BlockSpec(memory_space=pl.ANY)
    return pl.pallas_call(
        hold_kernel,
        in_specs=[anywhere] * (len(arrays) + len(after)),
        out_specs=[anywhere] * len(arrays),
        out_shape=[in_hbm(array.shape, array.dtype) for array in arrays],
        input_output_aliases={at: at for at in range(len(arrays))},
        cost_estimate=pl.CostEstimate(flops=0, bytes_accessed=0, transcendentals=0),
        name="hold",
    )(*[from_hbm(array) for array in (*arrays, *after)])


def pack_kernel(head_count, classes, place, query, key, value, query_gain, key_gain, weight, out, left, right, raw, ready, rows_held, in_sems, out_sems, row_in_sems, row_out_sems):
    heads = [head_of(classes, slot, head_count) for slot in range(TMAX)]
    gains = (query_gain, key_gain, None)
    frames, positions, _ = out.shape
    quarters = positions // ROWS
    tokens = frames * positions
    chunk = 8
    loads, stores = [], []
    for at in range(3 * TMAX):
        slot, which = divmod(at, 3)
        source = (query, key, value)[which].at[:, pl.ds(pl.multiple_of(heads[slot] * HD, HD), HD)]
        loads.append(pltpu.make_async_copy(source, raw.at[at], in_sems.at[at]))
        loads[-1].start()
    share = left.shape[0] // HD
    row_loads = []
    for step in range(share):
        head = head_of(classes, place[1] * share + step, head_count)
        source = weight.at[pl.ds(pl.multiple_of(head * HD, HD), HD), :]
        row_loads.append(pltpu.make_async_copy(source, rows_held.at[step], row_in_sems.at[step]))
        row_loads[-1].start()
    for at in range(3 * TMAX):
        gain = gains[at % 3]
        loads[at].wait()
        for first in range(0, frames, chunk):
            blocks = []
            for quarter in range(quarters):
                begin = quarter * (tokens // quarters) + first * ROWS
                rows = raw[at, begin : begin + chunk * ROWS].astype(jnp.float32)
                if gain is not None:
                    rows = scaled(rows, gain[...])
                blocks.append(rows.reshape(chunk, ROWS, HD))
            ready[at, first : first + chunk] = jnp.concatenate(blocks, axis=1).astype(jnp.bfloat16)
        stores.append(pltpu.make_async_copy(ready.at[at], out.at[:, :, pl.ds(at * HD, HD)], out_sems.at[at]))
        stores[-1].start()
    half = left.shape[1]
    for step in range(share):
        row_loads[step].wait()
        for side, target in enumerate((left, right)):
            source = rows_held.at[step, :, pl.ds(side * half, half)]
            target = target.at[pl.ds(step * HD, HD), :]
            stores.append(pltpu.make_async_copy(source, target, row_out_sems.at[2 * step + side]))
            stores[-1].start()
    for store in stores:
        store.wait()


def pack(head_class, place, query_rows, key_rows, value_rows, query_gain, key_gain, weight, frames):
    tokens, width = query_rows.shape
    positions = tokens // frames
    rows, columns = weight.shape
    share = rows // HD // CORES
    anywhere = pl.BlockSpec(memory_space=pl.ANY)
    gain_spec = pl.BlockSpec((1, HD), lambda step, classes, place: (0, 0))
    return pl.pallas_call(
        functools.partial(pack_kernel, width // HD),
        grid_spec=pltpu.PrefetchScalarGridSpec(
            num_scalar_prefetch=2,
            grid=(1,),
            in_specs=[anywhere] * 3 + [gain_spec] * 2 + [anywhere],
            out_specs=[anywhere] * 3,
            scratch_shapes=[
                pltpu.VMEM((3 * TMAX, tokens, HD), jnp.bfloat16),
                pltpu.VMEM((3 * TMAX, frames, positions, HD), jnp.bfloat16),
                pltpu.VMEM((share, HD, columns), jnp.bfloat16),
                pltpu.SemaphoreType.DMA((3 * TMAX,)),
                pltpu.SemaphoreType.DMA((3 * TMAX,)),
                pltpu.SemaphoreType.DMA((share,)),
                pltpu.SemaphoreType.DMA((2 * share,)),
            ],
        ),
        out_shape=[
            in_hbm((frames, positions, TMAX * 3 * HD), jnp.bfloat16),
            in_hbm((share * HD, columns // 2), jnp.bfloat16),
            in_hbm((share * HD, columns // 2), jnp.bfloat16),
        ],
        cost_estimate=pl.CostEstimate(flops=8 * tokens * TMAX * HD, bytes_accessed=12 * tokens * TMAX * HD, transcendentals=0),
        name="pack",
    )(head_class, place, from_hbm(query_rows), from_hbm(key_rows), from_hbm(value_rows), query_gain, key_gain, from_hbm(weight))


def spatial_kernel(head_count, classes, query, key, other_key, value, other_value, query_gain, key_gain, out, keys, values):
    slot = pl.program_id(0)
    tokens = query.shape[0]
    chunk = tokens // 4

    @pl.when(slot >= temporal_count(classes, head_count))
    def _():
        keys[:tokens] = normed(key[...], key_gain[...])
        keys[tokens:] = normed(other_key[...], key_gain[...])
        values[:tokens, :HD] = value[...]
        values[tokens:, :HD] = other_value[...]
        values[:, HD:] = jnp.ones((2 * tokens, HD), jnp.bfloat16)

        def step(index, carry):
            rows = pl.ds(pl.multiple_of(index * chunk, chunk), chunk)
            queries = normed(query[rows, :], query_gain[...])
            weights = jnp.exp2(scores_of(queries, keys[...]) * LOG2_SCALE).astype(jnp.bfloat16)
            summed = jnp.dot(weights, values[...], preferred_element_type=jnp.float32)
            out[rows, :] = (summed[:, :HD] / summed[:, HD:]).astype(jnp.bfloat16)
            return carry

        lax.fori_loop(0, tokens // chunk, step, 0)

    @pl.when(slot < temporal_count(classes, head_count))
    def _():
        out[...] = jnp.zeros_like(out)


def spatial(head_class, query_rows, key_rows, other_keys, value_rows, other_values, query_gain, key_gain):
    tokens, width = query_rows.shape
    head_count = width // HD

    def rows(slot, classes):
        return 0, head_of(classes, slot, head_count)

    row_spec = pl.BlockSpec((tokens, HD), rows)
    gain_spec = pl.BlockSpec((1, HD), lambda slot, classes: (0, 0))
    return pl.pallas_call(
        functools.partial(spatial_kernel, head_count),
        grid_spec=pltpu.PrefetchScalarGridSpec(
            num_scalar_prefetch=1,
            grid=(head_count,),
            in_specs=[row_spec] * 5 + [gain_spec] * 2,
            out_specs=pl.BlockSpec((tokens, HD), lambda slot, classes: (0, slot)),
            scratch_shapes=[
                pltpu.VMEM((2 * tokens, HD), jnp.bfloat16),
                pltpu.VMEM((2 * tokens, 2 * HD), jnp.bfloat16),
            ],
        ),
        out_shape=in_hbm((tokens, width), jnp.bfloat16),
        cost_estimate=pl.CostEstimate(
            flops=16 * tokens * tokens * width, bytes_accessed=12 * tokens * width, transcendentals=2 * tokens * tokens * head_count
        ),
        name="spatial",
    )(head_class, query_rows, key_rows, from_hbm(other_keys), value_rows, from_hbm(other_values), query_gain, key_gain)


def temporal_kernel(head_count, classes, packed, *rest):
    out = rest[-1]
    slot = pl.program_id(0)
    frames, positions, _ = packed.shape
    places = 2 * ROWS
    count = frames * places

    @pl.when(slot < temporal_count(classes, head_count))
    def _():
        row = lax.broadcasted_iota(jnp.int32, (count, count), 0)
        column = lax.broadcasted_iota(jnp.int32, (count, count), 1)
        same = (row & (places - 1)) == (column & (places - 1))
        base = pl.multiple_of(slot * 3 * HD, HD)
        for part in range(positions // places):
            at = slice(part * places, (part + 1) * places)
            queries, keys, values = (packed[:, at, pl.ds(base + which * HD, HD)].reshape(count, HD) for which in range(3))
            exponents = jnp.where(same, scores_of(queries, keys) * LOG2_SCALE, -1e30)
            weights = jnp.exp2(exponents).astype(jnp.bfloat16)
            both = jnp.concatenate([values, jnp.ones_like(values)], axis=1)
            summed = jnp.dot(weights, both, preferred_element_type=jnp.float32)
            result = (summed[:, :HD] / summed[:, HD:]).reshape(frames, 2, ROWS, HD)
            out[:, 2 * part : 2 * part + 2] = result.astype(jnp.bfloat16)

    @pl.when(slot >= temporal_count(classes, head_count))
    def _():
        out[...] = jnp.zeros_like(out)


def temporal(head_class, packed, after):
    frames, positions, _ = packed.shape
    quarters = positions // ROWS
    return pl.pallas_call(
        functools.partial(temporal_kernel, head_class.shape[0]),
        grid_spec=pltpu.PrefetchScalarGridSpec(
            num_scalar_prefetch=1,
            grid=(TMAX,),
            in_specs=[pl.BlockSpec(memory_space=pltpu.VMEM)] + [pl.BlockSpec(memory_space=pl.ANY)] * len(after),
            out_specs=pl.BlockSpec((frames, quarters, ROWS, HD), lambda slot, classes: (0, 0, 0, slot)),
        ),
        out_shape=in_hbm((frames, quarters, ROWS, TMAX * HD), jnp.bfloat16),
        compiler_params=pltpu.CompilerParams(vmem_limit_bytes=SMALL_VMEM),
        cost_estimate=pl.CostEstimate(
            flops=64 * frames * frames * positions * TMAX * HD,
            bytes_accessed=8 * frames * positions * TMAX * HD,
            transcendentals=16 * frames * frames * positions * TMAX,
        ),
        name="temporal",
    )(head_class, from_vmem(packed), *[from_hbm(array) for array in after])


def combine_kernel(place, returned, *refs):
    out = refs[-1]
    group_count = out.shape[0]
    width = returned.shape[-1]
    rows = out.shape[1]
    for by in range(group_count):
        group = lax.rem(place[0] + group_count - by, group_count)
        temporal_rows = returned[:, pl.ds(group, 1)].astype(jnp.float32).reshape(rows, width)
        out[by, :, :width] = (temporal_rows + refs[by][:, :width].astype(jnp.float32)).astype(jnp.bfloat16)
        out[by, :, width:] = refs[by][:, width:]


def combine(place, returned, pieces):
    rows, width = pieces[0].shape
    whole = pl.BlockSpec(memory_space=pltpu.VMEM)
    return pl.pallas_call(
        combine_kernel,
        grid_spec=pltpu.PrefetchScalarGridSpec(
            num_scalar_prefetch=1, grid=(1,), in_specs=[whole] * (1 + len(pieces)), out_specs=whole
        ),
        out_shape=pltpu.VMEM((len(pieces), rows, width), jnp.bfloat16),
        compiler_params=pltpu.CompilerParams(vmem_limit_bytes=SMALL_VMEM),
        cost_estimate=pl.CostEstimate(flops=0, bytes_accessed=8 * len(pieces) * rows * width, transcendentals=0),
        name="combine",
    )(place, from_vmem(returned), *[from_vmem(piece) for piece in pieces])


def project_kernel(by, place, heads, *refs):
    *weights, out, held, sems = refs
    group_count = heads.shape[0]
    block = lax.rem(place[0] + by, group_count)
    width = out.shape[1]
    columns = pl.ds(pl.multiple_of(lax.rem(block, 2) * width, width), width)
    share = held.shape[1]

    def load(at, side):
        return pltpu.make_async_copy(weights[2 * at + side].at[:, columns], held.at[at], sems.at[at])

    for side in range(2):

        @pl.when(block // 2 == side)
        def _(side=side):
            for at in range(CORES * group_count):
                load(at, side).start()

    total = jnp.zeros(out.shape, jnp.float32)
    for at in range(CORES * group_count):
        core, group = divmod(at, group_count)
        load(at, 0).wait()
        first = (place[1] if core == 0 else 1 - place[1]) * share
        rows = heads[group, :, pl.ds(pl.multiple_of(first, share), share)]
        total += jnp.dot(rows, held[at], preferred_element_type=jnp.float32)
    out[...] = total.astype(out.dtype)


def project(place, heads, weights, by):
    group_count, rows, depth = heads.shape
    share, width = weights[0].shape[0], weights[0].shape[1] * 2 // group_count
    whole = pl.BlockSpec(memory_space=pltpu.VMEM)
    return pl.pallas_call(
        functools.partial(project_kernel, by),
        grid_spec=pltpu.PrefetchScalarGridSpec(
            num_scalar_prefetch=1,
            grid=(1,),
            in_specs=[whole] + [pl.BlockSpec(memory_space=pl.ANY)] * len(weights),
            out_specs=whole,
            scratch_shapes=[
                pltpu.VMEM((len(weights) // 2, share, width), jnp.bfloat16),
                pltpu.SemaphoreType.DMA((len(weights) // 2,)),
            ],
        ),
        out_shape=jax.ShapeDtypeStruct((rows, width), jnp.bfloat16),
        compiler_params=pltpu.CompilerParams(vmem_limit_bytes=SMALL_VMEM),
        cost_estimate=pl.CostEstimate(
            flops=2 * group_count * rows * depth * width, bytes_accessed=2 * group_count * depth * width, transcendentals=0
        ),
        name="project",
    )(place, heads, *[from_hbm(weight) for weight in weights])


def join_kernel(place, *refs):
    *pieces, out, sems = refs
    rows = pieces[0].shape[0]
    group_count = len(pieces)
    copies = []
    for by, piece in enumerate(pieces):
        quarter = lax.rem(place[0] + group_count - by, group_count)
        target = out.at[pl.ds(pl.multiple_of(quarter * rows, rows), rows), :]
        copies.append(pltpu.make_async_copy(piece, target, sems.at[by]))
        copies[-1].start()
    for copy in copies:
        copy.wait()


def join(place, pieces):
    rows, width = pieces[0].shape
    return pl.pallas_call(
        join_kernel,
        grid_spec=pltpu.PrefetchScalarGridSpec(
            num_scalar_prefetch=1,
            grid=(1,),
            in_specs=[pl.BlockSpec(memory_space=pltpu.VMEM)] * len(pieces),
            out_specs=pl.BlockSpec(memory_space=pl.ANY),
            scratch_shapes=[pltpu.SemaphoreType.DMA((len(pieces),))],
        ),
        out_shape=in_hbm((len(pieces) * rows, width), jnp.bfloat16),
        compiler_params=pltpu.CompilerParams(vmem_limit_bytes=SMALL_VMEM),
        cost_estimate=pl.CostEstimate(flops=0, bytes_accessed=4 * len(pieces) * rows * width, transcendentals=0),
        name="join",
    )(place, *[from_vmem(piece) for piece in pieces])


def shifted(block, by):
    count = lax.axis_size("head")
    if by == 0:
        return block
    return lax.ppermute(block, "head", [(at, (at + by) % count) for at in range(count)])


def other_core(block):
    return lax.ppermute(block, "core", [(0, 1), (1, 0)])


def body(query_rows, key_rows, value_rows, query_gain, key_gain, head_class, out_weight):
    tokens = query_rows.shape[0]
    frames = lax.axis_size("frame")
    group_count = lax.axis_size("head")
    group = lax.axis_index("head")
    place = jnp.stack([group, lax.axis_index("core")]).astype(jnp.int32)
    query_gain = query_gain.reshape(1, HD)
    key_gain = key_gain.reshape(1, HD)
    packed, w_left, w_right = pack(head_class, place, query_rows, key_rows, value_rows, query_gain, key_gain, out_weight, frames)
    arrived = lax.all_to_all(packed, "frame", 0, 0)

    right_of_left, left_of_right = shifted(w_left, 1), shifted(w_right, -1)
    right_of_right, left_of_left = shifted(w_right, 1), shifted(w_left, -1)

    other_keys, other_values = other_core(key_rows), other_core(value_rows)
    near_out = spatial(head_class, query_rows, key_rows, other_keys, value_rows, other_values, query_gain, key_gain)
    right_of_left, left_of_right = hold((right_of_left, left_of_right), (near_out,))
    far_of_left, far_of_right = shifted(right_of_left, 1), shifted(left_of_right, -1)
    mine = (w_left, w_right, right_of_left, right_of_right, far_of_left, far_of_right, left_of_left, left_of_right)
    weights = (*mine, *[other_core(array) for array in mine])

    quarter = tokens // group_count
    pieces = []
    for by in range(group_count):
        first = lax.rem(group + by, group_count) * quarter
        pieces.append(shifted(lax.dynamic_slice_in_dim(near_out, first, quarter), by))

    sent = temporal(head_class, arrived, (near_out, right_of_right, left_of_left, far_of_left, far_of_right))
    sent = sent.reshape(frames * group_count, ROWS, TMAX * HD)
    returned = lax.all_to_all(sent, ("frame", "head"), 0, 0).reshape(frames, group_count, ROWS, TMAX * HD)
    heads = combine(place, returned, pieces)
    results = {by: shifted(project(place, heads, weights, by), by) for by in (2, 1, 3, 0)}
    return join(place, [results[by] for by in range(group_count)])


def solution(mesh):
    seq, head = mesh.devices.shape
    split = Mesh(mesh.devices.reshape(seq // CORES, CORES, head), ("frame", "core", "head"))
    rows = P(("frame", "core"), "head")
    return jax.shard_map(
        body,
        mesh=split,
        in_specs=(rows, rows, rows, P(), P(), P("head"), P("head", None)),
        out_specs=rows,
        check_vma=False,
    )
```

```python
import functools
import math

import jax
import jax.numpy as jnp
from jax import lax
from jax.experimental import pallas as pl
from jax.experimental.pallas import tpu as pltpu
from jax.sharding import PartitionSpec as P

FRAMES = 32
TMAX = 4
ORDER_WEIGHT = 20
SMALL_VMEM = 16 * 1024 * 1024
CORES = 2
HD = 128
EPSILON = 1e-06
LOG2_SCALE = math.log2(math.e) / math.sqrt(HD)


def in_hbm(shape, dtype):
    return pltpu.HBM(shape, dtype)


def from_hbm(array):
    return pltpu.with_memory_space_constraint(array, pltpu.HBM)


def from_vmem(array):
    return pltpu.with_memory_space_constraint(array, pltpu.VMEM)


def temporal_count(classes, head_count):
    total = classes[0]
    for head in range(1, head_count):
        total = total + classes[head]
    return total


def head_of(classes, slot, head_count):
    temporal_seen = jnp.int32(0)
    spatial_seen = temporal_count(classes, head_count)
    found = jnp.int32(0)
    for head in range(head_count):
        kind = classes[head]
        rank = jnp.where(kind == 1, temporal_seen, spatial_seen)
        found = jnp.where(rank == slot, jnp.int32(head), found)
        temporal_seen = temporal_seen + kind
        spatial_seen = spatial_seen + 1 - kind
    return found


def normed(rows, gain):
    widened = rows.astype(jnp.float32)
    mean = jnp.mean(widened * widened, axis=-1, keepdims=True)
    return (widened * lax.rsqrt(mean + EPSILON) * gain).astype(jnp.bfloat16)


def scores_of(queries, keys):
    return lax.dot_general(queries, keys, (((1,), (1,)), ((), ())), preferred_element_type=jnp.float32)


def hold_kernel(*refs):
    pass


def hold(arrays, after):
    anywhere = pl.BlockSpec(memory_space=pl.ANY)
    return pl.pallas_call(
        hold_kernel,
        in_specs=[anywhere] * (len(arrays) + len(after)),
        out_specs=[anywhere] * len(arrays),
        out_shape=[in_hbm(array.shape, array.dtype) for array in arrays],
        input_output_aliases={at: at for at in range(len(arrays))},
        cost_estimate=pl.CostEstimate(flops=0, bytes_accessed=0, transcendentals=0),
        name="hold",
    )(*[from_hbm(array) for array in arrays], *after)


def pack_kernel(head_count, classes, query, key, value, query_gain, key_gain, out, raw, ready, in_sems, out_sems):
    heads = [head_of(classes, slot, head_count) for slot in range(TMAX)]
    gains = (query_gain, key_gain, None)
    loads, stores = [], []
    for at in range(3 * TMAX):
        slot, which = divmod(at, 3)
        source = (query, key, value)[which].at[:, pl.ds(pl.multiple_of(heads[slot] * HD, HD), HD)]
        landing = raw if gains[which] is not None else ready
        loads.append(pltpu.make_async_copy(source, landing.at[at], in_sems.at[at]))
        loads[-1].start()
    for at in range(3 * TMAX):
        gain = gains[at % 3]
        loads[at].wait()
        if gain is not None:
            ready[at] = normed(raw[at], gain[...])
        stores.append(pltpu.make_async_copy(ready.at[at], out.at[:, pl.ds(at * HD, HD)], out_sems.at[at]))
        stores[-1].start()
    for store in stores:
        store.wait()


def pack(head_class, query_rows, key_rows, value_rows, query_gain, key_gain):
    tokens, width = query_rows.shape
    anywhere = pl.BlockSpec(memory_space=pl.ANY)
    gain_spec = pl.BlockSpec((1, HD), lambda step, classes: (0, 0))
    return pl.pallas_call(
        functools.partial(pack_kernel, width // HD),
        grid_spec=pltpu.PrefetchScalarGridSpec(
            num_scalar_prefetch=1,
            grid=(1,),
            in_specs=[anywhere] * 3 + [gain_spec] * 2,
            out_specs=anywhere,
            scratch_shapes=[
                pltpu.VMEM((3 * TMAX, tokens, HD), jnp.bfloat16),
                pltpu.VMEM((3 * TMAX, tokens, HD), jnp.bfloat16),
                pltpu.SemaphoreType.DMA((3 * TMAX,)),
                pltpu.SemaphoreType.DMA((3 * TMAX,)),
            ],
        ),
        out_shape=in_hbm((tokens, TMAX * 3 * HD), jnp.bfloat16),
        cost_estimate=pl.CostEstimate(flops=8 * tokens * TMAX * HD, bytes_accessed=12 * tokens * TMAX * HD, transcendentals=0),
        name="pack",
    )(head_class, from_hbm(query_rows), from_hbm(key_rows), from_hbm(value_rows), query_gain, key_gain)


def spatial_kernel(head_count, classes, query, key, other_key, value, other_value, query_gain, key_gain, front, back, keys, values):
    slot = pl.program_id(0)
    tokens = query.shape[0]
    chunk = tokens // 4
    is_front = slot < TMAX

    @pl.when(slot >= temporal_count(classes, head_count))
    def _():
        keys[:tokens] = normed(key[...], key_gain[...])
        keys[tokens:] = normed(other_key[...], key_gain[...])
        values[:tokens, :HD] = value[...]
        values[tokens:, :HD] = other_value[...]
        values[:, HD:] = jnp.ones((2 * tokens, HD), jnp.bfloat16)

        def step(index, carry):
            rows = pl.ds(pl.multiple_of(index * chunk, chunk), chunk)
            queries = normed(query[rows, :], query_gain[...])
            weights = jnp.exp2(scores_of(queries, keys[...]) * LOG2_SCALE).astype(jnp.bfloat16)
            summed = jnp.dot(weights, values[...], preferred_element_type=jnp.float32)
            result = (summed[:, :HD] / summed[:, HD:]).astype(jnp.bfloat16)

            @pl.when(is_front)
            def _():
                front[rows, :] = result

            @pl.when(jnp.logical_not(is_front))
            def _():
                back[rows, :] = result

            return carry

        lax.fori_loop(0, tokens // chunk, step, 0)

    @pl.when(slot < temporal_count(classes, head_count))
    def _():
        front[...] = jnp.zeros_like(front)


def spatial(head_class, query_rows, key_rows, other_keys, value_rows, other_values, query_gain, key_gain):
    tokens, width = query_rows.shape
    head_count = width // HD

    def rows(slot, classes):
        return 0, head_of(classes, slot, head_count)

    row_spec = pl.BlockSpec((tokens, HD), rows)
    gain_spec = pl.BlockSpec((1, HD), lambda slot, classes: (0, 0))
    return pl.pallas_call(
        functools.partial(spatial_kernel, head_count),
        grid_spec=pltpu.PrefetchScalarGridSpec(
            num_scalar_prefetch=1,
            grid=(head_count,),
            in_specs=[row_spec] * 5 + [gain_spec] * 2,
            out_specs=[
                pl.BlockSpec((tokens, HD), lambda slot, classes: (0, jnp.minimum(slot, TMAX - 1))),
                pl.BlockSpec((tokens, HD), lambda slot, classes: (0, jnp.maximum(slot - TMAX, 0))),
            ],
            scratch_shapes=[
                pltpu.VMEM((2 * tokens, HD), jnp.bfloat16),
                pltpu.VMEM((2 * tokens, 2 * HD), jnp.bfloat16),
            ],
        ),
        out_shape=[
            in_hbm((tokens, TMAX * HD), jnp.bfloat16),
            in_hbm((tokens, width - TMAX * HD), jnp.bfloat16),
        ],
        cost_estimate=pl.CostEstimate(
            flops=16 * tokens * tokens * width, bytes_accessed=12 * tokens * width, transcendentals=2 * tokens * tokens * head_count
        ),
        name="spatial",
    )(head_class, query_rows, key_rows, from_hbm(other_keys), value_rows, from_hbm(other_values), query_gain, key_gain)


def temporal_kernel(head_count, begin, classes, packed, *rest):
    out = rest[-1]
    slot = begin + pl.program_id(0)
    frames, positions, _ = packed.shape
    places = 16
    count = frames * places

    @pl.when(slot < temporal_count(classes, head_count))
    def _():
        row = lax.broadcasted_iota(jnp.int32, (count, count), 0)
        column = lax.broadcasted_iota(jnp.int32, (count, count), 1)
        same = (row & (places - 1)) == (column & (places - 1))
        base = pl.multiple_of(slot * 3 * HD, HD)
        for part in range(positions // places):
            at = slice(part * places, (part + 1) * places)
            queries, keys, values = (packed[:, at, pl.ds(base + which * HD, HD)].reshape(count, HD) for which in range(3))
            scaled = jnp.where(same, scores_of(queries, keys) * LOG2_SCALE, -1e30)
            weights = jnp.exp2(scaled).astype(jnp.bfloat16)
            both = jnp.concatenate([values, jnp.ones_like(values)], axis=1)
            summed = jnp.dot(weights, both, preferred_element_type=jnp.float32)
            out[:, at, :] = (summed[:, :HD] / summed[:, HD:]).astype(jnp.bfloat16).reshape(frames, places, HD)

    @pl.when(slot >= temporal_count(classes, head_count))
    def _():
        out[...] = jnp.zeros_like(out)


def temporal(head_class, packed, begin, slots, after):
    frames, positions, _ = packed.shape
    return pl.pallas_call(
        functools.partial(temporal_kernel, head_class.shape[0], begin),
        grid_spec=pltpu.PrefetchScalarGridSpec(
            num_scalar_prefetch=1,
            grid=(slots,),
            in_specs=[pl.BlockSpec(memory_space=pltpu.VMEM)] + [pl.BlockSpec(memory_space=pl.ANY)] * len(after),
            out_specs=pl.BlockSpec((frames, positions, HD), lambda slot, classes: (0, 0, slot)),
        ),
        out_shape=in_hbm((frames, positions, slots * HD), jnp.bfloat16),
        compiler_params=pltpu.CompilerParams(vmem_limit_bytes=SMALL_VMEM),
        cost_estimate=pl.CostEstimate(
            flops=64 * frames * frames * positions * slots * HD,
            bytes_accessed=8 * frames * positions * slots * HD,
            transcendentals=16 * frames * frames * positions * slots,
        ),
        name="temporal",
    )(head_class, from_vmem(packed), *[from_hbm(array) for array in after])


def weight_kernel(classes, place, weight, own, *others):
    width = own.shape[1]
    group_count = len(others) + 1

    def columns(shift):
        block = lax.rem(place[0] + shift, group_count)
        return weight[:, pl.ds(pl.multiple_of(block * width, width), width)]

    own[...] = columns(0)

    @pl.when(pl.program_id(0) // (pl.num_programs(0) // CORES) == place[1])
    def _():
        for shift, other in enumerate(others):
            other[...] = columns(shift + 1)


def weight_blocks(head_class, place, weight, group_count):
    rows, columns = weight.shape
    head_count = rows // HD
    share = head_count // CORES
    width = columns // group_count

    def half_rows(slot, classes, place):
        return jnp.clip(slot - place[1] * share, 0, share - 1), 0

    return pl.pallas_call(
        weight_kernel,
        grid_spec=pltpu.PrefetchScalarGridSpec(
            num_scalar_prefetch=2,
            grid=(head_count,),
            in_specs=[pl.BlockSpec((HD, columns), lambda slot, classes, place: (head_of(classes, slot, head_count), 0))],
            out_specs=[pl.BlockSpec((HD, width), lambda slot, classes, place: (slot, 0))]
            + [pl.BlockSpec((HD, width), half_rows)] * (group_count - 1),
        ),
        out_shape=[in_hbm((rows, width), jnp.bfloat16)] + [in_hbm((rows // CORES, width), jnp.bfloat16)] * (group_count - 1),
        cost_estimate=pl.CostEstimate(flops=0, bytes_accessed=4 * rows * columns, transcendentals=0),
        name="weight_blocks",
    )(head_class, place, weight)


def product(rows, weight, first):
    return jnp.dot(rows, weight[first : first + rows.shape[1]], preferred_element_type=jnp.float32)


def near_sum(own, right, left, w_own, w_others, first):
    return product(own[...], w_own, first) + product(right[...], w_others.at[0], first) + product(left[...], w_others.at[2], first)


def all_kernel(first, own_top, own_bottom, right_top, right_bottom, left_top, left_bottom, far_top, far_bottom, w_own, w_others, *rest):
    out = rest[-1]
    half = own_top.shape[0]
    parts = ((own_top, right_top, left_top, far_top), (own_bottom, right_bottom, left_bottom, far_bottom))
    for part, (own, right, left, far) in enumerate(parts):
        rows = slice(part * half, (part + 1) * half)
        total = near_sum(own, right, left, w_own, w_others, first) + product(far[...], w_others.at[1], first)
        out[rows] = total if len(rest) == 1 else total + rest[0][rows]


def near_kernel(first, own_top, own_bottom, right_top, right_bottom, left_top, left_bottom, w_own, w_others, total, out):
    half = own_top.shape[0]
    for part, (own, right, left) in enumerate(((own_top, right_top, left_top), (own_bottom, right_bottom, left_bottom))):
        rows = slice(part * half, (part + 1) * half)
        out[rows] = total[rows] + near_sum(own, right, left, w_own, w_others, first)


def far_kernel(first, far_top, far_bottom, w_others, total, out):
    for part, far in enumerate((far_top, far_bottom)):

        @pl.when(pl.program_id(0) == part)
        def _(far=far):
            out[...] = (product(far[...], w_others.at[1], first) + total[...]).astype(out.dtype)


def summing(kernel, name, operands, depth_terms):
    tokens, width = 2 * operands[0].shape[0], operands[-1].shape[-1]
    depth = operands[0].shape[1]
    whole = pl.BlockSpec(memory_space=pltpu.VMEM)
    return pl.pallas_call(
        kernel,
        in_specs=[whole] * len(operands),
        out_specs=whole,
        out_shape=pltpu.VMEM((tokens, width), jnp.float32),
        compiler_params=pltpu.CompilerParams(vmem_limit_bytes=SMALL_VMEM),
        cost_estimate=pl.CostEstimate(
            flops=ORDER_WEIGHT * depth_terms * tokens * depth * width, bytes_accessed=8 * tokens * width, transcendentals=0
        ),
        name=name,
    )(*[from_vmem(array) for array in operands])


def project_all(name, first, pieces, w_own, w_others, *total):
    return summing(functools.partial(all_kernel, first), name, (*pieces, w_own, w_others, *total), 4)


def project_last(first, pieces, w_own, w_others, total):
    near = summing(functools.partial(near_kernel, first), "near", (*pieces[:6], w_own, w_others, total), 3)
    tokens, width = near.shape
    half, depth = pieces[0].shape
    whole = pl.BlockSpec(memory_space=pltpu.VMEM)
    sum_spec = pl.BlockSpec((half, width), lambda step: (step, 0))
    return pl.pallas_call(
        functools.partial(far_kernel, first),
        grid=(2,),
        in_specs=[whole] * 3 + [sum_spec],
        out_specs=sum_spec,
        out_shape=in_hbm((tokens, width), jnp.bfloat16),
        compiler_params=pltpu.CompilerParams(vmem_limit_bytes=SMALL_VMEM),
        cost_estimate=pl.CostEstimate(flops=2 * tokens * depth * width, bytes_accessed=8 * tokens * width, transcendentals=0),
        name="far",
    )(*[from_vmem(array) for array in (*pieces[6:], w_others, near)])


def shifted(block, by):
    count = lax.axis_size("head")
    return lax.ppermute(block, "head", [(at, (at + by) % count) for at in range(count)])


def ring(top, bottom):
    right_top, left_bottom = shifted(top, 1), shifted(bottom, -1)
    right_bottom, left_top = shifted(bottom, 1), shifted(top, -1)
    far_top, far_bottom = shifted(right_top, 1), shifted(left_bottom, -1)
    return top, bottom, right_top, right_bottom, left_top, left_bottom, far_top, far_bottom


def other_core(block):
    count = lax.axis_size("seq")
    return lax.ppermute(block, "seq", [(at, at ^ 1) for at in range(count)])


def over_frames(blocks):
    count = lax.axis_size("seq")
    groups = [list(range(core, count, CORES)) for core in range(CORES)]
    return lax.all_to_all(blocks, "seq", 0, 0, axis_index_groups=groups)


def body(query_rows, key_rows, value_rows, query_gain, key_gain, head_class, out_weight):
    tokens = query_rows.shape[0]
    group_count = lax.axis_size("head")
    query_gain = query_gain.reshape(1, HD)
    key_gain = key_gain.reshape(1, HD)
    packed = pack(head_class, query_rows, key_rows, value_rows, query_gain, key_gain)
    arrived = over_frames(packed.reshape(FRAMES, tokens // FRAMES, TMAX * 3 * HD))

    other_keys, other_values = other_core(key_rows), other_core(value_rows)
    front, back = spatial(head_class, query_rows, key_rows, other_keys, value_rows, other_values, query_gain, key_gain)
    core = lax.rem(lax.axis_index("seq"), CORES)
    place = jnp.stack([lax.axis_index("head"), core]).astype(jnp.int32)
    w_own, *halves = weight_blocks(head_class, place, out_weight, group_count)

    fetched = [shifted(half, by + 1) for by, half in enumerate(halves)]
    fetched = jnp.stack(hold(fetched, (back,)))
    rest = other_core(fetched)
    w_others = jnp.where(core == 0, jnp.concatenate([fetched, rest], axis=1), jnp.concatenate([rest, fetched], axis=1))

    middle = tokens // 2
    early = ring(back[:middle], back[middle:])
    half = TMAX // 2
    width = half * HD
    sent = [temporal(head_class, arrived, part * half, half, (*early[2:], w_others)) for part in range(2)]

    returned = over_frames(sent[0]).reshape(tokens, width)
    (front,) = hold((front,), (sent[1],))
    first = ring(returned[:middle] + front[:middle, :width], returned[middle:] + front[middle:, :width])
    (later,) = hold((sent[1],), first[:2])
    returned = over_frames(later).reshape(tokens, width)
    total = project_all("early", TMAX * HD, early, w_own, w_others)
    (rest,) = hold((front,), (*first[2:], total))
    last = ring(returned[:middle] + rest[:middle, width:], returned[middle:] + rest[middle:, width:])

    total = project_all("first", 0, first, w_own, w_others, total)
    return project_last(width, last, w_own, w_others, total)


def solution(mesh):
    return jax.shard_map(
        body,
        mesh=mesh,
        in_specs=(
            P("seq", "head"),
            P("seq", "head"),
            P("seq", "head"),
            P(),
            P(),
            P("head"),
            P("head", None),
        ),
        out_specs=P("seq", "head"),
        check_vma=False,
    )
```

```python
import functools
import math

import jax
import jax.numpy as jnp
from jax import lax
from jax.experimental import pallas as pl
from jax.experimental.pallas import tpu as pltpu
from jax.sharding import PartitionSpec as P

FRAMES = 32
TMAX = 4
ORDER_WEIGHT = 20
SMALL_VMEM = 16 * 1024 * 1024
CORES = 2
HD = 128
EPSILON = 1e-06
LOG2_SCALE = math.log2(math.e) / math.sqrt(HD)


def in_hbm(shape, dtype):
    return pltpu.HBM(shape, dtype)


def from_hbm(array):
    return pltpu.with_memory_space_constraint(array, pltpu.HBM)


def from_vmem(array):
    return pltpu.with_memory_space_constraint(array, pltpu.VMEM)


def temporal_count(classes, head_count):
    total = classes[0]
    for head in range(1, head_count):
        total = total + classes[head]
    return total


def head_of(classes, slot, head_count):
    temporal_seen = jnp.int32(0)
    spatial_seen = temporal_count(classes, head_count)
    found = jnp.int32(0)
    for head in range(head_count):
        kind = classes[head]
        rank = jnp.where(kind == 1, temporal_seen, spatial_seen)
        found = jnp.where(rank == slot, jnp.int32(head), found)
        temporal_seen = temporal_seen + kind
        spatial_seen = spatial_seen + 1 - kind
    return found


def normed(rows, gain):
    widened = rows.astype(jnp.float32)
    mean = jnp.mean(widened * widened, axis=-1, keepdims=True)
    return (widened * lax.rsqrt(mean + EPSILON) * gain).astype(jnp.bfloat16)


def scores_of(queries, keys):
    return lax.dot_general(queries, keys, (((1,), (1,)), ((), ())), preferred_element_type=jnp.float32)


def hold_kernel(*refs):
    pass


def hold(arrays, after):
    anywhere = pl.BlockSpec(memory_space=pl.ANY)
    return pl.pallas_call(
        hold_kernel,
        in_specs=[anywhere] * (len(arrays) + len(after)),
        out_specs=[anywhere] * len(arrays),
        out_shape=[in_hbm(array.shape, array.dtype) for array in arrays],
        input_output_aliases={at: at for at in range(len(arrays))},
        cost_estimate=pl.CostEstimate(flops=0, bytes_accessed=0, transcendentals=0),
        name="hold",
    )(*[from_hbm(array) for array in arrays], *after)


def pack_kernel(head_count, classes, query, key, value, query_gain, key_gain, out, raw, ready, in_sems, out_sems):
    heads = [head_of(classes, slot, head_count) for slot in range(TMAX)]
    gains = (query_gain, key_gain, None)
    loads, stores = [], []
    for at in range(3 * TMAX):
        slot, which = divmod(at, 3)
        source = (query, key, value)[which].at[:, pl.ds(pl.multiple_of(heads[slot] * HD, HD), HD)]
        landing = raw if gains[which] is not None else ready
        loads.append(pltpu.make_async_copy(source, landing.at[at], in_sems.at[at]))
        loads[-1].start()
    for at in range(3 * TMAX):
        gain = gains[at % 3]
        loads[at].wait()
        if gain is not None:
            ready[at] = normed(raw[at], gain[...])
        stores.append(pltpu.make_async_copy(ready.at[at], out.at[:, pl.ds(at * HD, HD)], out_sems.at[at]))
        stores[-1].start()
    for store in stores:
        store.wait()


def pack(head_class, query_rows, key_rows, value_rows, query_gain, key_gain):
    tokens, width = query_rows.shape
    anywhere = pl.BlockSpec(memory_space=pl.ANY)
    gain_spec = pl.BlockSpec((1, HD), lambda step, classes: (0, 0))
    return pl.pallas_call(
        functools.partial(pack_kernel, width // HD),
        grid_spec=pltpu.PrefetchScalarGridSpec(
            num_scalar_prefetch=1,
            grid=(1,),
            in_specs=[anywhere] * 3 + [gain_spec] * 2,
            out_specs=anywhere,
            scratch_shapes=[
                pltpu.VMEM((3 * TMAX, tokens, HD), jnp.bfloat16),
                pltpu.VMEM((3 * TMAX, tokens, HD), jnp.bfloat16),
                pltpu.SemaphoreType.DMA((3 * TMAX,)),
                pltpu.SemaphoreType.DMA((3 * TMAX,)),
            ],
        ),
        out_shape=in_hbm((tokens, TMAX * 3 * HD), jnp.bfloat16),
        cost_estimate=pl.CostEstimate(flops=8 * tokens * TMAX * HD, bytes_accessed=12 * tokens * TMAX * HD, transcendentals=0),
        name="pack",
    )(head_class, from_hbm(query_rows), from_hbm(key_rows), from_hbm(value_rows), query_gain, key_gain)


def spatial_kernel(head_count, classes, query, key, other_key, value, other_value, query_gain, key_gain, out, keys, values):
    slot = pl.program_id(0)
    tokens = query.shape[0]
    chunk = tokens // 4

    @pl.when(slot >= temporal_count(classes, head_count))
    def _():
        keys[:tokens] = normed(key[...], key_gain[...])
        keys[tokens:] = normed(other_key[...], key_gain[...])
        values[:tokens, :HD] = value[...]
        values[tokens:, :HD] = other_value[...]
        values[:, HD:] = jnp.ones((2 * tokens, HD), jnp.bfloat16)

        def step(index, carry):
            rows = pl.ds(pl.multiple_of(index * chunk, chunk), chunk)
            queries = normed(query[rows, :], query_gain[...])
            weights = jnp.exp2(scores_of(queries, keys[...]) * LOG2_SCALE).astype(jnp.bfloat16)
            summed = jnp.dot(weights, values[...], preferred_element_type=jnp.float32)
            out[rows, :] = (summed[:, :HD] / summed[:, HD:]).astype(jnp.bfloat16)
            return carry

        lax.fori_loop(0, tokens // chunk, step, 0)

    @pl.when(slot < temporal_count(classes, head_count))
    def _():
        out[...] = jnp.zeros_like(out)


def spatial(head_class, query_rows, key_rows, other_keys, value_rows, other_values, query_gain, key_gain):
    tokens, width = query_rows.shape
    head_count = width // HD

    def rows(slot, classes):
        return 0, head_of(classes, slot, head_count)

    row_spec = pl.BlockSpec((tokens, HD), rows)
    gain_spec = pl.BlockSpec((1, HD), lambda slot, classes: (0, 0))
    return pl.pallas_call(
        functools.partial(spatial_kernel, head_count),
        grid_spec=pltpu.PrefetchScalarGridSpec(
            num_scalar_prefetch=1,
            grid=(head_count,),
            in_specs=[row_spec] * 5 + [gain_spec] * 2,
            out_specs=pl.BlockSpec((tokens, HD), lambda slot, classes: (0, slot)),
            scratch_shapes=[
                pltpu.VMEM((2 * tokens, HD), jnp.bfloat16),
                pltpu.VMEM((2 * tokens, 2 * HD), jnp.bfloat16),
            ],
        ),
        out_shape=in_hbm((tokens, width), jnp.bfloat16),
        cost_estimate=pl.CostEstimate(
            flops=16 * tokens * tokens * width, bytes_accessed=12 * tokens * width, transcendentals=2 * tokens * tokens * head_count
        ),
        name="spatial",
    )(head_class, query_rows, key_rows, from_hbm(other_keys), value_rows, from_hbm(other_values), query_gain, key_gain)


def temporal_kernel(head_count, begin, classes, packed, *rest):
    out = rest[-1]
    slot = begin + pl.program_id(0)
    frames, positions, _ = packed.shape
    places = 16
    count = frames * places

    @pl.when(slot < temporal_count(classes, head_count))
    def _():
        row = lax.broadcasted_iota(jnp.int32, (count, count), 0)
        column = lax.broadcasted_iota(jnp.int32, (count, count), 1)
        same = (row & (places - 1)) == (column & (places - 1))
        base = pl.multiple_of(slot * 3 * HD, HD)
        for part in range(positions // places):
            at = slice(part * places, (part + 1) * places)
            queries, keys, values = (packed[:, at, pl.ds(base + which * HD, HD)].reshape(count, HD) for which in range(3))
            scaled = jnp.where(same, scores_of(queries, keys) * LOG2_SCALE, -1e30)
            weights = jnp.exp2(scaled).astype(jnp.bfloat16)
            both = jnp.concatenate([values, jnp.ones_like(values)], axis=1)
            summed = jnp.dot(weights, both, preferred_element_type=jnp.float32)
            out[:, at, :] = (summed[:, :HD] / summed[:, HD:]).astype(jnp.bfloat16).reshape(frames, places, HD)

    @pl.when(slot >= temporal_count(classes, head_count))
    def _():
        out[...] = jnp.zeros_like(out)


def temporal(head_class, packed, begin, slots, after):
    frames, positions, _ = packed.shape
    return pl.pallas_call(
        functools.partial(temporal_kernel, head_class.shape[0], begin),
        grid_spec=pltpu.PrefetchScalarGridSpec(
            num_scalar_prefetch=1,
            grid=(slots,),
            in_specs=[pl.BlockSpec(memory_space=pltpu.VMEM)] + [pl.BlockSpec(memory_space=pl.ANY)] * len(after),
            out_specs=pl.BlockSpec((frames, positions, HD), lambda slot, classes: (0, 0, slot)),
        ),
        out_shape=in_hbm((frames, positions, slots * HD), jnp.bfloat16),
        compiler_params=pltpu.CompilerParams(vmem_limit_bytes=SMALL_VMEM),
        cost_estimate=pl.CostEstimate(
            flops=64 * frames * frames * positions * slots * HD,
            bytes_accessed=8 * frames * positions * slots * HD,
            transcendentals=16 * frames * frames * positions * slots,
        ),
        name="temporal",
    )(head_class, from_vmem(packed), *[from_hbm(array) for array in after])


def weight_kernel(classes, place, weight, own, *others):
    width = own.shape[1]
    group_count = len(others) + 1

    def columns(shift):
        block = lax.rem(place[0] + shift, group_count)
        return weight[:, pl.ds(pl.multiple_of(block * width, width), width)]

    own[...] = columns(0)

    @pl.when(pl.program_id(0) // (pl.num_programs(0) // CORES) == place[1])
    def _():
        for shift, other in enumerate(others):
            other[...] = columns(shift + 1)


def weight_blocks(head_class, place, weight, group_count):
    rows, columns = weight.shape
    head_count = rows // HD
    share = head_count // CORES
    width = columns // group_count

    def half_rows(slot, classes, place):
        return jnp.clip(slot - place[1] * share, 0, share - 1), 0

    return pl.pallas_call(
        weight_kernel,
        grid_spec=pltpu.PrefetchScalarGridSpec(
            num_scalar_prefetch=2,
            grid=(head_count,),
            in_specs=[pl.BlockSpec((HD, columns), lambda slot, classes, place: (head_of(classes, slot, head_count), 0))],
            out_specs=[pl.BlockSpec((HD, width), lambda slot, classes, place: (slot, 0))]
            + [pl.BlockSpec((HD, width), half_rows)] * (group_count - 1),
        ),
        out_shape=[in_hbm((rows, width), jnp.bfloat16)] + [in_hbm((rows // CORES, width), jnp.bfloat16)] * (group_count - 1),
        cost_estimate=pl.CostEstimate(flops=0, bytes_accessed=4 * rows * columns, transcendentals=0),
        name="weight_blocks",
    )(head_class, place, weight)


def product(rows, weight, first):
    return jnp.dot(rows, weight[first : first + rows.shape[1]], preferred_element_type=jnp.float32)


def near_sum(own, right, left, w_own, w_others, first, rows):
    total = product(own[rows], w_own, first)
    return total + product(right[rows], w_others.at[0], first) + product(left[rows], w_others.at[2], first)


def halves(tokens):
    return slice(0, tokens // 2), slice(tokens // 2, tokens)


def all_kernel(first, own, right, left, far_top, far_bottom, w_own, w_others, *rest):
    out = rest[-1]
    for rows, far in zip(halves(own.shape[0]), (far_top, far_bottom), strict=True):
        total = near_sum(own, right, left, w_own, w_others, first, rows) + product(far[...], w_others.at[1], first)
        out[rows] = total if len(rest) == 1 else total + rest[0][rows]


def near_kernel(first, own, right, left, w_own, w_others, total, out):
    for rows in halves(own.shape[0]):
        out[rows] = total[rows] + near_sum(own, right, left, w_own, w_others, first, rows)


def far_kernel(first, far_top, far_bottom, w_others, total, out):
    for part, far in enumerate((far_top, far_bottom)):

        @pl.when(pl.program_id(0) == part)
        def _(far=far):
            out[...] = (product(far[...], w_others.at[1], first) + total[...]).astype(out.dtype)


def summing(kernel, name, operands, depth_terms):
    tokens, width = operands[0].shape[0], operands[-1].shape[-1]
    depth = operands[0].shape[1]
    whole = pl.BlockSpec(memory_space=pltpu.VMEM)
    return pl.pallas_call(
        kernel,
        in_specs=[whole] * len(operands),
        out_specs=whole,
        out_shape=pltpu.VMEM((tokens, width), jnp.float32),
        compiler_params=pltpu.CompilerParams(vmem_limit_bytes=SMALL_VMEM),
        cost_estimate=pl.CostEstimate(
            flops=ORDER_WEIGHT * depth_terms * tokens * depth * width, bytes_accessed=8 * tokens * width, transcendentals=0
        ),
        name=name,
    )(*[from_vmem(array) for array in operands])


def project_all(name, first, pieces, w_own, w_others, *total):
    return summing(functools.partial(all_kernel, first), name, (*pieces, w_own, w_others, *total), 4)


def project_last(first, pieces, w_own, w_others, total):
    near = summing(functools.partial(near_kernel, first), "near", (*pieces[:3], w_own, w_others, total), 3)
    tokens, width = near.shape
    half, depth = pieces[3].shape
    whole = pl.BlockSpec(memory_space=pltpu.VMEM)
    sum_spec = pl.BlockSpec((half, width), lambda step: (step, 0))
    return pl.pallas_call(
        functools.partial(far_kernel, first),
        grid=(2,),
        in_specs=[whole] * 3 + [sum_spec],
        out_specs=sum_spec,
        out_shape=in_hbm((tokens, width), jnp.bfloat16),
        compiler_params=pltpu.CompilerParams(vmem_limit_bytes=SMALL_VMEM),
        cost_estimate=pl.CostEstimate(flops=2 * tokens * depth * width, bytes_accessed=8 * tokens * width, transcendentals=0),
        name="far",
    )(*[from_vmem(array) for array in (*pieces[3:], w_others, near)])


def shifted(block, by):
    count = lax.axis_size("head")
    return lax.ppermute(block, "head", [(at, (at + by) % count) for at in range(count)])


def ring(block):
    half = block.shape[0] // 2
    right, left = shifted(block, 1), shifted(block, -1)
    return block, right, left, shifted(right[:half], 1), shifted(left[half:], -1)


def other_core(block):
    count = lax.axis_size("seq")
    return lax.ppermute(block, "seq", [(at, at ^ 1) for at in range(count)])


def over_frames(blocks):
    count = lax.axis_size("seq")
    groups = [list(range(core, count, CORES)) for core in range(CORES)]
    return lax.all_to_all(blocks, "seq", 0, 0, axis_index_groups=groups)


def body(query_rows, key_rows, value_rows, query_gain, key_gain, head_class, out_weight):
    tokens = query_rows.shape[0]
    group_count = lax.axis_size("head")
    query_gain = query_gain.reshape(1, HD)
    key_gain = key_gain.reshape(1, HD)
    packed = pack(head_class, query_rows, key_rows, value_rows, query_gain, key_gain)
    arrived = over_frames(packed.reshape(FRAMES, tokens // FRAMES, TMAX * 3 * HD))

    core = lax.rem(lax.axis_index("seq"), CORES)
    place = jnp.stack([lax.axis_index("head"), core]).astype(jnp.int32)
    w_own, *halves_of_others = weight_blocks(head_class, place, out_weight, group_count)
    (other_keys,) = hold((other_core(key_rows),), halves_of_others)
    other_values = other_core(value_rows)
    near_out = spatial(head_class, query_rows, key_rows, other_keys, value_rows, other_values, query_gain, key_gain)

    fetched = [shifted(half, by + 1) for by, half in enumerate(halves_of_others)]
    fetched = jnp.stack(hold(fetched, (near_out,)))
    rest = other_core(fetched)
    w_others = jnp.where(core == 0, jnp.concatenate([fetched, rest], axis=1), jnp.concatenate([rest, fetched], axis=1))

    early = ring(near_out)
    half = TMAX // 2
    width = half * HD
    sent = [temporal(head_class, arrived, part * half, half, (*early[1:3], w_others)) for part in range(2)]

    returned = over_frames(sent[0])
    (later,) = hold((sent[1],), (returned,))
    (returned,) = hold((returned,), (later,))
    first = ring(returned.reshape(tokens, width))
    total = project_all("early", 0, early, w_own, w_others)
    returned = over_frames(later)
    (returned,) = hold((returned,), (*first[1:], total))
    last = ring(returned.reshape(tokens, width))

    total = project_all("first", 0, first, w_own, w_others, total)
    return project_last(width, last, w_own, w_others, total)


def solution(mesh):
    return jax.shard_map(
        body,
        mesh=mesh,
        in_specs=(
            P("seq", "head"),
            P("seq", "head"),
            P("seq", "head"),
            P(),
            P(),
            P("head"),
            P("head", None),
        ),
        out_specs=P("seq", "head"),
        check_vma=False,
    )
```

```python
import functools
import math

import jax
import jax.numpy as jnp
from jax import lax
from jax.experimental import pallas as pl
from jax.experimental.pallas import tpu as pltpu
from jax.sharding import PartitionSpec as P

FRAMES = 32
TMAX = 4
SMALL_VMEM = 16 * 1024 * 1024
CORES = 2
ROWS = 8
HD = 128
EPSILON = 1e-06
LOG2_SCALE = math.log2(math.e) / math.sqrt(HD)


def in_hbm(shape, dtype):
    return pltpu.HBM(shape, dtype)


def from_hbm(array):
    return pltpu.with_memory_space_constraint(array, pltpu.HBM)


def from_vmem(array):
    return pltpu.with_memory_space_constraint(array, pltpu.VMEM)


def temporal_count(classes, head_count):
    total = classes[0]
    for head in range(1, head_count):
        total = total + classes[head]
    return total


def head_of(classes, slot, head_count):
    temporal_seen = jnp.int32(0)
    spatial_seen = temporal_count(classes, head_count)
    found = jnp.int32(0)
    for head in range(head_count):
        kind = classes[head]
        rank = jnp.where(kind == 1, temporal_seen, spatial_seen)
        found = jnp.where(rank == slot, jnp.int32(head), found)
        temporal_seen = temporal_seen + kind
        spatial_seen = spatial_seen + 1 - kind
    return found


def normed(rows, gain):
    widened = rows.astype(jnp.float32)
    mean = jnp.mean(widened * widened, axis=-1, keepdims=True)
    return (widened * lax.rsqrt(mean + EPSILON) * gain).astype(jnp.bfloat16)


def scores_of(queries, keys):
    return lax.dot_general(queries, keys, (((1,), (1,)), ((), ())), preferred_element_type=jnp.float32)


def hold_kernel(*refs):
    pass


def hold(arrays, after):
    anywhere = pl.BlockSpec(memory_space=pl.ANY)
    return pl.pallas_call(
        hold_kernel,
        in_specs=[anywhere] * (len(arrays) + len(after)),
        out_specs=[anywhere] * len(arrays),
        out_shape=[in_hbm(array.shape, array.dtype) for array in arrays],
        input_output_aliases={at: at for at in range(len(arrays))},
        cost_estimate=pl.CostEstimate(flops=0, bytes_accessed=0, transcendentals=0),
        name="hold",
    )(*[from_hbm(array) for array in (*arrays, *after)])


def pack_kernel(head_count, classes, query, key, value, query_gain, key_gain, out, raw, ready, in_sems, out_sems):
    heads = [head_of(classes, slot, head_count) for slot in range(TMAX)]
    gains = (query_gain, key_gain, None)
    loads, stores = [], []
    for at in range(3 * TMAX):
        slot, which = divmod(at, 3)
        source = (query, key, value)[which].at[:, pl.ds(pl.multiple_of(heads[slot] * HD, HD), HD)]
        landing = raw if gains[which] is not None else ready
        loads.append(pltpu.make_async_copy(source, landing.at[at], in_sems.at[at]))
        loads[-1].start()
    for at in range(3 * TMAX):
        gain = gains[at % 3]
        loads[at].wait()
        if gain is not None:
            ready[at] = normed(raw[at], gain[...])
        stores.append(pltpu.make_async_copy(ready.at[at], out.at[:, pl.ds(at * HD, HD)], out_sems.at[at]))
        stores[-1].start()
    for store in stores:
        store.wait()


def pack(head_class, query_rows, key_rows, value_rows, query_gain, key_gain):
    tokens, width = query_rows.shape
    anywhere = pl.BlockSpec(memory_space=pl.ANY)
    gain_spec = pl.BlockSpec((1, HD), lambda step, classes: (0, 0))
    return pl.pallas_call(
        functools.partial(pack_kernel, width // HD),
        grid_spec=pltpu.PrefetchScalarGridSpec(
            num_scalar_prefetch=1,
            grid=(1,),
            in_specs=[anywhere] * 3 + [gain_spec] * 2,
            out_specs=anywhere,
            scratch_shapes=[
                pltpu.VMEM((3 * TMAX, tokens, HD), jnp.bfloat16),
                pltpu.VMEM((3 * TMAX, tokens, HD), jnp.bfloat16),
                pltpu.SemaphoreType.DMA((3 * TMAX,)),
                pltpu.SemaphoreType.DMA((3 * TMAX,)),
            ],
        ),
        out_shape=in_hbm((tokens, TMAX * 3 * HD), jnp.bfloat16),
        cost_estimate=pl.CostEstimate(flops=8 * tokens * TMAX * HD, bytes_accessed=12 * tokens * TMAX * HD, transcendentals=0),
        name="pack",
    )(head_class, from_hbm(query_rows), from_hbm(key_rows), from_hbm(value_rows), query_gain, key_gain)


def spatial_kernel(head_count, classes, query, key, other_key, value, other_value, query_gain, key_gain, front, back, keys, values):
    slot = pl.program_id(0)
    tokens = query.shape[0]
    chunk = tokens // 4
    is_front = slot < TMAX

    @pl.when(slot >= temporal_count(classes, head_count))
    def _():
        keys[:tokens] = normed(key[...], key_gain[...])
        keys[tokens:] = normed(other_key[...], key_gain[...])
        values[:tokens, :HD] = value[...]
        values[tokens:, :HD] = other_value[...]
        values[:, HD:] = jnp.ones((2 * tokens, HD), jnp.bfloat16)

        def step(index, carry):
            rows = pl.ds(pl.multiple_of(index * chunk, chunk), chunk)
            queries = normed(query[rows, :], query_gain[...])
            weights = jnp.exp2(scores_of(queries, keys[...]) * LOG2_SCALE).astype(jnp.bfloat16)
            summed = jnp.dot(weights, values[...], preferred_element_type=jnp.float32)
            result = (summed[:, :HD] / summed[:, HD:]).astype(jnp.bfloat16)

            @pl.when(is_front)
            def _():
                front[rows, :] = result

            @pl.when(jnp.logical_not(is_front))
            def _():
                back[rows, :] = result

            return carry

        lax.fori_loop(0, tokens // chunk, step, 0)

    @pl.when(slot < temporal_count(classes, head_count))
    def _():
        front[...] = jnp.zeros_like(front)


def spatial(head_class, query_rows, key_rows, other_keys, value_rows, other_values, query_gain, key_gain):
    tokens, width = query_rows.shape
    head_count = width // HD

    def rows(slot, classes):
        return 0, head_of(classes, slot, head_count)

    row_spec = pl.BlockSpec((tokens, HD), rows)
    gain_spec = pl.BlockSpec((1, HD), lambda slot, classes: (0, 0))
    return pl.pallas_call(
        functools.partial(spatial_kernel, head_count),
        grid_spec=pltpu.PrefetchScalarGridSpec(
            num_scalar_prefetch=1,
            grid=(head_count,),
            in_specs=[row_spec] * 5 + [gain_spec] * 2,
            out_specs=[
                pl.BlockSpec((tokens, HD), lambda slot, classes: (0, jnp.minimum(slot, TMAX - 1))),
                pl.BlockSpec((tokens, HD), lambda slot, classes: (0, jnp.maximum(slot - TMAX, 0))),
            ],
            scratch_shapes=[
                pltpu.VMEM((2 * tokens, HD), jnp.bfloat16),
                pltpu.VMEM((2 * tokens, 2 * HD), jnp.bfloat16),
            ],
        ),
        out_shape=[
            in_hbm((tokens, TMAX * HD), jnp.bfloat16),
            in_hbm((tokens, width - TMAX * HD), jnp.bfloat16),
        ],
        cost_estimate=pl.CostEstimate(
            flops=16 * tokens * tokens * width, bytes_accessed=12 * tokens * width, transcendentals=2 * tokens * tokens * head_count
        ),
        name="spatial",
    )(head_class, query_rows, key_rows, from_hbm(other_keys), value_rows, from_hbm(other_values), query_gain, key_gain)


def temporal_kernel(head_count, classes, packed, *rest):
    out, held, sems = rest[-3:]
    frames, positions, _ = packed.shape
    count = frames * ROWS
    row = lax.broadcasted_iota(jnp.int32, (count, count), 0)
    column = lax.broadcasted_iota(jnp.int32, (count, count), 1)
    same = (row & (ROWS - 1)) == (column & (ROWS - 1))
    total = temporal_count(classes, head_count)

    def attend(queries, keys, values):
        exponents = jnp.where(same, scores_of(queries, keys) * LOG2_SCALE, -1e30)
        weights = jnp.exp2(exponents).astype(jnp.bfloat16)
        both = jnp.concatenate([values, jnp.ones_like(values)], axis=1)
        summed = jnp.dot(weights, both, preferred_element_type=jnp.float32)
        return (summed[:, :HD] / summed[:, HD:]).reshape(frames, ROWS, HD)

    def store(slot):
        return pltpu.make_async_copy(held.at[slot], out.at[:, :, pl.ds(slot * HD, HD)], sems.at[slot])

    for slot in range(TMAX):

        @pl.when(slot < total)
        def _(slot=slot):
            for begin in range(0, positions, 2 * ROWS):
                at = slice(begin, begin + 2 * ROWS)
                columns = [slice((3 * slot + which) * HD, (3 * slot + which + 1) * HD) for which in range(3)]
                wide = [packed[:, at, column].astype(jnp.float32) for column in columns]
                results = []
                for first in (0, ROWS):
                    parts = [array[:, first : first + ROWS].reshape(count, HD).astype(jnp.bfloat16) for array in wide]
                    results.append(attend(*parts))
                held[slot, :, at] = jnp.concatenate(results, axis=1).astype(jnp.bfloat16)

        @pl.when(slot >= total)
        def _(slot=slot):
            held[slot] = jnp.zeros(held.shape[1:], held.dtype)

        store(slot).start()
    for slot in range(TMAX):
        store(slot).wait()


def temporal(head_class, packed, after):
    frames, positions, _ = packed.shape
    return pl.pallas_call(
        functools.partial(temporal_kernel, head_class.shape[0]),
        grid_spec=pltpu.PrefetchScalarGridSpec(
            num_scalar_prefetch=1,
            grid=(1,),
            in_specs=[pl.BlockSpec(memory_space=pltpu.VMEM)] + [pl.BlockSpec(memory_space=pl.ANY)] * len(after),
            out_specs=pl.BlockSpec(memory_space=pl.ANY),
            scratch_shapes=[
                pltpu.VMEM((TMAX, frames, positions, HD), jnp.bfloat16),
                pltpu.SemaphoreType.DMA((TMAX,)),
            ],
        ),
        out_shape=in_hbm((frames, positions, TMAX * HD), jnp.bfloat16),
        compiler_params=pltpu.CompilerParams(vmem_limit_bytes=SMALL_VMEM),
        cost_estimate=pl.CostEstimate(
            flops=32 * frames * frames * positions * TMAX * HD,
            bytes_accessed=8 * frames * positions * TMAX * HD,
            transcendentals=8 * frames * frames * positions * TMAX,
        ),
        name="temporal",
    )(head_class, from_vmem(packed), *[from_hbm(array) for array in after])


def weight_kernel(classes, place, weight, own, *others):
    width = own.shape[1]
    group_count = len(others) + 1

    def columns(shift):
        block = lax.rem(place[0] + shift, group_count)
        return weight[:, pl.ds(pl.multiple_of(block * width, width), width)]

    own[...] = columns(0)

    @pl.when(pl.program_id(0) // (pl.num_programs(0) // CORES) == place[1])
    def _():
        for shift, other in enumerate(others):
            other[...] = columns(shift + 1)


def weight_blocks(head_class, place, weight, group_count):
    rows, columns = weight.shape
    head_count = rows // HD
    share = head_count // CORES
    width = columns // group_count

    def half_rows(slot, classes, place):
        return jnp.clip(slot - place[1] * share, 0, share - 1), 0

    return pl.pallas_call(
        weight_kernel,
        grid_spec=pltpu.PrefetchScalarGridSpec(
            num_scalar_prefetch=2,
            grid=(head_count,),
            in_specs=[pl.BlockSpec((HD, columns), lambda slot, classes, place: (head_of(classes, slot, head_count), 0))],
            out_specs=[pl.BlockSpec((HD, width), lambda slot, classes, place: (slot, 0))]
            + [pl.BlockSpec((HD, width), half_rows)] * (group_count - 1),
        ),
        out_shape=[in_hbm((rows, width), jnp.bfloat16)] + [in_hbm((rows // CORES, width), jnp.bfloat16)] * (group_count - 1),
        cost_estimate=pl.CostEstimate(flops=0, bytes_accessed=4 * rows * columns, transcendentals=0),
        name="weight_blocks",
    )(head_class, place, weight)


def product(rows, weight, first):
    return jnp.dot(rows, weight[first : first + rows.shape[1]], preferred_element_type=jnp.float32)


def near_sum(own, right, left, w_own, w_others, first):
    return product(own[...], w_own, first) + product(right[...], w_others.at[0], first) + product(left[...], w_others.at[2], first)


def early_kernel(first, own_top, own_bottom, right_top, right_bottom, left_top, left_bottom, far_top, far_bottom, w_own, w_others, out):
    half = own_top.shape[0]
    parts = ((own_top, right_top, left_top, far_top), (own_bottom, right_bottom, left_bottom, far_bottom))
    for part, (own, right, left, far) in enumerate(parts):
        total = near_sum(own, right, left, w_own, w_others, first) + product(far[...], w_others.at[1], first)
        out[part * half : (part + 1) * half] = total


def near_kernel(own_top, own_bottom, right_top, right_bottom, left_top, left_bottom, w_own, w_others, total, out):
    half = own_top.shape[0]
    for part, (own, right, left) in enumerate(((own_top, right_top, left_top), (own_bottom, right_bottom, left_bottom))):
        rows = slice(part * half, (part + 1) * half)
        out[rows] = total[rows] + near_sum(own, right, left, w_own, w_others, 0)


def far_kernel(far_top, far_bottom, w_others, total, out, held, sems):
    steps, rows, _ = held.shape
    stores = []
    for step in range(steps):
        far = (far_top, far_bottom)[2 * step // steps]
        begin = step * rows % far.shape[0]
        summed = product(far[begin : begin + rows], w_others.at[1], 0) + total[step * rows : (step + 1) * rows]
        held[step] = summed.astype(held.dtype)
        stores.append(pltpu.make_async_copy(held.at[step], out.at[pl.ds(step * rows, rows)], sems.at[step]))
        stores[-1].start()
    for store in stores:
        store.wait()


def summing(kernel, name, operands, depth_terms):
    tokens, width = 2 * operands[0].shape[0], operands[-1].shape[-1]
    depth = operands[0].shape[1]
    whole = pl.BlockSpec(memory_space=pltpu.VMEM)
    return pl.pallas_call(
        kernel,
        in_specs=[whole] * len(operands),
        out_specs=whole,
        out_shape=pltpu.VMEM((tokens, width), jnp.float32),
        compiler_params=pltpu.CompilerParams(vmem_limit_bytes=SMALL_VMEM),
        cost_estimate=pl.CostEstimate(
            flops=2 * depth_terms * tokens * depth * width, bytes_accessed=8 * tokens * width, transcendentals=0
        ),
        name=name,
    )(*[from_vmem(array) for array in operands])


def project_early(pieces, w_own, w_others):
    first = TMAX * HD
    return summing(functools.partial(early_kernel, first), "project_early", (*pieces, w_own, w_others), 4)


def project_late(pieces, w_own, w_others, total):
    near = summing(near_kernel, "near", (*pieces[:6], w_own, w_others, total), 3)
    tokens, width = near.shape
    depth = pieces[0].shape[1]
    steps = 4
    return pl.pallas_call(
        far_kernel,
        in_specs=[pl.BlockSpec(memory_space=pltpu.VMEM)] * 4,
        out_specs=pl.BlockSpec(memory_space=pl.ANY),
        out_shape=in_hbm((tokens, width), jnp.bfloat16),
        scratch_shapes=[pltpu.VMEM((steps, tokens // steps, width), jnp.bfloat16), pltpu.SemaphoreType.DMA((steps,))],
        compiler_params=pltpu.CompilerParams(vmem_limit_bytes=SMALL_VMEM),
        cost_estimate=pl.CostEstimate(flops=2 * tokens * depth * width, bytes_accessed=8 * tokens * width, transcendentals=0),
        name="far",
    )(*[from_vmem(array) for array in (*pieces[6:], w_others, near)])


def shifted(block, by):
    count = lax.axis_size("head")
    return lax.ppermute(block, "head", [(at, (at + by) % count) for at in range(count)])


def ring(top, bottom):
    right_top, left_bottom = shifted(top, 1), shifted(bottom, -1)
    right_bottom, left_top = shifted(bottom, 1), shifted(top, -1)
    far_top, far_bottom = shifted(right_top, 1), shifted(left_bottom, -1)
    return top, bottom, right_top, right_bottom, left_top, left_bottom, far_top, far_bottom


def other_core(block):
    count = lax.axis_size("seq")
    return lax.ppermute(block, "seq", [(at, at ^ 1) for at in range(count)])


def over_frames(blocks):
    count = lax.axis_size("seq")
    groups = [list(range(core, count, CORES)) for core in range(CORES)]
    return lax.all_to_all(blocks, "seq", 0, 0, axis_index_groups=groups)


def body(query_rows, key_rows, value_rows, query_gain, key_gain, head_class, out_weight):
    tokens = query_rows.shape[0]
    group_count = lax.axis_size("head")
    query_gain = query_gain.reshape(1, HD)
    key_gain = key_gain.reshape(1, HD)
    packed = pack(head_class, query_rows, key_rows, value_rows, query_gain, key_gain)
    arrived = over_frames(packed.reshape(FRAMES, tokens // FRAMES, TMAX * 3 * HD))

    other_keys, other_values = other_core(key_rows), other_core(value_rows)
    front, back = spatial(head_class, query_rows, key_rows, other_keys, value_rows, other_values, query_gain, key_gain)
    core = lax.rem(lax.axis_index("seq"), CORES)
    place = jnp.stack([lax.axis_index("head"), core]).astype(jnp.int32)
    w_own, *halves = weight_blocks(head_class, place, out_weight, group_count)

    fetched = [shifted(half, by + 1) for by, half in enumerate(halves)]
    fetched = jnp.stack(hold(fetched, (back,)))
    rest = other_core(fetched)
    w_others = jnp.where(core == 0, jnp.concatenate([fetched, rest], axis=1), jnp.concatenate([rest, fetched], axis=1))

    middle = tokens // 2
    pieces = ring(back[:middle], back[middle:])
    returned = over_frames(temporal(head_class, arrived, (*pieces[2:], w_others))).reshape(tokens, TMAX * HD)
    early = project_early(pieces, w_own, w_others)
    pieces = ring(returned[:middle] + front[:middle], returned[middle:] + front[middle:])
    return project_late(pieces, w_own, w_others, early)


def solution(mesh):
    return jax.shard_map(
        body,
        mesh=mesh,
        in_specs=(
            P("seq", "head"),
            P("seq", "head"),
            P("seq", "head"),
            P(),
            P(),
            P("head"),
            P("head", None),
        ),
        out_specs=P("seq", "head"),
        check_vma=False,
    )
```

```python
import functools
import math

import jax
import jax.numpy as jnp
from jax import lax
from jax.experimental import pallas as pl
from jax.experimental.pallas import tpu as pltpu
from jax.sharding import PartitionSpec as P

FRAMES = 32
TMAX = 4
ORDER_WEIGHT = 20
SMALL_VMEM = 16 * 1024 * 1024
CORES = 2
FIRST = 2
ROWS = 8
HD = 128
EPSILON = 1e-06
LOG2_SCALE = math.log2(math.e) / math.sqrt(HD)


def in_hbm(shape, dtype):
    return pltpu.HBM(shape, dtype)


def from_hbm(array):
    return pltpu.with_memory_space_constraint(array, pltpu.HBM)


def from_vmem(array):
    return pltpu.with_memory_space_constraint(array, pltpu.VMEM)


def temporal_count(classes, head_count):
    total = classes[0]
    for head in range(1, head_count):
        total = total + classes[head]
    return total


def head_of(classes, slot, head_count):
    temporal_seen = jnp.int32(0)
    spatial_seen = temporal_count(classes, head_count)
    found = jnp.int32(0)
    for head in range(head_count):
        kind = classes[head]
        rank = jnp.where(kind == 1, temporal_seen, spatial_seen)
        found = jnp.where(rank == slot, jnp.int32(head), found)
        temporal_seen = temporal_seen + kind
        spatial_seen = spatial_seen + 1 - kind
    return found


def normed(rows, gain):
    widened = rows.astype(jnp.float32)
    mean = jnp.mean(widened * widened, axis=-1, keepdims=True)
    return (widened * lax.rsqrt(mean + EPSILON) * gain).astype(jnp.bfloat16)


def scores_of(queries, keys):
    return lax.dot_general(queries, keys, (((1,), (1,)), ((), ())), preferred_element_type=jnp.float32)


def hold_kernel(*refs):
    pass


def hold(arrays, after):
    anywhere = pl.BlockSpec(memory_space=pl.ANY)
    return pl.pallas_call(
        hold_kernel,
        in_specs=[anywhere] * (len(arrays) + len(after)),
        out_specs=[anywhere] * len(arrays),
        out_shape=[in_hbm(array.shape, array.dtype) for array in arrays],
        input_output_aliases={at: at for at in range(len(arrays))},
        cost_estimate=pl.CostEstimate(flops=0, bytes_accessed=0, transcendentals=0),
        name="hold",
    )(*[from_hbm(array) for array in arrays], *after)


def pack_kernel(head_count, classes, query, key, value, query_gain, key_gain, now, later, raw, ready, in_sems, out_sems):
    heads = [head_of(classes, slot, head_count) for slot in range(TMAX)]
    gains = (query_gain, key_gain, None)
    loads, stores = [], []
    for at in range(3 * TMAX):
        slot, which = divmod(at, 3)
        source = (query, key, value)[which].at[:, pl.ds(pl.multiple_of(heads[slot] * HD, HD), HD)]
        landing = raw if gains[which] is not None else ready
        loads.append(pltpu.make_async_copy(source, landing.at[at], in_sems.at[at]))
        loads[-1].start()
    for at in range(3 * TMAX):
        gain = gains[at % 3]
        loads[at].wait()
        if gain is not None:
            ready[at] = normed(raw[at], gain[...])
        split = 3 * FIRST
        if at < split:
            target = now.at[:, pl.ds(at * HD, HD)]
        else:
            target = later.at[:, pl.ds((FIRST + at - split) * HD, HD)]
        stores.append(pltpu.make_async_copy(ready.at[at], target, out_sems.at[at]))
        stores[-1].start()
    for store in stores:
        store.wait()


def pack(head_class, query_rows, key_rows, value_rows, query_gain, key_gain):
    tokens, width = query_rows.shape
    anywhere = pl.BlockSpec(memory_space=pl.ANY)
    gain_spec = pl.BlockSpec((1, HD), lambda step, classes: (0, 0))
    return pl.pallas_call(
        functools.partial(pack_kernel, width // HD),
        grid_spec=pltpu.PrefetchScalarGridSpec(
            num_scalar_prefetch=1,
            grid=(1,),
            in_specs=[anywhere] * 3 + [gain_spec] * 2,
            out_specs=[anywhere] * 2,
            scratch_shapes=[
                pltpu.VMEM((3 * TMAX, tokens, HD), jnp.bfloat16),
                pltpu.VMEM((3 * TMAX, tokens, HD), jnp.bfloat16),
                pltpu.SemaphoreType.DMA((3 * TMAX,)),
                pltpu.SemaphoreType.DMA((3 * TMAX,)),
            ],
        ),
        out_shape=[
            in_hbm((tokens, FIRST * 3 * HD), jnp.bfloat16),
            in_hbm((tokens, (FIRST + (TMAX - FIRST) * 3) * HD), jnp.bfloat16),
        ],
        cost_estimate=pl.CostEstimate(flops=8 * tokens * TMAX * HD, bytes_accessed=12 * tokens * TMAX * HD, transcendentals=0),
        name="pack",
    )(head_class, from_hbm(query_rows), from_hbm(key_rows), from_hbm(value_rows), query_gain, key_gain)


def spatial_kernel(head_count, classes, query, key, other_key, value, other_value, query_gain, key_gain, front, back, keys, values):
    slot = pl.program_id(0)
    tokens = query.shape[0]
    chunk = tokens // 4
    is_front = slot < TMAX

    @pl.when(slot >= temporal_count(classes, head_count))
    def _():
        keys[:tokens] = normed(key[...], key_gain[...])
        keys[tokens:] = normed(other_key[...], key_gain[...])
        values[:tokens, :HD] = value[...]
        values[tokens:, :HD] = other_value[...]
        values[:, HD:] = jnp.ones((2 * tokens, HD), jnp.bfloat16)

        def step(index, carry):
            rows = pl.ds(pl.multiple_of(index * chunk, chunk), chunk)
            queries = normed(query[rows, :], query_gain[...])
            weights = jnp.exp2(scores_of(queries, keys[...]) * LOG2_SCALE).astype(jnp.bfloat16)
            summed = jnp.dot(weights, values[...], preferred_element_type=jnp.float32)
            result = (summed[:, :HD] / summed[:, HD:]).astype(jnp.bfloat16)

            @pl.when(is_front)
            def _():
                front[rows, :] = result

            @pl.when(jnp.logical_not(is_front))
            def _():
                back[rows, :] = result

            return carry

        lax.fori_loop(0, tokens // chunk, step, 0)

    @pl.when(slot < temporal_count(classes, head_count))
    def _():
        front[...] = jnp.zeros_like(front)


def spatial(head_class, query_rows, key_rows, other_keys, value_rows, other_values, query_gain, key_gain):
    tokens, width = query_rows.shape
    head_count = width // HD

    def rows(slot, classes):
        return 0, head_of(classes, slot, head_count)

    row_spec = pl.BlockSpec((tokens, HD), rows)
    gain_spec = pl.BlockSpec((1, HD), lambda slot, classes: (0, 0))
    return pl.pallas_call(
        functools.partial(spatial_kernel, head_count),
        grid_spec=pltpu.PrefetchScalarGridSpec(
            num_scalar_prefetch=1,
            grid=(head_count,),
            in_specs=[row_spec] * 5 + [gain_spec] * 2,
            out_specs=[
                pl.BlockSpec((tokens, HD), lambda slot, classes: (0, jnp.minimum(slot, TMAX - 1))),
                pl.BlockSpec((tokens, HD), lambda slot, classes: (0, jnp.maximum(slot - TMAX, 0))),
            ],
            scratch_shapes=[
                pltpu.VMEM((2 * tokens, HD), jnp.bfloat16),
                pltpu.VMEM((2 * tokens, 2 * HD), jnp.bfloat16),
            ],
        ),
        out_shape=[
            in_hbm((tokens, TMAX * HD), jnp.bfloat16),
            in_hbm((tokens, width - TMAX * HD), jnp.bfloat16),
        ],
        cost_estimate=pl.CostEstimate(
            flops=16 * tokens * tokens * width, bytes_accessed=12 * tokens * width, transcendentals=2 * tokens * tokens * head_count
        ),
        name="spatial",
    )(head_class, query_rows, key_rows, from_hbm(other_keys), value_rows, from_hbm(other_values), query_gain, key_gain)


def temporal_kernel(head_count, begin, slots, base, classes, packed, *rest):
    out, held, sems = rest[-3:]
    frames, positions, _ = packed.shape
    count = frames * ROWS
    row = lax.broadcasted_iota(jnp.int32, (count, count), 0)
    column = lax.broadcasted_iota(jnp.int32, (count, count), 1)
    same = (row & (ROWS - 1)) == (column & (ROWS - 1))
    total = temporal_count(classes, head_count)

    def attend(queries, keys, values):
        exponents = jnp.where(same, scores_of(queries, keys) * LOG2_SCALE, -1e30)
        weights = jnp.exp2(exponents).astype(jnp.bfloat16)
        both = jnp.concatenate([values, jnp.ones_like(values)], axis=1)
        summed = jnp.dot(weights, both, preferred_element_type=jnp.float32)
        return (summed[:, :HD] / summed[:, HD:]).reshape(frames, ROWS, HD)

    def store(slot):
        return pltpu.make_async_copy(held.at[slot], out.at[:, :, pl.ds(slot * HD, HD)], sems.at[slot])

    for slot in range(slots):

        @pl.when(begin + slot < total)
        def _(slot=slot):
            for start in range(0, positions, 2 * ROWS):
                at = slice(start, start + 2 * ROWS)
                columns = [slice(base + (3 * slot + which) * HD, base + (3 * slot + which + 1) * HD) for which in range(3)]
                wide = [packed[:, at, column].astype(jnp.float32) for column in columns]
                results = []
                for first in (0, ROWS):
                    parts = [array[:, first : first + ROWS].reshape(count, HD).astype(jnp.bfloat16) for array in wide]
                    results.append(attend(*parts))
                held[slot, :, at] = jnp.concatenate(results, axis=1).astype(jnp.bfloat16)

        @pl.when(begin + slot >= total)
        def _(slot=slot):
            held[slot] = jnp.zeros(held.shape[1:], held.dtype)

        store(slot).start()
    for slot in range(slots):
        store(slot).wait()


def temporal(head_class, packed, begin, slots, base, after, into=None):
    frames, positions, _ = packed.shape
    anywhere = pl.BlockSpec(memory_space=pl.ANY)
    shape = (frames, positions, slots * HD) if into is None else into.shape
    extra = [] if into is None else [into]
    return pl.pallas_call(
        functools.partial(temporal_kernel, head_class.shape[0], begin, slots, base),
        grid_spec=pltpu.PrefetchScalarGridSpec(
            num_scalar_prefetch=1,
            grid=(1,),
            in_specs=[pl.BlockSpec(memory_space=pltpu.VMEM)] + [anywhere] * (len(after) + len(extra)),
            out_specs=anywhere,
            scratch_shapes=[
                pltpu.VMEM((slots, frames, positions, HD), jnp.bfloat16),
                pltpu.SemaphoreType.DMA((slots,)),
            ],
        ),
        out_shape=in_hbm(shape, jnp.bfloat16),
        input_output_aliases={} if into is None else {2 + len(after): 0},
        compiler_params=pltpu.CompilerParams(vmem_limit_bytes=SMALL_VMEM),
        cost_estimate=pl.CostEstimate(
            flops=32 * frames * frames * positions * slots * HD,
            bytes_accessed=8 * frames * positions * slots * HD,
            transcendentals=8 * frames * frames * positions * slots,
        ),
        name="temporal",
    )(head_class, from_vmem(packed), *[from_hbm(array) for array in (*after, *extra)])


def weight_kernel(classes, place, weight, own, *others):
    width = own.shape[1]
    group_count = len(others) + 1

    def columns(shift):
        block = lax.rem(place[0] + shift, group_count)
        return weight[:, pl.ds(pl.multiple_of(block * width, width), width)]

    own[...] = columns(0)

    @pl.when(pl.program_id(0) // (pl.num_programs(0) // CORES) == place[1])
    def _():
        for shift, other in enumerate(others):
            other[...] = columns(shift + 1)


def weight_blocks(head_class, place, weight, group_count):
    rows, columns = weight.shape
    head_count = rows // HD
    share = head_count // CORES
    width = columns // group_count

    def half_rows(slot, classes, place):
        return jnp.clip(slot - place[1] * share, 0, share - 1), 0

    return pl.pallas_call(
        weight_kernel,
        grid_spec=pltpu.PrefetchScalarGridSpec(
            num_scalar_prefetch=2,
            grid=(head_count,),
            in_specs=[pl.BlockSpec((HD, columns), lambda slot, classes, place: (head_of(classes, slot, head_count), 0))],
            out_specs=[pl.BlockSpec((HD, width), lambda slot, classes, place: (slot, 0))]
            + [pl.BlockSpec((HD, width), half_rows)] * (group_count - 1),
        ),
        out_shape=[in_hbm((rows, width), jnp.bfloat16)] + [in_hbm((rows // CORES, width), jnp.bfloat16)] * (group_count - 1),
        cost_estimate=pl.CostEstimate(flops=0, bytes_accessed=4 * rows * columns, transcendentals=0),
        name="weight_blocks",
    )(head_class, place, weight)


def product(rows, weight, first):
    return jnp.dot(rows, weight[first : first + rows.shape[1]], preferred_element_type=jnp.float32)


def near_sum(own, right, left, w_own, w_others, first, rows):
    total = product(own[rows], w_own, first)
    return total + product(right[rows], w_others.at[0], first) + product(left[rows], w_others.at[2], first)


def halves(tokens):
    return slice(0, tokens // 2), slice(tokens // 2, tokens)


def all_kernel(first, own, right, left, far_top, far_bottom, w_own, w_others, *rest):
    out = rest[-1]
    for rows, far in zip(halves(own.shape[0]), (far_top, far_bottom), strict=True):
        total = near_sum(own, right, left, w_own, w_others, first, rows) + product(far[...], w_others.at[1], first)
        out[rows] = total if len(rest) == 1 else total + rest[0][rows]


def near_kernel(first, own, right, left, w_own, w_others, total, out):
    for rows in halves(own.shape[0]):
        out[rows] = total[rows] + near_sum(own, right, left, w_own, w_others, first, rows)


def far_kernel(first, far_top, far_bottom, w_others, total, out, held, sems):
    steps, rows, _ = held.shape
    stores = []
    for step in range(steps):
        far = (far_top, far_bottom)[2 * step // steps]
        begin = step * rows % far.shape[0]
        summed = product(far[begin : begin + rows], w_others.at[1], first) + total[step * rows : (step + 1) * rows]
        held[step] = summed.astype(held.dtype)
        stores.append(pltpu.make_async_copy(held.at[step], out.at[pl.ds(step * rows, rows)], sems.at[step]))
        stores[-1].start()
    for store in stores:
        store.wait()


def summing(kernel, name, operands, depth_terms):
    tokens, width = operands[0].shape[0], operands[-1].shape[-1]
    depth = operands[0].shape[1]
    whole = pl.BlockSpec(memory_space=pltpu.VMEM)
    return pl.pallas_call(
        kernel,
        in_specs=[whole] * len(operands),
        out_specs=whole,
        out_shape=pltpu.VMEM((tokens, width), jnp.float32),
        compiler_params=pltpu.CompilerParams(vmem_limit_bytes=SMALL_VMEM),
        cost_estimate=pl.CostEstimate(
            flops=ORDER_WEIGHT * depth_terms * tokens * depth * width, bytes_accessed=8 * tokens * width, transcendentals=0
        ),
        name=name,
    )(*[from_vmem(array) for array in operands])


def project_all(name, first, pieces, w_own, w_others, *total):
    return summing(functools.partial(all_kernel, first), name, (*pieces, w_own, w_others, *total), 4)


def project_last(first, pieces, w_own, w_others, total):
    near = summing(functools.partial(near_kernel, first), "near", (*pieces[:3], w_own, w_others, total), 3)
    tokens, width = near.shape
    depth = pieces[0].shape[1]
    steps = 4
    return pl.pallas_call(
        functools.partial(far_kernel, first),
        in_specs=[pl.BlockSpec(memory_space=pltpu.VMEM)] * 4,
        out_specs=pl.BlockSpec(memory_space=pl.ANY),
        out_shape=in_hbm((tokens, width), jnp.bfloat16),
        scratch_shapes=[pltpu.VMEM((steps, tokens // steps, width), jnp.bfloat16), pltpu.SemaphoreType.DMA((steps,))],
        compiler_params=pltpu.CompilerParams(vmem_limit_bytes=SMALL_VMEM),
        cost_estimate=pl.CostEstimate(flops=2 * tokens * depth * width, bytes_accessed=8 * tokens * width, transcendentals=0),
        name="far",
    )(*[from_vmem(array) for array in (*pieces[3:], w_others, near)])


def shifted(block, by):
    count = lax.axis_size("head")
    return lax.ppermute(block, "head", [(at, (at + by) % count) for at in range(count)])


def ring(block):
    half = block.shape[0] // 2
    right, left = shifted(block, 1), shifted(block, -1)
    return block, right, left, shifted(right[:half], 1), shifted(left[half:], -1)


def other_core(block):
    count = lax.axis_size("seq")
    return lax.ppermute(block, "seq", [(at, at ^ 1) for at in range(count)])


def over_frames(blocks):
    count = lax.axis_size("seq")
    groups = [list(range(core, count, CORES)) for core in range(CORES)]
    return lax.all_to_all(blocks, "seq", 0, 0, axis_index_groups=groups)


def body(query_rows, key_rows, value_rows, query_gain, key_gain, head_class, out_weight):
    tokens = query_rows.shape[0]
    group_count = lax.axis_size("head")
    query_gain = query_gain.reshape(1, HD)
    key_gain = key_gain.reshape(1, HD)
    now, later = pack(head_class, query_rows, key_rows, value_rows, query_gain, key_gain)
    arrived = over_frames(now.reshape(FRAMES, tokens // FRAMES, -1))

    core = lax.rem(lax.axis_index("seq"), CORES)
    place = jnp.stack([lax.axis_index("head"), core]).astype(jnp.int32)
    w_own, *halves_of_others = weight_blocks(head_class, place, out_weight, group_count)
    (other_keys,) = hold((other_core(key_rows),), halves_of_others)
    other_values = other_core(value_rows)
    front, back = spatial(head_class, query_rows, key_rows, other_keys, value_rows, other_values, query_gain, key_gain)

    fetched = [shifted(half, by + 1) for by, half in enumerate(halves_of_others)]
    fetched = hold(fetched, (back,))
    fetched_first = fetched
    fetched = jnp.stack(fetched)
    rest = other_core(fetched)
    w_others = jnp.where(core == 0, jnp.concatenate([fetched, rest], axis=1), jnp.concatenate([rest, fetched], axis=1))

    width = FIRST * HD
    early = ring(back)
    mixed = temporal(head_class, arrived, 0, FIRST, 0, (front, *fetched_first), into=later.reshape(FRAMES, tokens // FRAMES, -1))
    arrived = over_frames(mixed)
    (front,) = hold((front,), (*early[1:], w_others))
    sent = temporal(head_class, arrived, FIRST, TMAX - FIRST, width, (front,))
    (front,) = hold((front,), (sent,))
    chosen = arrived[:, :, :width].reshape(tokens, width) + front[:, :width]
    first = ring(chosen)
    (sent,) = hold((sent,), (chosen,))
    total = project_all("early", TMAX * HD, early, w_own, w_others)
    returned = over_frames(sent).reshape(tokens, -1)
    (rest,) = hold((front,), (*first[1:], total))
    last = ring(returned + rest[:, width:])

    total = project_all("first", 0, first, w_own, w_others, total)
    return project_last(width, last, w_own, w_others, total)


def solution(mesh):
    return jax.shard_map(
        body,
        mesh=mesh,
        in_specs=(
            P("seq", "head"),
            P("seq", "head"),
            P("seq", "head"),
            P(),
            P(),
            P("head"),
            P("head", None),
        ),
        out_specs=P("seq", "head"),
        check_vma=False,
    )
```

```python
import functools
import math

import jax
import jax.numpy as jnp
from jax import lax
from jax.experimental import pallas as pl
from jax.experimental.pallas import tpu as pltpu
from jax.sharding import PartitionSpec as P

FRAMES = 32
TMAX = 4
SMALL_VMEM = 16 * 1024 * 1024
CORES = 2
ROWS = 8
HD = 128
EPSILON = 1e-06
LOG2_SCALE = math.log2(math.e) / math.sqrt(HD)


def in_hbm(shape, dtype):
    return pltpu.HBM(shape, dtype)


def from_hbm(array):
    return pltpu.with_memory_space_constraint(array, pltpu.HBM)


def from_vmem(array):
    return pltpu.with_memory_space_constraint(array, pltpu.VMEM)


def temporal_count(classes, head_count):
    total = classes[0]
    for head in range(1, head_count):
        total = total + classes[head]
    return total


def head_of(classes, slot, head_count):
    temporal_seen = jnp.int32(0)
    spatial_seen = temporal_count(classes, head_count)
    found = jnp.int32(0)
    for head in range(head_count):
        kind = classes[head]
        rank = jnp.where(kind == 1, temporal_seen, spatial_seen)
        found = jnp.where(rank == slot, jnp.int32(head), found)
        temporal_seen = temporal_seen + kind
        spatial_seen = spatial_seen + 1 - kind
    return found


def normed(rows, gain):
    widened = rows.astype(jnp.float32)
    mean = jnp.mean(widened * widened, axis=-1, keepdims=True)
    return (widened * lax.rsqrt(mean + EPSILON) * gain).astype(jnp.bfloat16)


def scores_of(queries, keys):
    return lax.dot_general(queries, keys, (((1,), (1,)), ((), ())), preferred_element_type=jnp.float32)


def hold_kernel(*refs):
    pass


def hold(arrays, after):
    anywhere = pl.BlockSpec(memory_space=pl.ANY)
    return pl.pallas_call(
        hold_kernel,
        in_specs=[anywhere] * (len(arrays) + len(after)),
        out_specs=[anywhere] * len(arrays),
        out_shape=[in_hbm(array.shape, array.dtype) for array in arrays],
        input_output_aliases={at: at for at in range(len(arrays))},
        cost_estimate=pl.CostEstimate(flops=0, bytes_accessed=0, transcendentals=0),
        name="hold",
    )(*[from_hbm(array) for array in (*arrays, *after)])


def pack_kernel(head_count, classes, query, key, value, query_gain, key_gain, out, raw, ready, in_sems, out_sems):
    heads = [head_of(classes, slot, head_count) for slot in range(TMAX)]
    gains = (query_gain, key_gain, None)
    loads, stores = [], []
    for at in range(3 * TMAX):
        slot, which = divmod(at, 3)
        source = (query, key, value)[which].at[:, pl.ds(pl.multiple_of(heads[slot] * HD, HD), HD)]
        landing = raw if gains[which] is not None else ready
        loads.append(pltpu.make_async_copy(source, landing.at[at], in_sems.at[at]))
        loads[-1].start()
    for at in range(3 * TMAX):
        gain = gains[at % 3]
        loads[at].wait()
        if gain is not None:
            ready[at] = normed(raw[at], gain[...])
        stores.append(pltpu.make_async_copy(ready.at[at], out.at[:, pl.ds(at * HD, HD)], out_sems.at[at]))
        stores[-1].start()
    for store in stores:
        store.wait()


def pack(head_class, query_rows, key_rows, value_rows, query_gain, key_gain):
    tokens, width = query_rows.shape
    anywhere = pl.BlockSpec(memory_space=pl.ANY)
    gain_spec = pl.BlockSpec((1, HD), lambda step, classes: (0, 0))
    return pl.pallas_call(
        functools.partial(pack_kernel, width // HD),
        grid_spec=pltpu.PrefetchScalarGridSpec(
            num_scalar_prefetch=1,
            grid=(1,),
            in_specs=[anywhere] * 3 + [gain_spec] * 2,
            out_specs=anywhere,
            scratch_shapes=[
                pltpu.VMEM((3 * TMAX, tokens, HD), jnp.bfloat16),
                pltpu.VMEM((3 * TMAX, tokens, HD), jnp.bfloat16),
                pltpu.SemaphoreType.DMA((3 * TMAX,)),
                pltpu.SemaphoreType.DMA((3 * TMAX,)),
            ],
        ),
        out_shape=in_hbm((tokens, TMAX * 3 * HD), jnp.bfloat16),
        cost_estimate=pl.CostEstimate(flops=8 * tokens * TMAX * HD, bytes_accessed=12 * tokens * TMAX * HD, transcendentals=0),
        name="pack",
    )(head_class, from_hbm(query_rows), from_hbm(key_rows), from_hbm(value_rows), query_gain, key_gain)


def spatial_kernel(head_count, classes, query, key, other_key, value, other_value, query_gain, key_gain, front, back, keys, values):
    slot = pl.program_id(0)
    tokens = query.shape[0]
    chunk = tokens // 4
    is_front = slot < TMAX

    @pl.when(slot >= temporal_count(classes, head_count))
    def _():
        keys[:tokens] = normed(key[...], key_gain[...])
        keys[tokens:] = normed(other_key[...], key_gain[...])
        values[:tokens, :HD] = value[...]
        values[tokens:, :HD] = other_value[...]
        values[:, HD:] = jnp.ones((2 * tokens, HD), jnp.bfloat16)

        def step(index, carry):
            rows = pl.ds(pl.multiple_of(index * chunk, chunk), chunk)
            queries = normed(query[rows, :], query_gain[...])
            weights = jnp.exp2(scores_of(queries, keys[...]) * LOG2_SCALE).astype(jnp.bfloat16)
            summed = jnp.dot(weights, values[...], preferred_element_type=jnp.float32)
            result = (summed[:, :HD] / summed[:, HD:]).astype(jnp.bfloat16)

            @pl.when(is_front)
            def _():
                front[rows, :] = result

            @pl.when(jnp.logical_not(is_front))
            def _():
                back[rows, :] = result

            return carry

        lax.fori_loop(0, tokens // chunk, step, 0)

    @pl.when(slot < temporal_count(classes, head_count))
    def _():
        front[...] = jnp.zeros_like(front)


def spatial(head_class, query_rows, key_rows, other_keys, value_rows, other_values, query_gain, key_gain):
    tokens, width = query_rows.shape
    head_count = width // HD

    def rows(slot, classes):
        return 0, head_of(classes, slot, head_count)

    row_spec = pl.BlockSpec((tokens, HD), rows)
    gain_spec = pl.BlockSpec((1, HD), lambda slot, classes: (0, 0))
    return pl.pallas_call(
        functools.partial(spatial_kernel, head_count),
        grid_spec=pltpu.PrefetchScalarGridSpec(
            num_scalar_prefetch=1,
            grid=(head_count,),
            in_specs=[row_spec] * 5 + [gain_spec] * 2,
            out_specs=[
                pl.BlockSpec((tokens, HD), lambda slot, classes: (0, jnp.minimum(slot, TMAX - 1))),
                pl.BlockSpec((tokens, HD), lambda slot, classes: (0, jnp.maximum(slot - TMAX, 0))),
            ],
            scratch_shapes=[
                pltpu.VMEM((2 * tokens, HD), jnp.bfloat16),
                pltpu.VMEM((2 * tokens, 2 * HD), jnp.bfloat16),
            ],
        ),
        out_shape=[
            in_hbm((tokens, TMAX * HD), jnp.bfloat16),
            in_hbm((tokens, width - TMAX * HD), jnp.bfloat16),
        ],
        cost_estimate=pl.CostEstimate(
            flops=16 * tokens * tokens * width, bytes_accessed=12 * tokens * width, transcendentals=2 * tokens * tokens * head_count
        ),
        name="spatial",
    )(head_class, query_rows, key_rows, from_hbm(other_keys), value_rows, from_hbm(other_values), query_gain, key_gain)


def temporal_kernel(head_count, classes, packed, *rest):
    out, held, sems = rest[-3:]
    frames, positions, _ = packed.shape
    count = frames * ROWS
    row = lax.broadcasted_iota(jnp.int32, (count, count), 0)
    column = lax.broadcasted_iota(jnp.int32, (count, count), 1)
    same = (row & (ROWS - 1)) == (column & (ROWS - 1))
    total = temporal_count(classes, head_count)

    ones = jnp.ones((count, HD), jnp.bfloat16)

    def store(slot):
        return pltpu.make_async_copy(held.at[slot], out.at[:, :, pl.ds(slot * HD, HD)], sems.at[slot])

    for slot in range(TMAX):
        parts = []
        for begin in range(0, positions, 2 * ROWS):
            columns = [slice((3 * slot + which) * HD, (3 * slot + which + 1) * HD) for which in range(3)]
            wide = [packed[:, begin : begin + 2 * ROWS, column].astype(jnp.float32) for column in columns]
            for first in (0, ROWS):
                parts.append([array[:, first : first + ROWS].reshape(count, HD).astype(jnp.bfloat16) for array in wide])
        scores = [scores_of(queries, keys) for queries, keys, _ in parts]
        weights = [jnp.exp2(jnp.where(same, score * LOG2_SCALE, -1e30)).astype(jnp.bfloat16) for score in scores]
        results = []
        for weight, (_, _, values) in zip(weights, parts, strict=True):
            summed = jnp.dot(weight, jnp.concatenate([values, ones], axis=1), preferred_element_type=jnp.float32)
            result = jnp.where(slot < total, summed[:, :HD] / summed[:, HD:], 0.0)
            results.append(result.reshape(frames, ROWS, HD))
        for pair in range(len(results) // 2):
            both = jnp.concatenate(results[2 * pair : 2 * pair + 2], axis=1)
            held[slot, :, 2 * ROWS * pair : 2 * ROWS * (pair + 1)] = both.astype(jnp.bfloat16)
        store(slot).start()
    for slot in range(TMAX):
        store(slot).wait()


def temporal(head_class, packed, after):
    frames, positions, _ = packed.shape
    return pl.pallas_call(
        functools.partial(temporal_kernel, head_class.shape[0]),
        grid_spec=pltpu.PrefetchScalarGridSpec(
            num_scalar_prefetch=1,
            grid=(1,),
            in_specs=[pl.BlockSpec(memory_space=pltpu.VMEM)] + [pl.BlockSpec(memory_space=pl.ANY)] * len(after),
            out_specs=pl.BlockSpec(memory_space=pl.ANY),
            scratch_shapes=[
                pltpu.VMEM((TMAX, frames, positions, HD), jnp.bfloat16),
                pltpu.SemaphoreType.DMA((TMAX,)),
            ],
        ),
        out_shape=in_hbm((frames, positions, TMAX * HD), jnp.bfloat16),
        compiler_params=pltpu.CompilerParams(vmem_limit_bytes=SMALL_VMEM),
        cost_estimate=pl.CostEstimate(
            flops=32 * frames * frames * positions * TMAX * HD,
            bytes_accessed=8 * frames * positions * TMAX * HD,
            transcendentals=8 * frames * frames * positions * TMAX,
        ),
        name="temporal",
    )(head_class, from_vmem(packed), *[from_hbm(array) for array in after])


def weight_kernel(classes, place, weight, own, *others):
    width = own.shape[1]
    group_count = len(others) + 1

    def columns(shift):
        block = lax.rem(place[0] + shift, group_count)
        return weight[:, pl.ds(pl.multiple_of(block * width, width), width)]

    own[...] = columns(0)

    @pl.when(pl.program_id(0) // (pl.num_programs(0) // CORES) == place[1])
    def _():
        for shift, other in enumerate(others):
            other[...] = columns(shift + 1)


def weight_blocks(head_class, place, weight, group_count):
    rows, columns = weight.shape
    head_count = rows // HD
    share = head_count // CORES
    width = columns // group_count

    def half_rows(slot, classes, place):
        return jnp.clip(slot - place[1] * share, 0, share - 1), 0

    return pl.pallas_call(
        weight_kernel,
        grid_spec=pltpu.PrefetchScalarGridSpec(
            num_scalar_prefetch=2,
            grid=(head_count,),
            in_specs=[pl.BlockSpec((HD, columns), lambda slot, classes, place: (head_of(classes, slot, head_count), 0))],
            out_specs=[pl.BlockSpec((HD, width), lambda slot, classes, place: (slot, 0))]
            + [pl.BlockSpec((HD, width), half_rows)] * (group_count - 1),
        ),
        out_shape=[in_hbm((rows, width), jnp.bfloat16)] + [in_hbm((rows // CORES, width), jnp.bfloat16)] * (group_count - 1),
        cost_estimate=pl.CostEstimate(flops=0, bytes_accessed=4 * rows * columns, transcendentals=0),
        name="weight_blocks",
    )(head_class, place, weight)


def product(rows, weight, first):
    return jnp.dot(rows, weight[first : first + rows.shape[1]], preferred_element_type=jnp.float32)


def near_sum(own, right, left, w_own, w_others, first):
    return product(own[...], w_own, first) + product(right[...], w_others.at[0], first) + product(left[...], w_others.at[2], first)


def early_kernel(first, own_top, own_bottom, right_top, right_bottom, left_top, left_bottom, far_top, far_bottom, w_own, w_others, out):
    half = own_top.shape[0]
    parts = ((own_top, right_top, left_top, far_top), (own_bottom, right_bottom, left_bottom, far_bottom))
    for part, (own, right, left, far) in enumerate(parts):
        total = near_sum(own, right, left, w_own, w_others, first) + product(far[...], w_others.at[1], first)
        out[part * half : (part + 1) * half] = total


def near_kernel(own_top, own_bottom, right_top, right_bottom, left_top, left_bottom, w_own, w_others, total, out):
    half = own_top.shape[0]
    for part, (own, right, left) in enumerate(((own_top, right_top, left_top), (own_bottom, right_bottom, left_bottom))):
        rows = slice(part * half, (part + 1) * half)
        out[rows] = total[rows] + near_sum(own, right, left, w_own, w_others, 0)


def far_kernel(far_top, far_bottom, w_others, total, out, held, sems):
    steps, rows, _ = held.shape
    stores = []
    for step in range(steps):
        far = (far_top, far_bottom)[2 * step // steps]
        begin = step * rows % far.shape[0]
        summed = product(far[begin : begin + rows], w_others.at[1], 0) + total[step * rows : (step + 1) * rows]
        held[step] = summed.astype(held.dtype)
        stores.append(pltpu.make_async_copy(held.at[step], out.at[pl.ds(step * rows, rows)], sems.at[step]))
        stores[-1].start()
    for store in stores:
        store.wait()


def summing(kernel, name, operands, depth_terms):
    tokens, width = 2 * operands[0].shape[0], operands[-1].shape[-1]
    depth = operands[0].shape[1]
    whole = pl.BlockSpec(memory_space=pltpu.VMEM)
    return pl.pallas_call(
        kernel,
        in_specs=[whole] * len(operands),
        out_specs=whole,
        out_shape=pltpu.VMEM((tokens, width), jnp.float32),
        compiler_params=pltpu.CompilerParams(vmem_limit_bytes=SMALL_VMEM),
        cost_estimate=pl.CostEstimate(
            flops=2 * depth_terms * tokens * depth * width, bytes_accessed=8 * tokens * width, transcendentals=0
        ),
        name=name,
    )(*[from_vmem(array) for array in operands])


def project_early(pieces, w_own, w_others):
    first = TMAX * HD
    return summing(functools.partial(early_kernel, first), "project_early", (*pieces, w_own, w_others), 4)


def project_late(pieces, w_own, w_others, total):
    near = summing(near_kernel, "near", (*pieces[:6], w_own, w_others, total), 3)
    tokens, width = near.shape
    depth = pieces[0].shape[1]
    steps = 4
    return pl.pallas_call(
        far_kernel,
        in_specs=[pl.BlockSpec(memory_space=pltpu.VMEM)] * 4,
        out_specs=pl.BlockSpec(memory_space=pl.ANY),
        out_shape=in_hbm((tokens, width), jnp.bfloat16),
        scratch_shapes=[pltpu.VMEM((steps, tokens // steps, width), jnp.bfloat16), pltpu.SemaphoreType.DMA((steps,))],
        compiler_params=pltpu.CompilerParams(vmem_limit_bytes=SMALL_VMEM),
        cost_estimate=pl.CostEstimate(flops=2 * tokens * depth * width, bytes_accessed=8 * tokens * width, transcendentals=0),
        name="far",
    )(*[from_vmem(array) for array in (*pieces[6:], w_others, near)])


def shifted(block, by):
    count = lax.axis_size("head")
    return lax.ppermute(block, "head", [(at, (at + by) % count) for at in range(count)])


def ring(top, bottom):
    right_top, left_bottom = shifted(top, 1), shifted(bottom, -1)
    right_bottom, left_top = shifted(bottom, 1), shifted(top, -1)
    far_top, far_bottom = shifted(right_top, 1), shifted(left_bottom, -1)
    return top, bottom, right_top, right_bottom, left_top, left_bottom, far_top, far_bottom


def other_core(block):
    count = lax.axis_size("seq")
    return lax.ppermute(block, "seq", [(at, at ^ 1) for at in range(count)])


def over_frames(blocks):
    count = lax.axis_size("seq")
    groups = [list(range(core, count, CORES)) for core in range(CORES)]
    return lax.all_to_all(blocks, "seq", 0, 0, axis_index_groups=groups)


def body(query_rows, key_rows, value_rows, query_gain, key_gain, head_class, out_weight):
    tokens = query_rows.shape[0]
    group_count = lax.axis_size("head")
    query_gain = query_gain.reshape(1, HD)
    key_gain = key_gain.reshape(1, HD)
    packed = pack(head_class, query_rows, key_rows, value_rows, query_gain, key_gain)
    arrived = over_frames(packed.reshape(FRAMES, tokens // FRAMES, TMAX * 3 * HD))

    other_keys, other_values = other_core(key_rows), other_core(value_rows)
    front, back = spatial(head_class, query_rows, key_rows, other_keys, value_rows, other_values, query_gain, key_gain)
    core = lax.rem(lax.axis_index("seq"), CORES)
    place = jnp.stack([lax.axis_index("head"), core]).astype(jnp.int32)
    w_own, *halves = weight_blocks(head_class, place, out_weight, group_count)

    fetched = [shifted(half, by + 1) for by, half in enumerate(halves)]
    fetched = jnp.stack(hold(fetched, (back,)))
    rest = other_core(fetched)
    w_others = jnp.where(core == 0, jnp.concatenate([fetched, rest], axis=1), jnp.concatenate([rest, fetched], axis=1))

    middle = tokens // 2
    pieces = ring(back[:middle], back[middle:])
    returned = over_frames(temporal(head_class, arrived, (*pieces[2:], w_others))).reshape(tokens, TMAX * HD)
    early = project_early(pieces, w_own, w_others)
    pieces = ring(returned[:middle] + front[:middle], returned[middle:] + front[middle:])
    return project_late(pieces, w_own, w_others, early)


def solution(mesh):
    return jax.shard_map(
        body,
        mesh=mesh,
        in_specs=(
            P("seq", "head"),
            P("seq", "head"),
            P("seq", "head"),
            P(),
            P(),
            P("head"),
            P("head", None),
        ),
        out_specs=P("seq", "head"),
        check_vma=False,
    )
```

```python
import functools
import math

import jax
import jax.numpy as jnp
from jax import lax
from jax.experimental import pallas as pl
from jax.experimental.pallas import tpu as pltpu
from jax.sharding import PartitionSpec as P

FRAMES = 32
TMAX = 4
SMALL_VMEM = 16 * 1024 * 1024
CORES = 2
ROWS = 8
HD = 128
EPSILON = 1e-06
LOG2_SCALE = math.log2(math.e) / math.sqrt(HD)


def in_hbm(shape, dtype):
    return pltpu.HBM(shape, dtype)


def from_hbm(array):
    return pltpu.with_memory_space_constraint(array, pltpu.HBM)


def from_vmem(array):
    return pltpu.with_memory_space_constraint(array, pltpu.VMEM)


def temporal_count(classes, head_count):
    total = classes[0]
    for head in range(1, head_count):
        total = total + classes[head]
    return total


def head_of(classes, slot, head_count):
    temporal_seen = jnp.int32(0)
    spatial_seen = temporal_count(classes, head_count)
    found = jnp.int32(0)
    for head in range(head_count):
        kind = classes[head]
        rank = jnp.where(kind == 1, temporal_seen, spatial_seen)
        found = jnp.where(rank == slot, jnp.int32(head), found)
        temporal_seen = temporal_seen + kind
        spatial_seen = spatial_seen + 1 - kind
    return found


def normed(rows, gain):
    widened = rows.astype(jnp.float32)
    mean = jnp.mean(widened * widened, axis=-1, keepdims=True)
    return (widened * lax.rsqrt(mean + EPSILON) * gain).astype(jnp.bfloat16)


def scores_of(queries, keys):
    return lax.dot_general(queries, keys, (((1,), (1,)), ((), ())), preferred_element_type=jnp.float32)


def hold_kernel(*refs):
    pass


def hold(arrays, after):
    anywhere = pl.BlockSpec(memory_space=pl.ANY)
    return pl.pallas_call(
        hold_kernel,
        in_specs=[anywhere] * (len(arrays) + len(after)),
        out_specs=[anywhere] * len(arrays),
        out_shape=[in_hbm(array.shape, array.dtype) for array in arrays],
        input_output_aliases={at: at for at in range(len(arrays))},
        cost_estimate=pl.CostEstimate(flops=0, bytes_accessed=0, transcendentals=0),
        name="hold",
    )(*[from_hbm(array) for array in (*arrays, *after)])


def pack_kernel(head_count, classes, query, key, value, query_gain, key_gain, out, raw, ready, in_sems, out_sems):
    heads = [head_of(classes, slot, head_count) for slot in range(TMAX)]
    gains = (query_gain, key_gain, None)
    loads, stores = [], []
    for at in range(3 * TMAX):
        slot, which = divmod(at, 3)
        source = (query, key, value)[which].at[:, pl.ds(pl.multiple_of(heads[slot] * HD, HD), HD)]
        landing = raw if gains[which] is not None else ready
        loads.append(pltpu.make_async_copy(source, landing.at[at], in_sems.at[at]))
        loads[-1].start()
    for at in range(3 * TMAX):
        gain = gains[at % 3]
        loads[at].wait()
        if gain is not None:
            ready[at] = normed(raw[at], gain[...])
        stores.append(pltpu.make_async_copy(ready.at[at], out.at[:, pl.ds(at * HD, HD)], out_sems.at[at]))
        stores[-1].start()
    for store in stores:
        store.wait()


def pack(head_class, query_rows, key_rows, value_rows, query_gain, key_gain):
    tokens, width = query_rows.shape
    anywhere = pl.BlockSpec(memory_space=pl.ANY)
    gain_spec = pl.BlockSpec((1, HD), lambda step, classes: (0, 0))
    return pl.pallas_call(
        functools.partial(pack_kernel, width // HD),
        grid_spec=pltpu.PrefetchScalarGridSpec(
            num_scalar_prefetch=1,
            grid=(1,),
            in_specs=[anywhere] * 3 + [gain_spec] * 2,
            out_specs=anywhere,
            scratch_shapes=[
                pltpu.VMEM((3 * TMAX, tokens, HD), jnp.bfloat16),
                pltpu.VMEM((3 * TMAX, tokens, HD), jnp.bfloat16),
                pltpu.SemaphoreType.DMA((3 * TMAX,)),
                pltpu.SemaphoreType.DMA((3 * TMAX,)),
            ],
        ),
        out_shape=in_hbm((tokens, TMAX * 3 * HD), jnp.bfloat16),
        cost_estimate=pl.CostEstimate(flops=8 * tokens * TMAX * HD, bytes_accessed=12 * tokens * TMAX * HD, transcendentals=0),
        name="pack",
    )(head_class, from_hbm(query_rows), from_hbm(key_rows), from_hbm(value_rows), query_gain, key_gain)


def spatial_kernel(head_count, classes, query, key, other_key, value, other_value, query_gain, key_gain, front, back, keys, values):
    slot = pl.program_id(0)
    tokens = query.shape[0]
    chunk = tokens // 4
    is_front = slot < TMAX

    @pl.when(slot >= temporal_count(classes, head_count))
    def _():
        keys[:tokens] = normed(key[...], key_gain[...])
        keys[tokens:] = normed(other_key[...], key_gain[...])
        values[:tokens, :HD] = value[...]
        values[tokens:, :HD] = other_value[...]
        values[:, HD:] = jnp.ones((2 * tokens, HD), jnp.bfloat16)

        def step(index, carry):
            rows = pl.ds(pl.multiple_of(index * chunk, chunk), chunk)
            queries = normed(query[rows, :], query_gain[...])
            weights = jnp.exp2(scores_of(queries, keys[...]) * LOG2_SCALE).astype(jnp.bfloat16)
            summed = jnp.dot(weights, values[...], preferred_element_type=jnp.float32)
            result = (summed[:, :HD] / summed[:, HD:]).astype(jnp.bfloat16)

            @pl.when(is_front)
            def _():
                front[rows, :] = result

            @pl.when(jnp.logical_not(is_front))
            def _():
                back[rows, :] = result

            return carry

        lax.fori_loop(0, tokens // chunk, step, 0)

    @pl.when(slot < temporal_count(classes, head_count))
    def _():
        front[...] = jnp.zeros_like(front)


def spatial(head_class, query_rows, key_rows, other_keys, value_rows, other_values, query_gain, key_gain):
    tokens, width = query_rows.shape
    head_count = width // HD

    def rows(slot, classes):
        return 0, head_of(classes, slot, head_count)

    row_spec = pl.BlockSpec((tokens, HD), rows)
    gain_spec = pl.BlockSpec((1, HD), lambda slot, classes: (0, 0))
    return pl.pallas_call(
        functools.partial(spatial_kernel, head_count),
        grid_spec=pltpu.PrefetchScalarGridSpec(
            num_scalar_prefetch=1,
            grid=(head_count,),
            in_specs=[row_spec] * 5 + [gain_spec] * 2,
            out_specs=[
                pl.BlockSpec((tokens, HD), lambda slot, classes: (0, jnp.minimum(slot, TMAX - 1))),
                pl.BlockSpec((tokens, HD), lambda slot, classes: (0, jnp.maximum(slot - TMAX, 0))),
            ],
            scratch_shapes=[
                pltpu.VMEM((2 * tokens, HD), jnp.bfloat16),
                pltpu.VMEM((2 * tokens, 2 * HD), jnp.bfloat16),
            ],
        ),
        out_shape=[
            in_hbm((tokens, TMAX * HD), jnp.bfloat16),
            in_hbm((tokens, width - TMAX * HD), jnp.bfloat16),
        ],
        cost_estimate=pl.CostEstimate(
            flops=16 * tokens * tokens * width, bytes_accessed=12 * tokens * width, transcendentals=2 * tokens * tokens * head_count
        ),
        name="spatial",
    )(head_class, query_rows, key_rows, from_hbm(other_keys), value_rows, from_hbm(other_values), query_gain, key_gain)


def temporal_kernel(head_count, classes, packed, *rest):
    out, held, sems = rest[-3:]
    frames, positions, _ = packed.shape
    count = frames * ROWS
    row = lax.broadcasted_iota(jnp.int32, (count, count), 0)
    column = lax.broadcasted_iota(jnp.int32, (count, count), 1)
    same = (row & (ROWS - 1)) == (column & (ROWS - 1))
    total = temporal_count(classes, head_count)

    ones = jnp.ones((count, HD), jnp.bfloat16)

    def store(slot):
        return pltpu.make_async_copy(held.at[slot], out.at[:, :, pl.ds(slot * HD, HD)], sems.at[slot])

    for slot in range(TMAX):
        parts = []
        for begin in range(0, positions, 2 * ROWS):
            columns = [slice((3 * slot + which) * HD, (3 * slot + which + 1) * HD) for which in range(3)]
            wide = [packed[:, begin : begin + 2 * ROWS, column].astype(jnp.float32) for column in columns]
            for first in (0, ROWS):
                parts.append([array[:, first : first + ROWS].reshape(count, HD).astype(jnp.bfloat16) for array in wide])
        scores = [scores_of(queries, keys) for queries, keys, _ in parts]
        weights = [jnp.exp2(jnp.where(same, score * LOG2_SCALE, -1e30)).astype(jnp.bfloat16) for score in scores]
        results = []
        for weight, (_, _, values) in zip(weights, parts, strict=True):
            summed = jnp.dot(weight, jnp.concatenate([values, ones], axis=1), preferred_element_type=jnp.float32)
            result = jnp.where(slot < total, summed[:, :HD] / summed[:, HD:], 0.0)
            results.append(result.reshape(frames, ROWS, HD))
        for pair in range(len(results) // 2):
            both = jnp.concatenate(results[2 * pair : 2 * pair + 2], axis=1)
            held[slot, :, 2 * ROWS * pair : 2 * ROWS * (pair + 1)] = both.astype(jnp.bfloat16)
        store(slot).start()
    for slot in range(TMAX):
        store(slot).wait()


def temporal(head_class, packed, after):
    frames, positions, _ = packed.shape
    return pl.pallas_call(
        functools.partial(temporal_kernel, head_class.shape[0]),
        grid_spec=pltpu.PrefetchScalarGridSpec(
            num_scalar_prefetch=1,
            grid=(1,),
            in_specs=[pl.BlockSpec(memory_space=pltpu.VMEM)] + [pl.BlockSpec(memory_space=pl.ANY)] * len(after),
            out_specs=pl.BlockSpec(memory_space=pl.ANY),
            scratch_shapes=[
                pltpu.VMEM((TMAX, frames, positions, HD), jnp.bfloat16),
                pltpu.SemaphoreType.DMA((TMAX,)),
            ],
        ),
        out_shape=in_hbm((frames, positions, TMAX * HD), jnp.bfloat16),
        compiler_params=pltpu.CompilerParams(vmem_limit_bytes=SMALL_VMEM),
        cost_estimate=pl.CostEstimate(
            flops=32 * frames * frames * positions * TMAX * HD,
            bytes_accessed=8 * frames * positions * TMAX * HD,
            transcendentals=8 * frames * frames * positions * TMAX,
        ),
        name="temporal",
    )(head_class, from_vmem(packed), *[from_hbm(array) for array in after])


def weight_kernel(classes, place, weight, own, *others):
    width = own.shape[1]
    group_count = len(others) + 1

    def columns(shift):
        block = lax.rem(place[0] + shift, group_count)
        return weight[:, pl.ds(pl.multiple_of(block * width, width), width)]

    own[...] = columns(0)

    @pl.when(pl.program_id(0) // (pl.num_programs(0) // CORES) == place[1])
    def _():
        for shift, other in enumerate(others):
            other[...] = columns(shift + 1)


def weight_blocks(head_class, place, weight, group_count):
    rows, columns = weight.shape
    head_count = rows // HD
    share = head_count // CORES
    width = columns // group_count

    def half_rows(slot, classes, place):
        return jnp.clip(slot - place[1] * share, 0, share - 1), 0

    return pl.pallas_call(
        weight_kernel,
        grid_spec=pltpu.PrefetchScalarGridSpec(
            num_scalar_prefetch=2,
            grid=(head_count,),
            in_specs=[pl.BlockSpec((HD, columns), lambda slot, classes, place: (head_of(classes, slot, head_count), 0))],
            out_specs=[pl.BlockSpec((HD, width), lambda slot, classes, place: (slot, 0))]
            + [pl.BlockSpec((HD, width), half_rows)] * (group_count - 1),
        ),
        out_shape=[in_hbm((rows, width), jnp.bfloat16)] + [in_hbm((rows // CORES, width), jnp.bfloat16)] * (group_count - 1),
        cost_estimate=pl.CostEstimate(flops=0, bytes_accessed=4 * rows * columns, transcendentals=0),
        name="weight_blocks",
    )(head_class, place, weight)


def product(rows, weight, first):
    return jnp.dot(rows, weight[first : first + rows.shape[1]], preferred_element_type=jnp.float32)


def near_sum(own, right, left, w_own, w_others, first):
    return product(own[...], w_own, first) + product(right[...], w_others.at[0], first) + product(left[...], w_others.at[2], first)


def early_kernel(first, own_top, own_bottom, right_top, right_bottom, left_top, left_bottom, far_top, far_bottom, w_own, w_others, out):
    half = own_top.shape[0]
    parts = ((own_top, right_top, left_top, far_top), (own_bottom, right_bottom, left_bottom, far_bottom))
    for part, (own, right, left, far) in enumerate(parts):
        total = near_sum(own, right, left, w_own, w_others, first) + product(far[...], w_others.at[1], first)
        out[part * half : (part + 1) * half] = total


def near_kernel(own_top, own_bottom, right_top, right_bottom, left_top, left_bottom, w_own, w_others, total, out):
    half = own_top.shape[0]
    for part, (own, right, left) in enumerate(((own_top, right_top, left_top), (own_bottom, right_bottom, left_bottom))):
        rows = slice(part * half, (part + 1) * half)
        out[rows] = total[rows] + near_sum(own, right, left, w_own, w_others, 0)


def far_kernel(begin, far, w_others, total, *rest):
    out, held, sems = rest[-3:]
    stores = []
    for step in range(held.shape[0]):
        rows = held.shape[1]
        at = step * rows
        summed = product(far[at : at + rows], w_others.at[1], 0) + total[begin + at : begin + at + rows]
        held[step] = summed.astype(held.dtype)
        stores.append(pltpu.make_async_copy(held.at[step], out.at[pl.ds(begin + at, rows)], sems.at[step]))
        stores[-1].start()
    for store in stores:
        store.wait()


def project_far(begin, far, w_others, total, into):
    tokens, width = total.shape
    rows, depth = far.shape
    steps = 2
    extra = [] if into is None else [from_hbm(into)]
    return pl.pallas_call(
        functools.partial(far_kernel, begin),
        in_specs=[pl.BlockSpec(memory_space=pltpu.VMEM)] * 3 + [pl.BlockSpec(memory_space=pl.ANY)] * len(extra),
        out_specs=pl.BlockSpec(memory_space=pl.ANY),
        out_shape=in_hbm((tokens, width), jnp.bfloat16),
        scratch_shapes=[pltpu.VMEM((steps, rows // steps, width), jnp.bfloat16), pltpu.SemaphoreType.DMA((steps,))],
        input_output_aliases={3: 0} if extra else {},
        compiler_params=pltpu.CompilerParams(vmem_limit_bytes=SMALL_VMEM),
        cost_estimate=pl.CostEstimate(flops=2 * rows * depth * width, bytes_accessed=6 * rows * width, transcendentals=0),
        name="far",
    )(*[from_vmem(array) for array in (far, w_others, total)], *extra)


def summing(kernel, name, operands, depth_terms):
    tokens, width = 2 * operands[0].shape[0], operands[-1].shape[-1]
    depth = operands[0].shape[1]
    whole = pl.BlockSpec(memory_space=pltpu.VMEM)
    return pl.pallas_call(
        kernel,
        in_specs=[whole] * len(operands),
        out_specs=whole,
        out_shape=pltpu.VMEM((tokens, width), jnp.float32),
        compiler_params=pltpu.CompilerParams(vmem_limit_bytes=SMALL_VMEM),
        cost_estimate=pl.CostEstimate(
            flops=2 * depth_terms * tokens * depth * width, bytes_accessed=8 * tokens * width, transcendentals=0
        ),
        name=name,
    )(*[from_vmem(array) for array in operands])


def project_early(pieces, w_own, w_others):
    first = TMAX * HD
    return summing(functools.partial(early_kernel, first), "project_early", (*pieces, w_own, w_others), 4)


def project_late(pieces, w_own, w_others, total):
    near = summing(near_kernel, "near", (*pieces[:6], w_own, w_others, total), 3)
    far_top, far_bottom = pieces[6:]
    out = project_far(0, far_top, w_others, near, None)
    return project_far(far_top.shape[0], far_bottom, w_others, near, out)


def shifted(block, by):
    count = lax.axis_size("head")
    return lax.ppermute(block, "head", [(at, (at + by) % count) for at in range(count)])


def ring(top, bottom):
    right_top, left_bottom = shifted(top, 1), shifted(bottom, -1)
    right_bottom, left_top = shifted(bottom, 1), shifted(top, -1)
    far_top, far_bottom = shifted(right_top, 1), shifted(left_bottom, -1)
    return top, bottom, right_top, right_bottom, left_top, left_bottom, far_top, far_bottom


def other_core(block):
    count = lax.axis_size("seq")
    return lax.ppermute(block, "seq", [(at, at ^ 1) for at in range(count)])


def over_frames(blocks):
    count = lax.axis_size("seq")
    groups = [list(range(core, count, CORES)) for core in range(CORES)]
    return lax.all_to_all(blocks, "seq", 0, 0, axis_index_groups=groups)


def body(query_rows, key_rows, value_rows, query_gain, key_gain, head_class, out_weight):
    tokens = query_rows.shape[0]
    group_count = lax.axis_size("head")
    query_gain = query_gain.reshape(1, HD)
    key_gain = key_gain.reshape(1, HD)
    packed = pack(head_class, query_rows, key_rows, value_rows, query_gain, key_gain)
    arrived = over_frames(packed.reshape(FRAMES, tokens // FRAMES, TMAX * 3 * HD))

    other_keys, other_values = other_core(key_rows), other_core(value_rows)
    front, back = spatial(head_class, query_rows, key_rows, other_keys, value_rows, other_values, query_gain, key_gain)
    core = lax.rem(lax.axis_index("seq"), CORES)
    place = jnp.stack([lax.axis_index("head"), core]).astype(jnp.int32)
    w_own, *halves = weight_blocks(head_class, place, out_weight, group_count)

    fetched = [shifted(half, by + 1) for by, half in enumerate(halves)]
    fetched = jnp.stack(hold(fetched, (back,)))
    rest = other_core(fetched)
    w_others = jnp.where(core == 0, jnp.concatenate([fetched, rest], axis=1), jnp.concatenate([rest, fetched], axis=1))

    middle = tokens // 2
    pieces = ring(back[:middle], back[middle:])
    returned = over_frames(temporal(head_class, arrived, (*pieces[2:], w_others))).reshape(tokens, TMAX * HD)
    early = project_early(pieces, w_own, w_others)
    pieces = ring(returned[:middle] + front[:middle], returned[middle:] + front[middle:])
    return project_late(pieces, w_own, w_others, early)


def solution(mesh):
    return jax.shard_map(
        body,
        mesh=mesh,
        in_specs=(
            P("seq", "head"),
            P("seq", "head"),
            P("seq", "head"),
            P(),
            P(),
            P("head"),
            P("head", None),
        ),
        out_specs=P("seq", "head"),
        check_vma=False,
    )
```

```python
import functools
import math

import jax
import jax.numpy as jnp
from jax import lax
from jax.experimental import pallas as pl
from jax.experimental.pallas import tpu as pltpu
from jax.sharding import PartitionSpec as P

FRAMES = 32
TMAX = 4
SMALL_VMEM = 16 * 1024 * 1024
CORES = 2
ROWS = 8
HD = 128
EPSILON = 1e-06
LOG2_SCALE = math.log2(math.e) / math.sqrt(HD)


def in_hbm(shape, dtype):
    return pltpu.HBM(shape, dtype)


def from_hbm(array):
    return pltpu.with_memory_space_constraint(array, pltpu.HBM)


def from_vmem(array):
    return pltpu.with_memory_space_constraint(array, pltpu.VMEM)


def temporal_count(classes, head_count):
    total = classes[0]
    for head in range(1, head_count):
        total = total + classes[head]
    return total


def head_of(classes, slot, head_count):
    temporal_seen = jnp.int32(0)
    spatial_seen = temporal_count(classes, head_count)
    found = jnp.int32(0)
    for head in range(head_count):
        kind = classes[head]
        rank = jnp.where(kind == 1, temporal_seen, spatial_seen)
        found = jnp.where(rank == slot, jnp.int32(head), found)
        temporal_seen = temporal_seen + kind
        spatial_seen = spatial_seen + 1 - kind
    return found


def normed(rows, gain):
    widened = rows.astype(jnp.float32)
    mean = jnp.mean(widened * widened, axis=-1, keepdims=True)
    return (widened * lax.rsqrt(mean + EPSILON) * gain).astype(jnp.bfloat16)


def scores_of(queries, keys):
    return lax.dot_general(queries, keys, (((1,), (1,)), ((), ())), preferred_element_type=jnp.float32)


def hold_kernel(*refs):
    pass


def hold(arrays, after):
    anywhere = pl.BlockSpec(memory_space=pl.ANY)
    return pl.pallas_call(
        hold_kernel,
        in_specs=[anywhere] * (len(arrays) + len(after)),
        out_specs=[anywhere] * len(arrays),
        out_shape=[in_hbm(array.shape, array.dtype) for array in arrays],
        input_output_aliases={at: at for at in range(len(arrays))},
        cost_estimate=pl.CostEstimate(flops=0, bytes_accessed=0, transcendentals=0),
        name="hold",
    )(*[from_hbm(array) for array in (*arrays, *after)])


def pack_kernel(head_count, classes, query, key, value, query_gain, key_gain, out, raw, ready, in_sems, out_sems):
    heads = [head_of(classes, slot, head_count) for slot in range(TMAX)]
    gains = (query_gain, key_gain, None)
    loads, stores = [], []
    for at in range(3 * TMAX):
        slot, which = divmod(at, 3)
        source = (query, key, value)[which].at[:, pl.ds(pl.multiple_of(heads[slot] * HD, HD), HD)]
        landing = raw.at[at] if gains[which] is not None else ready.at[slot, :, pl.ds(which * HD, HD)]
        loads.append(pltpu.make_async_copy(source, landing, in_sems.at[at]))
        loads[-1].start()
    for at in range(3 * TMAX):
        slot, which = divmod(at, 3)
        loads[at].wait()
        if gains[which] is not None:
            ready[slot, :, which * HD : (which + 1) * HD] = normed(raw[at], gains[which][...])
        if which == 2:
            target = out.at[:, pl.ds(3 * slot * HD, 3 * HD)]
            stores.append(pltpu.make_async_copy(ready.at[slot], target, out_sems.at[slot]))
            stores[-1].start()
    for store in stores:
        store.wait()


def pack(head_class, query_rows, key_rows, value_rows, query_gain, key_gain):
    tokens, width = query_rows.shape
    anywhere = pl.BlockSpec(memory_space=pl.ANY)
    gain_spec = pl.BlockSpec((1, HD), lambda step, classes: (0, 0))
    return pl.pallas_call(
        functools.partial(pack_kernel, width // HD),
        grid_spec=pltpu.PrefetchScalarGridSpec(
            num_scalar_prefetch=1,
            grid=(1,),
            in_specs=[anywhere] * 3 + [gain_spec] * 2,
            out_specs=anywhere,
            scratch_shapes=[
                pltpu.VMEM((3 * TMAX, tokens, HD), jnp.bfloat16),
                pltpu.VMEM((TMAX, tokens, 3 * HD), jnp.bfloat16),
                pltpu.SemaphoreType.DMA((3 * TMAX,)),
                pltpu.SemaphoreType.DMA((TMAX,)),
            ],
        ),
        out_shape=in_hbm((tokens, TMAX * 3 * HD), jnp.bfloat16),
        cost_estimate=pl.CostEstimate(flops=8 * tokens * TMAX * HD, bytes_accessed=12 * tokens * TMAX * HD, transcendentals=0),
        name="pack",
    )(head_class, from_hbm(query_rows), from_hbm(key_rows), from_hbm(value_rows), query_gain, key_gain)


def spatial_kernel(head_count, classes, query, key, other_key, value, other_value, query_gain, key_gain, front, back, keys, values):
    slot = pl.program_id(0)
    tokens = query.shape[0]
    chunk = tokens // 4
    is_front = slot < TMAX

    @pl.when(slot >= temporal_count(classes, head_count))
    def _():
        keys[:tokens] = normed(key[...], key_gain[...])
        keys[tokens:] = normed(other_key[...], key_gain[...])
        values[:tokens, :HD] = value[...]
        values[tokens:, :HD] = other_value[...]
        values[:, HD:] = jnp.ones((2 * tokens, HD), jnp.bfloat16)

        def step(index, carry):
            rows = pl.ds(pl.multiple_of(index * chunk, chunk), chunk)
            queries = normed(query[rows, :], query_gain[...])
            weights = jnp.exp2(scores_of(queries, keys[...]) * LOG2_SCALE).astype(jnp.bfloat16)
            summed = jnp.dot(weights, values[...], preferred_element_type=jnp.float32)
            result = (summed[:, :HD] / summed[:, HD:]).astype(jnp.bfloat16)

            @pl.when(is_front)
            def _():
                front[rows, :] = result

            @pl.when(jnp.logical_not(is_front))
            def _():
                back[rows, :] = result

            return carry

        lax.fori_loop(0, tokens // chunk, step, 0)

    @pl.when(slot < temporal_count(classes, head_count))
    def _():
        front[...] = jnp.zeros_like(front)


def spatial(head_class, query_rows, key_rows, other_keys, value_rows, other_values, query_gain, key_gain):
    tokens, width = query_rows.shape
    head_count = width // HD

    def rows(slot, classes):
        return 0, head_of(classes, slot, head_count)

    row_spec = pl.BlockSpec((tokens, HD), rows)
    gain_spec = pl.BlockSpec((1, HD), lambda slot, classes: (0, 0))
    return pl.pallas_call(
        functools.partial(spatial_kernel, head_count),
        grid_spec=pltpu.PrefetchScalarGridSpec(
            num_scalar_prefetch=1,
            grid=(head_count,),
            in_specs=[row_spec] * 5 + [gain_spec] * 2,
            out_specs=[
                pl.BlockSpec((tokens, HD), lambda slot, classes: (0, jnp.minimum(slot, TMAX - 1))),
                pl.BlockSpec((tokens, HD), lambda slot, classes: (0, jnp.maximum(slot - TMAX, 0))),
            ],
            scratch_shapes=[
                pltpu.VMEM((2 * tokens, HD), jnp.bfloat16),
                pltpu.VMEM((2 * tokens, 2 * HD), jnp.bfloat16),
            ],
        ),
        out_shape=[
            in_hbm((tokens, TMAX * HD), jnp.bfloat16),
            in_hbm((tokens, width - TMAX * HD), jnp.bfloat16),
        ],
        cost_estimate=pl.CostEstimate(
            flops=16 * tokens * tokens * width, bytes_accessed=12 * tokens * width, transcendentals=2 * tokens * tokens * head_count
        ),
        name="spatial",
    )(head_class, query_rows, key_rows, from_hbm(other_keys), value_rows, from_hbm(other_values), query_gain, key_gain)


def temporal_kernel(head_count, classes, packed, *rest):
    out, held, sems = rest[-3:]
    frames, positions, _ = packed.shape
    count = frames * ROWS
    row = lax.broadcasted_iota(jnp.int32, (count, count), 0)
    column = lax.broadcasted_iota(jnp.int32, (count, count), 1)
    same = (row & (ROWS - 1)) == (column & (ROWS - 1))
    total = temporal_count(classes, head_count)

    ones = jnp.ones((count, HD), jnp.bfloat16)

    def store(slot):
        return pltpu.make_async_copy(held.at[slot], out.at[:, :, pl.ds(slot * HD, HD)], sems.at[slot])

    for slot in range(TMAX):
        parts = []
        for begin in range(0, positions, 2 * ROWS):
            columns = [slice((3 * slot + which) * HD, (3 * slot + which + 1) * HD) for which in range(3)]
            wide = [packed[:, begin : begin + 2 * ROWS, column].astype(jnp.float32) for column in columns]
            for first in (0, ROWS):
                parts.append([array[:, first : first + ROWS].reshape(count, HD).astype(jnp.bfloat16) for array in wide])
        scores = [scores_of(queries, keys) for queries, keys, _ in parts]
        weights = [jnp.exp2(jnp.where(same, score * LOG2_SCALE, -1e30)).astype(jnp.bfloat16) for score in scores]
        results = []
        for weight, (_, _, values) in zip(weights, parts, strict=True):
            summed = jnp.dot(weight, jnp.concatenate([values, ones], axis=1), preferred_element_type=jnp.float32)
            result = jnp.where(slot < total, summed[:, :HD] / summed[:, HD:], 0.0)
            results.append(result.reshape(frames, ROWS, HD))
        for pair in range(len(results) // 2):
            both = jnp.concatenate(results[2 * pair : 2 * pair + 2], axis=1)
            held[slot, :, 2 * ROWS * pair : 2 * ROWS * (pair + 1)] = both.astype(jnp.bfloat16)
        store(slot).start()
    for slot in range(TMAX):
        store(slot).wait()


def temporal(head_class, packed, after):
    frames, positions, _ = packed.shape
    return pl.pallas_call(
        functools.partial(temporal_kernel, head_class.shape[0]),
        grid_spec=pltpu.PrefetchScalarGridSpec(
            num_scalar_prefetch=1,
            grid=(1,),
            in_specs=[pl.BlockSpec(memory_space=pltpu.VMEM)] + [pl.BlockSpec(memory_space=pl.ANY)] * len(after),
            out_specs=pl.BlockSpec(memory_space=pl.ANY),
            scratch_shapes=[
                pltpu.VMEM((TMAX, frames, positions, HD), jnp.bfloat16),
                pltpu.SemaphoreType.DMA((TMAX,)),
            ],
        ),
        out_shape=in_hbm((frames, positions, TMAX * HD), jnp.bfloat16),
        compiler_params=pltpu.CompilerParams(vmem_limit_bytes=SMALL_VMEM),
        cost_estimate=pl.CostEstimate(
            flops=32 * frames * frames * positions * TMAX * HD,
            bytes_accessed=8 * frames * positions * TMAX * HD,
            transcendentals=8 * frames * frames * positions * TMAX,
        ),
        name="temporal",
    )(head_class, from_vmem(packed), *[from_hbm(array) for array in after])


def weight_kernel(classes, place, weight, own, *others):
    width = own.shape[1]
    group_count = len(others) + 1

    def columns(shift):
        block = lax.rem(place[0] + shift, group_count)
        return weight[:, pl.ds(pl.multiple_of(block * width, width), width)]

    own[...] = columns(0)

    @pl.when(pl.program_id(0) // (pl.num_programs(0) // CORES) == place[1])
    def _():
        for shift, other in enumerate(others):
            other[...] = columns(shift + 1)


def weight_blocks(head_class, place, weight, group_count):
    rows, columns = weight.shape
    head_count = rows // HD
    share = head_count // CORES
    width = columns // group_count

    def half_rows(slot, classes, place):
        return jnp.clip(slot - place[1] * share, 0, share - 1), 0

    return pl.pallas_call(
        weight_kernel,
        grid_spec=pltpu.PrefetchScalarGridSpec(
            num_scalar_prefetch=2,
            grid=(head_count,),
            in_specs=[pl.BlockSpec((HD, columns), lambda slot, classes, place: (head_of(classes, slot, head_count), 0))],
            out_specs=[pl.BlockSpec((HD, width), lambda slot, classes, place: (slot, 0))]
            + [pl.BlockSpec((HD, width), half_rows)] * (group_count - 1),
        ),
        out_shape=[in_hbm((rows, width), jnp.bfloat16)] + [in_hbm((rows // CORES, width), jnp.bfloat16)] * (group_count - 1),
        cost_estimate=pl.CostEstimate(flops=0, bytes_accessed=4 * rows * columns, transcendentals=0),
        name="weight_blocks",
    )(head_class, place, weight)


def product(rows, weight, first):
    return jnp.dot(rows, weight[first : first + rows.shape[1]], preferred_element_type=jnp.float32)


def near_sum(own, right, left, w_own, w_others, first):
    return product(own[...], w_own, first) + product(right[...], w_others.at[0], first) + product(left[...], w_others.at[2], first)


def early_kernel(first, own_top, own_bottom, right_top, right_bottom, left_top, left_bottom, far_top, far_bottom, w_own, w_others, out):
    half = own_top.shape[0]
    parts = ((own_top, right_top, left_top, far_top), (own_bottom, right_bottom, left_bottom, far_bottom))
    for part, (own, right, left, far) in enumerate(parts):
        total = near_sum(own, right, left, w_own, w_others, first) + product(far[...], w_others.at[1], first)
        out[part * half : (part + 1) * half] = total


def near_kernel(own_top, own_bottom, right_top, right_bottom, left_top, left_bottom, w_own, w_others, total, out):
    half = own_top.shape[0]
    for part, (own, right, left) in enumerate(((own_top, right_top, left_top), (own_bottom, right_bottom, left_bottom))):
        rows = slice(part * half, (part + 1) * half)
        out[rows] = total[rows] + near_sum(own, right, left, w_own, w_others, 0)


def far_kernel(far_top, far_bottom, w_others, total, out, held, sems):
    steps, rows, _ = held.shape
    stores = []
    for step in range(steps):
        far = (far_top, far_bottom)[2 * step // steps]
        begin = step * rows % far.shape[0]
        summed = product(far[begin : begin + rows], w_others.at[1], 0) + total[step * rows : (step + 1) * rows]
        held[step] = summed.astype(held.dtype)
        stores.append(pltpu.make_async_copy(held.at[step], out.at[pl.ds(step * rows, rows)], sems.at[step]))
        stores[-1].start()
    for store in stores:
        store.wait()


def summing(kernel, name, operands, depth_terms):
    tokens, width = 2 * operands[0].shape[0], operands[-1].shape[-1]
    depth = operands[0].shape[1]
    whole = pl.BlockSpec(memory_space=pltpu.VMEM)
    return pl.pallas_call(
        kernel,
        in_specs=[whole] * len(operands),
        out_specs=whole,
        out_shape=pltpu.VMEM((tokens, width), jnp.float32),
        compiler_params=pltpu.CompilerParams(vmem_limit_bytes=SMALL_VMEM),
        cost_estimate=pl.CostEstimate(
            flops=2 * depth_terms * tokens * depth * width, bytes_accessed=8 * tokens * width, transcendentals=0
        ),
        name=name,
    )(*[from_vmem(array) for array in operands])


def project_early(pieces, w_own, w_others):
    first = TMAX * HD
    return summing(functools.partial(early_kernel, first), "project_early", (*pieces, w_own, w_others), 4)


def project_late(pieces, w_own, w_others, total):
    near = summing(near_kernel, "near", (*pieces[:6], w_own, w_others, total), 3)
    tokens, width = near.shape
    depth = pieces[0].shape[1]
    steps = 4
    return pl.pallas_call(
        far_kernel,
        in_specs=[pl.BlockSpec(memory_space=pltpu.VMEM)] * 4,
        out_specs=pl.BlockSpec(memory_space=pl.ANY),
        out_shape=in_hbm((tokens, width), jnp.bfloat16),
        scratch_shapes=[pltpu.VMEM((steps, tokens // steps, width), jnp.bfloat16), pltpu.SemaphoreType.DMA((steps,))],
        compiler_params=pltpu.CompilerParams(vmem_limit_bytes=SMALL_VMEM),
        cost_estimate=pl.CostEstimate(flops=2 * tokens * depth * width, bytes_accessed=8 * tokens * width, transcendentals=0),
        name="far",
    )(*[from_vmem(array) for array in (*pieces[6:], w_others, near)])


def shifted(block, by):
    count = lax.axis_size("head")
    return lax.ppermute(block, "head", [(at, (at + by) % count) for at in range(count)])


def ring(top, bottom):
    right_top, left_bottom = shifted(top, 1), shifted(bottom, -1)
    right_bottom, left_top = shifted(bottom, 1), shifted(top, -1)
    far_top, far_bottom = shifted(right_top, 1), shifted(left_bottom, -1)
    return top, bottom, right_top, right_bottom, left_top, left_bottom, far_top, far_bottom


def other_core(block):
    count = lax.axis_size("seq")
    return lax.ppermute(block, "seq", [(at, at ^ 1) for at in range(count)])


def over_frames(blocks):
    count = lax.axis_size("seq")
    groups = [list(range(core, count, CORES)) for core in range(CORES)]
    return lax.all_to_all(blocks, "seq", 0, 0, axis_index_groups=groups)


def body(query_rows, key_rows, value_rows, query_gain, key_gain, head_class, out_weight):
    tokens = query_rows.shape[0]
    group_count = lax.axis_size("head")
    query_gain = query_gain.reshape(1, HD)
    key_gain = key_gain.reshape(1, HD)
    packed = pack(head_class, query_rows, key_rows, value_rows, query_gain, key_gain)
    arrived = over_frames(packed.reshape(FRAMES, tokens // FRAMES, TMAX * 3 * HD))

    other_keys, other_values = other_core(key_rows), other_core(value_rows)
    front, back = spatial(head_class, query_rows, key_rows, other_keys, value_rows, other_values, query_gain, key_gain)
    core = lax.rem(lax.axis_index("seq"), CORES)
    place = jnp.stack([lax.axis_index("head"), core]).astype(jnp.int32)
    w_own, *halves = weight_blocks(head_class, place, out_weight, group_count)

    fetched = [shifted(half, by + 1) for by, half in enumerate(halves)]
    fetched = jnp.stack(hold(fetched, (back,)))
    rest = other_core(fetched)
    w_others = jnp.where(core == 0, jnp.concatenate([fetched, rest], axis=1), jnp.concatenate([rest, fetched], axis=1))

    middle = tokens // 2
    pieces = ring(back[:middle], back[middle:])
    returned = over_frames(temporal(head_class, arrived, (*pieces[2:], w_others))).reshape(tokens, TMAX * HD)
    early = project_early(pieces, w_own, w_others)
    pieces = ring(returned[:middle] + front[:middle], returned[middle:] + front[middle:])
    return project_late(pieces, w_own, w_others, early)


def solution(mesh):
    return jax.shard_map(
        body,
        mesh=mesh,
        in_specs=(
            P("seq", "head"),
            P("seq", "head"),
            P("seq", "head"),
            P(),
            P(),
            P("head"),
            P("head", None),
        ),
        out_specs=P("seq", "head"),
        check_vma=False,
    )
```
